128 devices in a mesh: grp: 16 (over x, y_lo, core), ctx: 8 (over y_hi, z).
Axes of the slice: x: 4, y: 4 (y_hi: 2, y_lo: 2; y = y_hi * 2 + y_lo), z: 4, core: 2. Of those that a mesh axis runs over, the one named last changes fastest.
Arguments:
- inputs: bfloat16 [16, 1536, 1024], P('grp', 'ctx'), may hold values from -6 to 6
- cotangent: bfloat16 [16, 1536, 1024], P('grp', 'ctx'), may hold values from -6 to 6
- segments: int32 [16, 1536], P('grp'), may hold values from 0 to 2, as said below
- norm_one_gain: bfloat16 [2, 1024], P(None, 'ctx'), may hold values from 0.5 to 1.5
- norm_one_bias: bfloat16 [2, 1024], P(None, 'ctx'), may hold values from -1.25 to 1.25
- input_weight: bfloat16 [2, 1024, 3072], P(None, 'ctx'), may hold values from -1 to 1
- input_bias: bfloat16 [2, 2048], P(None, 'ctx'), may hold values from -2 to 2
- project_weight: bfloat16 [2, 1024, 1024], P(None, 'ctx'), may hold values from -0.75 to 0.75
- project_bias: bfloat16 [2, 1024], P(None, 'ctx'), may hold values from -1.25 to 1.25
- norm_two_gain: bfloat16 [2, 1024], P(None, 'ctx'), may hold values from 0.5 to 1.5
- norm_two_bias: bfloat16 [2, 1024], P(None, 'ctx'), may hold values from -1.25 to 1.25
- up_weight: bfloat16 [2, 1024, 4096], P(None, 'ctx'), may hold values from -0.1875 to 0.1875
- up_bias: bfloat16 [2, 4096], P(None, 'ctx'), may hold values from -1.75 to 1.75
- down_weight: bfloat16 [2, 4096, 1024], P(None, 'ctx'), may hold values from -0.09375 to 0.09375
- down_bias: bfloat16 [2, 1024], P(None, 'ctx'), may hold values from -1.25 to 1.25
Outputs:
- block_output: float32 [16, 1536, 1024], P('grp', 'ctx')
- grad_inputs: float32 [16, 1536, 1024], P('grp', 'ctx')
- grad_norm_one_gain: float32 [2, 1024], P(None, 'ctx')
- grad_norm_one_bias: float32 [2, 1024], P(None, 'ctx')
- grad_input_weight: float32 [2, 1024, 3072], P(None, 'ctx')
- grad_input_bias: float32 [2, 2048], P(None, 'ctx')
- grad_project_weight: float32 [2, 1024, 1024], P(None, 'ctx')
- grad_project_bias: float32 [2, 1024], P(None, 'ctx')
- grad_norm_two_gain: float32 [2, 1024], P(None, 'ctx')
- grad_norm_two_bias: float32 [2, 1024], P(None, 'ctx')
- grad_up_weight: float32 [2, 1024, 4096], P(None, 'ctx')
- grad_up_bias: float32 [2, 4096], P(None, 'ctx')
- grad_down_weight: float32 [2, 4096, 1024], P(None, 'ctx')
- grad_down_bias: float32 [2, 1024], P(None, 'ctx')
The draws below stay inside these ranges and needn't reach their ends.
Inputs may be any that keep to these rules, and one draw needn't show every extreme that they name: `segments`: in every group the first 1024 tokens have segment 0, then come the tokens of continuation 1 and then those of continuation 2, each continuation one token or more.
All inputs are finite; a program needn't handle non-finite values.
Results may differ from the reference program's by a relative error of at most 0.03.
Values may be sent and summed in bfloat16 or wider, within the bound.
No kernel may reach another device: no remote copies, remote signals or barrier semaphores. Data moves between devices by JAX's collectives and lax.ppermute only.
A program may use at most 192 MiB of HBM per device.

```python
import jax
import jax.numpy as jnp
from jax import lax

D = 1024
HEADS = 16
HEAD_DIM = 64
FF = 4096
LAYERS = 2
NCONT = 2
GROUP_TOK = 1536
PROMPT = 1024
GROUPS = 16


anchor_count = 4


anchor_boost = 14.0


query_share = 0.5


def shared_signs(key):
    first_key, second_key = jax.random.split(key)
    anchor_dir = (2 * jax.random.randint(first_key, (D,), 0, 2) - 1).astype(jnp.float32)
    key_dir = (2 * jax.random.randint(second_key, (D,), 0, 2) - 1).astype(jnp.float32)
    return (anchor_dir, key_dir)


def draw_inputs(key, part):
    anchor_dir, key_dir = shared_signs(key)
    key = jax.random.fold_in(key, 21)
    noise_key, place_key = jax.random.split(key)
    noise = jnp.clip(jax.random.normal(noise_key, (GROUPS, GROUP_TOK, D), jnp.float32), -5.0, 5.0)
    spots = jax.random.randint(place_key, (GROUPS, anchor_count), 0, max(PROMPT // 4, 1))
    token_index = jnp.arange(GROUP_TOK, dtype=jnp.int32)
    is_anchor = jnp.any(token_index[None, :, None] == spots[:, None, :], axis=2)
    anchored = 3.0 * anchor_dir[None, None, :] + 0.5 * noise
    return jnp.where(is_anchor[:, :, None], anchored, noise).astype(jnp.bfloat16)


def draw_input_weight(key, part):
    anchor_dir, key_dir = shared_signs(key)
    key = jax.random.fold_in(key, 22)
    base = jnp.clip(jax.random.normal(key, (LAYERS, D, 3 * D), jnp.float32), -4.0, 4.0) * D ** (-0.5)
    strength = anchor_boost / (query_share * HEAD_DIM ** 0.5)
    extra = strength * anchor_dir[:, None] * key_dir[None, :] / D
    query_part = base[:, :, :D]
    key_part = base[:, :, D:2 * D] + extra[None]
    value_part = base[:, :, 2 * D:]
    return jnp.concatenate([query_part, key_part, value_part], axis=2).astype(jnp.bfloat16)


def draw_input_bias(key, part):
    anchor_dir, key_dir = shared_signs(key)
    key = jax.random.fold_in(key, 23)
    noise = 0.3 * jnp.clip(jax.random.normal(key, (LAYERS, 2 * D), jnp.float32), -4.0, 4.0)
    common = jnp.concatenate([query_share * key_dir, jnp.zeros((D,), jnp.float32)])
    return (noise + common[None, :]).astype(jnp.bfloat16)


def draw_segments(key, part):
    key = jax.random.fold_in(key, 11)
    remaining = GROUP_TOK - PROMPT
    cut_points = jax.random.randint(key, (GROUPS, 1), 1, remaining)
    position = jnp.arange(GROUP_TOK, dtype=jnp.int32)[None, :]
    second = jnp.where(position < PROMPT + cut_points, 1, NCONT)
    return jnp.where(position < PROMPT, 0, second).astype(jnp.int32)


def block_levels(stream_key, dims, cuts, smallest, largest):
    def one(axis_at, parts):
        heights = jax.random.uniform(jax.random.fold_in(jax.random.fold_in(stream_key, 6), axis_at), (parts,), jnp.float32, smallest / len(cuts), largest / len(cuts))
        return jnp.repeat(jnp.exp(heights), dims[axis_at] // parts).reshape((-1,) + (1,) * (len(dims) - axis_at - 1))

    level = one(*cuts[0])
    for cut in cuts[1:]:
        level = level * one(*cut)
    return level


def centred(own_key, shape, deviation, limit, shards=(), kind=jnp.bfloat16):
    values = deviation * jax.random.normal(own_key, shape, jnp.float32)
    if shards:
        values = values * block_levels(own_key, shape, shards, -0.22, 0.18)
    return jnp.clip(values, -limit, limit).astype(kind)


def setup_inputs(seed: int = 0) -> dict:
    streams_of = jax.random.split(jax.random.key(seed), 16)
    inputs = draw_inputs(jax.random.fold_in(streams_of[15], 71), 0)
    cotangent = centred(streams_of[1], (GROUPS, GROUP_TOK, D), 1.0, 6.0, ((0, 16), (1, 8)))
    segments = draw_segments(jax.random.fold_in(streams_of[15], 71), 0)
    norm_one_gain = jnp.clip(1.0 + 0.1 * jax.random.normal(streams_of[3], (LAYERS, D), jnp.float32), 0.5, 1.5).astype(jnp.bfloat16)
    norm_one_bias = centred(streams_of[4], (LAYERS, D), 0.2, 1.25, ((1, 8),))
    input_weight = draw_input_weight(jax.random.fold_in(streams_of[15], 71), 0)
    input_bias = draw_input_bias(jax.random.fold_in(streams_of[15], 71), 0)
    project_weight = centred(streams_of[7], (LAYERS, D, D), (D // 16) ** -0.5, 0.75, ((1, 8),))
    project_bias = centred(streams_of[8], (LAYERS, D), 0.2, 1.25, ((1, 8),))
    norm_two_gain = jnp.clip(1.0 + 0.1 * jax.random.normal(streams_of[9], (LAYERS, D), jnp.float32), 0.5, 1.5).astype(jnp.bfloat16)
    norm_two_bias = centred(streams_of[10], (LAYERS, D), 0.2, 1.25, ((1, 8),))
    up_weight = centred(streams_of[11], (LAYERS, D, FF), D ** -0.5, 0.1875, ((1, 8),))
    up_bias = centred(streams_of[12], (LAYERS, FF), 0.3, 1.75, ((1, 8),))
    down_weight = centred(streams_of[13], (LAYERS, FF, D), FF ** -0.5, 0.09375, ((1, 8),))
    down_bias = centred(streams_of[14], (LAYERS, D), 0.2, 1.25, ((1, 8),))
    return dict(inputs=inputs, cotangent=cotangent, segments=segments, norm_one_gain=norm_one_gain, norm_one_bias=norm_one_bias, input_weight=input_weight, input_bias=input_bias, project_weight=project_weight, project_bias=project_bias, norm_two_gain=norm_two_gain, norm_two_bias=norm_two_bias, up_weight=up_weight, up_bias=up_bias, down_weight=down_weight, down_bias=down_bias)


@jax.custom_vjp
def low(v):
    return lax.optimization_barrier(v.astype(jnp.bfloat16)).astype(jnp.float32)

@jax.custom_vjp
def low_back(v):
    return v

def low_keep(v):
    return (low(v), None)

def low_pass(kept, grad):
    return (grad,)

def back_keep(v):
    return (v, None)

def back_low(kept, grad):
    return (low(grad),)
low.defvjp(low_keep, low_pass)
low_back.defvjp(back_keep, back_low)
exact_mode = lax.Precision.HIGHEST
masked_value = -1e+30

def layer_norm(values, gain, offset):
    average = lax.optimization_barrier(jnp.mean(values, axis=-1, keepdims=True))
    centered = values - average
    variance = lax.optimization_barrier(jnp.mean(centered * centered, axis=-1, keepdims=True))
    return centered * lax.rsqrt(variance + 1e-05) * gain + offset

def token_places(segment_ids):
    length = segment_ids.shape[0]
    token_index = jnp.arange(length, dtype=jnp.int32)
    numbers = jnp.arange(NCONT + 1, dtype=jnp.int32)
    member = segment_ids[None, :] == numbers[:, None]
    starts = lax.optimization_barrier(jnp.min(jnp.where(member, token_index[None, :], length), axis=1)).astype(jnp.int32)
    seg_start = lax.optimization_barrier(jnp.sum(jnp.where(member, starts[:, None], 0), axis=0)).astype(jnp.int32)
    prompt_shift = jnp.where(segment_ids > 0, PROMPT, 0).astype(jnp.int32)
    return (token_index - seg_start + prompt_shift).astype(jnp.int32)

def head_slopes():
    return jnp.exp2(-8.0 * (jnp.arange(HEADS, dtype=jnp.float32) + 1.0) / HEADS)

def attention(query_rows, key_rows, value_rows, segment_ids, places):
    length = query_rows.shape[0]
    token_index = jnp.arange(length, dtype=jnp.int32)
    visible = (token_index[None, :] <= token_index[:, None]) & ((segment_ids[None, :] == 0) | (segment_ids[None, :] == segment_ids[:, None]))
    query_heads = query_rows.reshape(length, HEADS, HEAD_DIM)
    key_heads = key_rows.reshape(length, HEADS, HEAD_DIM)
    value_heads = value_rows.reshape(length, HEADS, HEAD_DIM)
    raw_scores = jnp.einsum('qhd,khd->hqk', query_heads, key_heads, precision=exact_mode)
    distance = (places[None, :] - places[:, None]).astype(jnp.float32)
    scores = low_back(raw_scores * HEAD_DIM ** (-0.5) + head_slopes()[:, None, None] * distance[None])
    scores = jnp.where(visible[None], scores, masked_value)
    row_top = lax.optimization_barrier(jnp.max(scores, axis=2, keepdims=True))
    exponent = jnp.exp(scores - row_top)
    shares = exponent / lax.optimization_barrier(jnp.sum(exponent, axis=2, keepdims=True))
    context = jnp.einsum('hqk,khd->qhd', low(shares), value_heads, precision=exact_mode)
    return context.reshape(length, HEADS * HEAD_DIM)

def one_layer(hidden, params, segment_ids, places):
    norm_one_gain, norm_one_bias, input_weight, input_bias, project_weight, project_bias, norm_two_gain, norm_two_bias, up_weight, up_bias, down_weight, down_bias = params
    normed = low(layer_norm(hidden, norm_one_gain, norm_one_bias))
    projected = jnp.dot(normed, input_weight, precision=exact_mode, preferred_element_type=jnp.float32)
    query_rows = low(low_back(projected[:, :D] + input_bias[:D]))
    key_rows = low(low_back(projected[:, D:2 * D]))
    value_rows = low(low_back(projected[:, 2 * D:] + input_bias[D:]))
    context = low(low_back(attention(query_rows, key_rows, value_rows, segment_ids, places)))
    branch = low_back(jnp.dot(context, project_weight, precision=exact_mode, preferred_element_type=jnp.float32) + project_bias)
    middle = hidden + branch
    normed_two = low(layer_norm(middle, norm_two_gain, norm_two_bias))
    before = low_back(jnp.dot(normed_two, up_weight, precision=exact_mode, preferred_element_type=jnp.float32) + up_bias)
    activated = low(jax.nn.gelu(before, approximate=True))
    result = low_back(jnp.dot(activated, down_weight, precision=exact_mode, preferred_element_type=jnp.float32) + down_bias)
    return middle + result

def forward(inputs, segments, weights):

    def one_group(group_pair):
        hidden, segment_ids = group_pair
        places = token_places(segment_ids)
        for layer_num in range(LAYERS):
            params = tuple((stacked[layer_num] for stacked in weights))
            hidden = one_layer(hidden, params, segment_ids, places)
        return hidden
    return lax.map(jax.checkpoint(one_group), (inputs, segments))

def reference(inputs, cotangent, segments, norm_one_gain, norm_one_bias, input_weight, input_bias, project_weight, project_bias, norm_two_gain, norm_two_bias, up_weight, up_bias, down_weight, down_bias):
    weights = tuple((tensor.astype(jnp.float32) for tensor in (norm_one_gain, norm_one_bias, input_weight, input_bias, project_weight, project_bias, norm_two_gain, norm_two_bias, up_weight, up_bias, down_weight, down_bias)))

    def primal(hidden_in, *weight_list):
        return forward(hidden_in, segments, weight_list)
    block_output, pullback = jax.vjp(primal, inputs.astype(jnp.float32), *weights)
    gradients = pullback(cotangent.astype(jnp.float32))
    return (block_output, gradients[0], gradients[1], gradients[2], gradients[3], gradients[4], gradients[5], gradients[6], gradients[7], gradients[8], gradients[9], gradients[10], gradients[11], gradients[12])
```

```python
import functools

import jax
import jax.numpy as jnp
from jax import lax
from jax.experimental import pallas as pl
from jax.experimental.pallas import tpu as pltpu
from jax.sharding import Mesh
from jax.sharding import PartitionSpec as P

D = 1024
HEADS = 16
HEAD_DIM = 64
FF = 4096
PROMPT = 1024
TOKENS = 1536
PIECE = 192
LAYERS = 2
TILE = 256
HALF = 4 * PIECE
SCALE = HEAD_DIM ** (-0.5)
masked_value = -1e30

GRP = ("x", "y_lo", "core")
CTX = ("y_hi", "z")
bf16 = jnp.bfloat16
f32 = jnp.float32


def shift_z(value, step):
    return lax.ppermute(value, "z", [(i, (i + step) % 4) for i in range(4)])


def shift_x(value, step):
    return lax.ppermute(value, "x", [(i, (i + step) % 4) for i in range(4)])


def swap(value, axis):
    return lax.ppermute(value, axis, [(0, 1), (1, 0)])


def gather_z(rows):
    return jnp.concatenate([rows] + [shift_z(rows, k) for k in (1, 2, 3)], axis=0)


def scatter_z(own, others):
    total = own
    for k in (1, 2, 3):
        block = others[(k - 1) * PIECE : k * PIECE]
        total = total + shift_z(block, -k).astype(f32)
    return total


def dot(left, right):
    return jnp.dot(left, right, preferred_element_type=f32)


def dot_t(left, right):
    return lax.dot_general(left, right, (((1,), (1,)), ((), ())), preferred_element_type=f32)


def outer(left, right):
    return lax.dot_general(left, right, (((0,), (0,)), ((), ())), preferred_element_type=f32)


def dot_scatter(left, weight, product):
    others = product(left[PIECE:], weight).astype(bf16)
    own = product(left[:PIECE], weight)
    return scatter_z(own, others)


def tile_mask(block, low, high, cut):
    keys = lax.broadcasted_iota(jnp.int32, (high - low, TILE), 0) + low
    queries = lax.broadcasted_iota(jnp.int32, (high - low, TILE), 1) + block * TILE
    visible = keys <= queries
    if block * TILE >= PROMPT:
        visible = visible & ((keys >= cut) | (queries < cut))
    return visible


def fill_bias(bias, slopes, cut):
    keys = lax.broadcasted_iota(jnp.int32, (TOKENS, 128), 0)
    places = jnp.where(keys >= cut, keys - cut + PROMPT, keys).astype(f32)
    for h in range(2):
        bias[h] = places * slopes[h]


def scores_t(keys, queries, bias, block, high, cut):
    low = min(block * TILE, PROMPT)
    scores = dot_t(keys, queries)
    scores = scores + jnp.concatenate([bias[0:high], bias[0:high]], axis=1)
    tail = jnp.where(tile_mask(block, low, high, cut), scores[low:high], masked_value)
    if low == 0:
        return tail
    return jnp.concatenate([scores[:low], tail], axis=0)


def piece_places(info):
    y, z = info[0], info[1]
    out = []
    for side in range(2):
        y_of = y if side == 0 else 1 - y
        for k in range(4):
            out.append(pl.multiple_of((y_of * 4 + ((z - k) & 3)) * PIECE, 64))
    return out


def attend_kernel(info, slopes, mine, other, ctx_mine, ctx_other, logsum, rows, ctx, vt, bias):
    spots = piece_places(info)
    cut = info[2]
    for k in range(4):
        span = slice(k * PIECE, (k + 1) * PIECE)
        rows[pl.ds(spots[k], PIECE), :] = mine[span, :]
        rows[pl.ds(spots[4 + k], PIECE), :] = other[span, :]
    fill_bias(bias, slopes, cut)
    vt[...] = rows[:, 256:384].astype(f32).T.astype(bf16)
    for block in range(TOKENS // TILE):
        high = (block + 1) * TILE
        span = slice(block * TILE, high)
        parts = []
        for h in range(2):
            lanes = slice(h * HEAD_DIM, (h + 1) * HEAD_DIM)
            key_lanes = slice(128 + h * HEAD_DIM, 128 + (h + 1) * HEAD_DIM)
            queries = rows[span, lanes] * jnp.asarray(SCALE, bf16)
            scores = scores_t(rows[0:high, key_lanes], queries, bias[h], block, high, cut)
            top = jnp.max(scores, axis=0, keepdims=True)
            weights = jnp.exp(scores - top)
            total = jnp.sum(weights, axis=0, keepdims=True)
            found = dot(vt[lanes, 0:high], weights.astype(bf16))
            parts.append(found * (1.0 / total))
            logsum[h : h + 1, span] = top + jnp.log(total)
        ctx[span, :] = jnp.concatenate(parts, axis=0).T.astype(bf16)
    for k in range(4):
        span = slice(k * PIECE, (k + 1) * PIECE)
        ctx_mine[span, :] = ctx[pl.ds(spots[k], PIECE), :]
        ctx_other[span, :] = ctx[pl.ds(spots[4 + k], PIECE), :]


def attend_back_kernel(
    info, slopes, rows, mine, other, logsum, out_mine, out_other, sums, grad, kt, bias, dq, dk, dv, out
):
    spots = piece_places(info)
    cut = info[2]
    for k in range(4):
        span = slice(k * PIECE, (k + 1) * PIECE)
        grad[pl.ds(spots[k], PIECE), :] = mine[span, :]
        grad[pl.ds(spots[4 + k], PIECE), :] = other[span, :]
    fill_bias(bias, slopes, cut)
    kt[...] = rows[:, 128:256].astype(f32).T.astype(bf16)
    dk[...] = jnp.zeros_like(dk)
    dv[...] = jnp.zeros_like(dv)
    for block in range(TOKENS // TILE):
        high = (block + 1) * TILE
        span = slice(block * TILE, high)
        parts = []
        for h in range(2):
            lanes = slice(h * HEAD_DIM, (h + 1) * HEAD_DIM)
            key_lanes = slice(128 + h * HEAD_DIM, 128 + (h + 1) * HEAD_DIM)
            value_lanes = slice(256 + h * HEAD_DIM, 256 + (h + 1) * HEAD_DIM)
            queries = rows[span, lanes] * jnp.asarray(SCALE, bf16)
            grads = grad[span, lanes]
            scores = scores_t(rows[0:high, key_lanes], queries, bias[h], block, high, cut)
            weights = jnp.exp(scores - logsum[h : h + 1, span])
            d_weights = dot_t(rows[0:high, value_lanes], grads)
            correction = jnp.sum(weights * d_weights, axis=0, keepdims=True)
            d_scores = (weights * (d_weights - correction)).astype(bf16)
            dv[h, 0:high, :] += dot(weights.astype(bf16), grads)
            dk[h, 0:high, :] += dot(d_scores, queries)
            parts.append(dot(kt[lanes, 0:high], d_scores))
        dq[span, :] = (jnp.concatenate(parts, axis=0) * SCALE).T
    out[:, 0:128] = dq[...].astype(bf16)
    out[:, 128:256] = jnp.concatenate([dk[0], dk[1]], axis=1).astype(bf16)
    out[:, 256:384] = jnp.concatenate([dv[0], dv[1]], axis=1).astype(bf16)
    sums[...] = jnp.sum(out[...].astype(f32), axis=0, keepdims=True)
    for k in range(4):
        span = slice(k * PIECE, (k + 1) * PIECE)
        out_mine[span, :] = out[pl.ds(spots[k], PIECE), :]
        out_other[span, :] = out[pl.ds(spots[4 + k], PIECE), :]


smem = pl.BlockSpec(memory_space=pltpu.SMEM)
vmem = pl.BlockSpec(memory_space=pltpu.VMEM)
LIMIT = 40 * 2**20


def attend(info, slopes, mine, other):
    return pl.pallas_call(
        attend_kernel,
        out_shape=(
            jax.ShapeDtypeStruct((HALF, 128), bf16),
            jax.ShapeDtypeStruct((HALF, 128), bf16),
            jax.ShapeDtypeStruct((2, TOKENS), f32),
            jax.ShapeDtypeStruct((TOKENS, 384), bf16),
        ),
        in_specs=[smem, smem, vmem, vmem],
        out_specs=(vmem, vmem, vmem, vmem),
        scratch_shapes=[
            pltpu.VMEM((TOKENS, 128), bf16),
            pltpu.VMEM((128, TOKENS), bf16),
            pltpu.VMEM((2, TOKENS, 128), f32),
        ],
        compiler_params=pltpu.CompilerParams(vmem_limit_bytes=LIMIT),
        cost_estimate=pl.CostEstimate(
            flops=4 * 2 * 1400000 * 64, bytes_accessed=3000000, transcendentals=2800000
        ),
        name="attend",
    )(info, slopes, mine, other)


def attend_back(info, slopes, rows, mine, other, logsum):
    return pl.pallas_call(
        attend_back_kernel,
        out_shape=(
            jax.ShapeDtypeStruct((HALF, 384), bf16),
            jax.ShapeDtypeStruct((HALF, 384), bf16),
            jax.ShapeDtypeStruct((1, 384), f32),
        ),
        in_specs=[smem, smem, vmem, vmem, vmem, vmem],
        out_specs=(vmem, vmem, vmem),
        scratch_shapes=[
            pltpu.VMEM((TOKENS, 128), bf16),
            pltpu.VMEM((128, TOKENS), bf16),
            pltpu.VMEM((2, TOKENS, 128), f32),
            pltpu.VMEM((TOKENS, 128), f32),
            pltpu.VMEM((2, TOKENS, HEAD_DIM), f32),
            pltpu.VMEM((2, TOKENS, HEAD_DIM), f32),
            pltpu.VMEM((TOKENS, 384), bf16),
        ],
        compiler_params=pltpu.CompilerParams(vmem_limit_bytes=LIMIT),
        cost_estimate=pl.CostEstimate(
            flops=10 * 2 * 1400000 * 64, bytes_accessed=5000000, transcendentals=2800000
        ),
        name="attend_back",
    )(info, slopes, rows, mine, other, logsum)


def norm_parts(values):
    average = jnp.mean(values, axis=-1, keepdims=True)
    centered = values - average
    variance = jnp.mean(centered * centered, axis=-1, keepdims=True)
    scale = lax.rsqrt(variance + 1e-05)
    return centered * scale, scale


def norm(values, gain, offset):
    return norm_parts(values)[0] * gain + offset


def norm_back(values, gain, grads):
    unit, scale = norm_parts(values)
    weighted = grads * gain
    mean_one = jnp.mean(weighted, axis=-1, keepdims=True)
    mean_two = jnp.mean(weighted * unit, axis=-1, keepdims=True)
    d_values = scale * (weighted - mean_one - unit * mean_two)
    return d_values, jnp.sum(grads * unit, axis=0), jnp.sum(grads, axis=0)


def gelu(values):
    return jax.nn.gelu(values, approximate=True)


def core_join(half, core):
    other = swap(half, "core")
    return jnp.where(
        core == 0, jnp.stack([half, other], axis=1), jnp.stack([other, half], axis=1)
    )


def columns_for_all(weight, parts):
    rows = weight.shape[0]
    split = weight.reshape(rows, parts, 8, -1)
    out = []
    for place in range(8):
        own = split[:, :, place].reshape(rows, -1)
        other = split[:, :, (place + 4) % 8].reshape(rows, -1)
        out.append(jnp.concatenate([own, other], axis=1))
    return jnp.stack(out)


def to_ctx(value):
    return lax.all_to_all(value, CTX, split_axis=0, concat_axis=0, tiled=True)


def core_half(value, core, axis):
    size = value.shape[axis] // 2
    return lax.dynamic_slice_in_dim(value, core * size, size, axis)


def gather_columns(blocks, core):
    got = to_ctx(core_half(blocks, core, 1))
    return core_join(got, core).reshape(D, -1)


def gather_rows(rows, core):
    got = swap(core_half(rows, core, 0), "y_hi")
    return core_join(got[None], core).reshape(rows.shape)


def forward(hidden, normed_all, params, info, slopes):
    (_, _, w_own, w_other, bias_own, bias_other, project, project_bias) = params[:8]
    (gain_two, offset_two, up, up_bias, down, down_bias) = params[8:]
    other = (dot(normed_all, w_other) + bias_other).astype(bf16)
    received = swap(other, "y_hi")
    mine = (dot(normed_all, w_own) + bias_own).astype(bf16)
    ctx_mine, ctx_other, logsum, rows = attend(info, slopes, mine, received)
    context = jnp.concatenate([ctx_mine, swap(ctx_other, "y_hi")], axis=1)
    middle = hidden + dot_scatter(context, project, dot) + project_bias
    normed_two = gather_z(norm(middle, gain_two, offset_two).astype(bf16))
    before = dot(normed_two, up) + up_bias
    activated = gelu(before).astype(bf16)
    result = middle + dot_scatter(activated, down, dot) + down_bias
    kept = (hidden, normed_all, logsum, rows, context, middle, normed_two, before, activated)
    return result, kept


def backward(gradient, params, kept, info, slopes):
    (gain_one, _, w_own, w_other, _, _, project, _) = params[:8]
    (gain_two, _, up, _, down, _) = params[8:]
    hidden, normed_all, logsum, rows, context, middle, normed_two, before, activated = kept
    grad_low = gradient.astype(bf16)
    grad_down = gather_z(grad_low)
    sum_down = jnp.sum(grad_low.astype(f32), axis=0)
    d_act = dot_t(grad_down, down)
    d_before = jax.vjp(gelu, before)[1](d_act)[0].astype(bf16)
    sum_up = jnp.sum(d_before.astype(f32), axis=0)
    d_normed = dot_scatter(d_before, up, dot_t)
    g_down = outer(activated, grad_down)
    g_up = outer(normed_two, d_before)
    d_values, sum_gain_two, sum_offset_two = norm_back(middle, gain_two, d_normed)
    d_middle = gradient + d_values
    grad_out = d_middle.astype(bf16)
    grad_out_all = gather_z(grad_out)
    sum_project = jnp.sum(grad_out.astype(f32), axis=0)
    ctx_other = dot_t(grad_out_all, project[128:]).astype(bf16)
    received = swap(ctx_other, "y_hi")
    ctx_mine = dot_t(grad_out_all, project[:128]).astype(bf16)
    g_project = outer(context, grad_out_all)
    d_mine, d_other, sums = attend_back(info, slopes, rows, ctx_mine, received, logsum)
    d_received = swap(d_other, "y_hi")
    d_joined = jnp.concatenate([d_mine, d_received], axis=1)
    w_both = jnp.concatenate([w_own, w_other], axis=1)
    d_normed_one = dot_scatter(d_joined, w_both, dot_t)
    g_input = outer(normed_all, d_joined)
    d_hidden, sum_gain_one, sum_offset_one = norm_back(hidden, gain_one, d_normed_one)
    big = (g_down, g_up, g_project, g_input)
    small = (
        sum_gain_one,
        sum_offset_one,
        sum_project,
        sum_gain_two,
        sum_offset_two,
        sum_down,
        sums,
        sum_up,
    )
    return d_middle + d_hidden, big, small


def other_half_first(value, width):
    return jnp.concatenate([value[..., width:], value[..., :width]], axis=-1)


def finish(down, up, project, inputs, y_hi, z):
    if down is not None:
        down = down[0].astype(f32) + swap(down[1], "y_hi").astype(f32)
        project = project[0].astype(f32) + swap(project[1], "y_hi").astype(f32)
    both = inputs if up is None else jnp.concatenate([up, inputs], axis=-1)
    return down, project, both


def spread_rows(both, widths, y_hi):
    keep = lax.dynamic_slice_in_dim(both, y_hi * 4, 4, 0).astype(f32)
    send = lax.dynamic_slice_in_dim(both, (1 - y_hi) * 4, 4, 0)
    got = swap(send, "y_hi")
    at = 0
    pieces = []
    for width in widths:
        pieces.append(other_half_first(got[..., at : at + width], width // 2))
        at += width
    total = (keep + jnp.concatenate(pieces, axis=-1).astype(f32)).astype(bf16)
    return lax.all_to_all(total, "z", split_axis=0, concat_axis=0, tiled=True)


def order_columns(rows, parts, y_hi):
    *lead, four, count, width = rows.shape
    split = rows.reshape(*lead, four, count, 2, parts, width // (2 * parts))
    split = jnp.where(y_hi == 0, split, split[..., ::-1, :, :])
    return split


def reduce_grp(pack):
    return lax.psum_scatter(pack, GRP, scatter_dimension=0, tiled=True)


def rows_by_group(value):
    return value.reshape(8, 16, 8, -1).transpose(1, 0, 2, 3).reshape(16, 64, -1)


def pack_big(g_down, g_up, g_project, g_input):
    pieces = [
        g_down.reshape(2, 16, 32, D).transpose(1, 0, 2, 3).reshape(16, 64, D),
        rows_by_group(g_up),
        g_project.reshape(2, 16, 8, 4, 256).transpose(1, 0, 2, 3, 4).reshape(16, 64, 256),
    ]
    if g_input is not None:
        pieces.append(rows_by_group(g_input))
    return jnp.concatenate([piece.astype(bf16) for piece in pieces], axis=-1)


def reduce_big(g_down, g_up, g_project, g_input, y_hi):
    packed = reduce_grp(pack_big(g_down, g_up, g_project, g_input)).reshape(64, -1)
    rows = jnp.concatenate([packed[:, :D], packed[:, 2 * D : 2 * D + 256]], axis=1)
    rows = rows.reshape(2, 32, D + 256)
    rows = rows[0].astype(f32) + swap(rows[1], "y_hi").astype(f32)
    widths = [D]
    both = packed[:, D : 2 * D]
    if g_input is not None:
        both = jnp.concatenate([both, packed[:, 2 * D + 256 :]], axis=1)
        widths.append(768)
    columns = spread_rows(both.reshape(8, 8, -1), widths, y_hi)
    full = jnp.concatenate([rows.astype(bf16), columns.reshape(32, -1)], axis=1)
    full = lax.all_gather(full, GRP, axis=0, tiled=False).astype(f32)
    down = full[:, :, :D].reshape(512, D)
    project = full[:, :, D : D + 256].reshape(16 * 8, D)
    up = input_columns(full[:, :, D + 256 : 2 * D + 256], 1, y_hi)
    inputs = None
    if g_input is not None:
        inputs = input_columns(full[:, :, 2 * D + 256 :], 3, y_hi)
    return down, up, project, inputs


def input_columns(rows, parts, y_hi):
    split = rows.reshape(16, 4, 8, 2, parts, -1)
    split = jnp.where(y_hi == 0, split, split[:, :, :, ::-1])
    return split.transpose(0, 2, 4, 3, 1, 5).reshape(128, -1)


def reduce_input(g_input, y_hi, x, y_lo, core):
    low = g_input.astype(bf16).reshape(8, 4, 2, 2, 8, 768)
    take = lambda value, at, axis: lax.dynamic_index_in_dim(value, at, axis, keepdims=False)
    total = take(low, core, 3).astype(f32) + swap(take(low, 1 - core, 3), "core").astype(f32)
    low = total.astype(bf16)
    total = take(total, x, 1)
    for k in (1, 2, 3):
        total = total + shift_x(take(low, (x + k) % 4, 1), k).astype(f32)
    low = total.astype(bf16)
    total = take(total, y_lo, 1) + swap(take(low, 1 - y_lo, 1), "y_lo").astype(f32)
    columns = spread_rows(total.astype(bf16), [768], y_hi).reshape(32, 768)
    full = lax.all_gather(columns, GRP, axis=0, tiled=False).astype(f32)
    return input_columns(full, 3, y_hi)


def pack_small(small, place):
    (gain_one, offset_one, project, gain_two, offset_two, down, sums, up) = small
    vectors = [
        v.reshape(8, 128) for v in (gain_one, offset_one, project, gain_two, offset_two, down)
    ]
    sums = sums.reshape(-1)
    inputs = lax.dynamic_update_slice_in_dim(jnp.zeros((2 * D,), f32), sums[:128], place * 128, 0)
    inputs = lax.dynamic_update_slice_in_dim(inputs, sums[256:], D + place * 128, 0)
    units = jnp.zeros((8, 512), f32)
    units = lax.dynamic_update_slice_in_dim(units, up[None, :512], place, 0)
    units = lax.dynamic_update_slice_in_dim(units, up[None, 512:], (place + 4) % 8, 0)
    return jnp.concatenate(vectors + [inputs.reshape(8, 256), units], axis=1)


def on_device(
    inputs,
    cotangent,
    segments,
    norm_one_gain,
    norm_one_bias,
    input_weight,
    input_bias,
    project_weight,
    project_bias,
    norm_two_gain,
    norm_two_bias,
    up_weight,
    up_bias,
    down_weight,
    down_bias,
):
    y_hi, z = lax.axis_index("y_hi"), lax.axis_index("z")
    x, y_lo, core = lax.axis_index("x"), lax.axis_index("y_lo"), lax.axis_index("core")
    place = y_hi * 4 + z
    cut = jnp.sum((segments[0] < 2).astype(jnp.int32))
    info = jnp.stack([y_hi, z, cut]).astype(jnp.int32)
    heads = (place * 2 + jnp.arange(2, dtype=jnp.int32)).astype(f32)
    slopes = jnp.exp2(-8.0 * (heads + 1.0) / HEADS)

    raw_all = gather_z(inputs[0])
    small = jnp.concatenate(
        [
            norm_one_gain,
            norm_one_bias,
            project_bias,
            norm_two_gain,
            norm_two_bias,
            down_bias,
            input_bias,
            up_bias,
        ],
        axis=1,
    )
    small = jnp.concatenate([small.reshape(4, 768), jnp.zeros((12, 768), bf16)], axis=0)
    first = core_half(columns_for_all(input_weight[0], 3), core, 1)
    first = jnp.concatenate([first, jnp.broadcast_to(small[None], (8, 16, 768))], axis=1)
    first = to_ctx(first)
    small = first[:, 64:68].reshape(8, LAYERS, -1).transpose(1, 0, 2).astype(f32)
    w_first = core_join(first[:, :64], core).reshape(D, 768)
    up_first = gather_columns(columns_for_all(up_weight[0], 1), core)
    second = gather_columns(
        jnp.concatenate(
            [columns_for_all(input_weight[1], 3), columns_for_all(up_weight[1], 1)], axis=2
        ),
        core,
    )
    w_all = (w_first, second[:, :768])
    up_all = (up_first, second[:, 768:])

    layers = []
    for layer in range(LAYERS):
        rows = jnp.concatenate([down_weight[layer], project_weight[layer]], axis=0)
        rows_other = gather_rows(rows, core)
        down = jnp.concatenate([rows[:512], rows_other[:512]], axis=0)
        project = jnp.concatenate([rows[512:], rows_other[512:]], axis=0)
        vectors = [small[layer, :, i * 128 : (i + 1) * 128].reshape(D) for i in range(6)]
        in_bias = small[layer, :, 768:1024].reshape(2 * D)
        unit_bias = small[layer, :, 1024:1536]

        def bias_of(at):
            query = lax.dynamic_slice_in_dim(in_bias, at * 128, 128)
            value = lax.dynamic_slice_in_dim(in_bias, D + at * 128, 128)
            return jnp.concatenate([query, jnp.zeros((128,), f32), value])

        partner = (place + 4) % 8
        unit = jnp.concatenate(
            [
                lax.dynamic_index_in_dim(unit_bias, place, 0, keepdims=False),
                lax.dynamic_index_in_dim(unit_bias, partner, 0, keepdims=False),
            ]
        )
        layers.append(
            (
                vectors[0],
                vectors[1],
                w_all[layer][:, :384],
                w_all[layer][:, 384:],
                bias_of(place),
                bias_of(partner),
                project,
                vectors[2],
                vectors[3],
                vectors[4],
                up_all[layer],
                unit,
                down,
                vectors[5],
            )
        )

    hidden = inputs[0].astype(f32)
    kept = []
    for layer in range(LAYERS):
        params = layers[layer]
        if layer == 0:
            normed_all = norm(raw_all.astype(f32), params[0], params[1]).astype(bf16)
        else:
            normed_all = gather_z(norm(hidden, params[0], params[1]).astype(bf16))
        hidden, state = forward(hidden, normed_all, params, info, slopes)
        kept.append(state)
    gradient = cotangent[0].astype(f32)
    bigs = [None] * LAYERS
    smalls = [None] * LAYERS
    for layer in (1, 0):
        gradient, big, smalls[layer] = backward(gradient, layers[layer], kept[layer], info, slopes)
        if layer == 1:
            bigs[1] = reduce_big(*big, y_hi)
        else:
            down, up, project, _ = reduce_big(*big[:3], None, y_hi)
            bigs[0] = (down, up, project, reduce_input(big[3], y_hi, x, y_lo, core))
    packed = jnp.concatenate([pack_small(s, place) for s in smalls], axis=1)
    vector = jnp.sum(to_ctx(packed), axis=0)
    vector = jnp.sum(lax.all_gather(vector.reshape(8, -1), GRP, axis=0, tiled=False), axis=0)
    vector = vector.reshape(LAYERS, -1)
    parts = [vector[:, i * 128 : (i + 1) * 128] for i in range(6)]
    both = [jnp.stack([bigs[0][i], bigs[1][i]]) for i in range(4)]
    return (
        hidden[None],
        gradient[None],
        parts[0],
        parts[1],
        both[3],
        vector[:, 768:1024],
        both[2],
        parts[2],
        parts[3],
        parts[4],
        both[1],
        vector[:, 1024:1536],
        both[0],
        parts[5],
    )


def solution(mesh):
    split = Mesh(mesh.devices.reshape(4, 2, 2, 2, 4), GRP + CTX)
    rows = P(GRP, CTX, None)
    vector = P(None, CTX)
    matrix = P(None, CTX, None)
    weights = (
        vector,
        vector,
        matrix,
        vector,
        matrix,
        vector,
        vector,
        vector,
        matrix,
        vector,
        matrix,
        vector,
    )
    return jax.shard_map(
        on_device,
        mesh=split,
        in_specs=(rows, rows, P(GRP, None)) + weights,
        out_specs=(rows, rows) + weights,
        check_vma=False,
    )
```

```python
import functools

import jax
import jax.numpy as jnp
from jax import lax
from jax.experimental import pallas as pl
from jax.experimental.pallas import tpu as pltpu
from jax.sharding import Mesh
from jax.sharding import PartitionSpec as P

D = 1024
HEADS = 16
HEAD_DIM = 64
FF = 4096
PROMPT = 1024
TOKENS = 1536
PIECE = 192
LAYERS = 2
TILE = 256
HALF = 4 * PIECE
SCALE = HEAD_DIM ** (-0.5)
masked_value = -1e30

GRP = ("x", "y_lo", "core")
CTX = ("y_hi", "z")
bf16 = jnp.bfloat16
f32 = jnp.float32


def shift_z(value, step):
    return lax.ppermute(value, "z", [(i, (i + step) % 4) for i in range(4)])


def shift_x(value, step):
    return lax.ppermute(value, "x", [(i, (i + step) % 4) for i in range(4)])


def swap(value, axis):
    return lax.ppermute(value, axis, [(0, 1), (1, 0)])


def regroup(value, core, y_hi):
    got = lax.ppermute(value, ("core", "y_hi"), [(1, 2), (2, 1)])
    return jnp.where(core == y_hi, value, got)


def after(value, *others):
    return lax.optimization_barrier((value, others))[0]


def gather_z(rows):
    return jnp.concatenate([rows] + [shift_z(rows, k) for k in (1, 2, 3)], axis=0)


def scatter_z(own, others):
    total = own
    for k in (1, 2, 3):
        block = others[(k - 1) * PIECE : k * PIECE]
        total = total + shift_z(block, -k).astype(f32)
    return total


def dot(left, right):
    return jnp.dot(left, right, preferred_element_type=f32)


def dot_t(left, right):
    return lax.dot_general(left, right, (((1,), (1,)), ((), ())), preferred_element_type=f32)


def outer(left, right):
    return lax.dot_general(left, right, (((0,), (0,)), ((), ())), preferred_element_type=f32)


def dot_scatter(left, weight, product):
    others = product(left[PIECE:], weight).astype(bf16)
    own = product(left[:PIECE], weight)
    return scatter_z(own, others)


def tile_mask(block, low, high, cut):
    keys = lax.broadcasted_iota(jnp.int32, (high - low, TILE), 0) + low
    queries = lax.broadcasted_iota(jnp.int32, (high - low, TILE), 1) + block * TILE
    visible = keys <= queries
    if block * TILE >= PROMPT:
        visible = visible & ((keys >= cut) | (queries < cut))
    return visible


def fill_bias(bias, slopes, cut):
    keys = lax.broadcasted_iota(jnp.int32, (TOKENS, 128), 0)
    places = jnp.where(keys >= cut, keys - cut + PROMPT, keys).astype(f32)
    for h in range(2):
        bias[h] = places * slopes[h]


def scores_t(keys, queries, bias, block, high, cut):
    low = min(block * TILE, PROMPT)
    scores = dot_t(keys, queries)
    scores = scores + jnp.concatenate([bias[0:high], bias[0:high]], axis=1)
    tail = jnp.where(tile_mask(block, low, high, cut), scores[low:high], masked_value)
    if low == 0:
        return tail
    return jnp.concatenate([scores[:low], tail], axis=0)


def piece_places(info):
    core, z = info[0], info[1]
    out = []
    for side in range(2):
        half = core if side == 0 else 1 - core
        for k in range(4):
            out.append(pl.multiple_of((half * 4 + ((z - k) & 3)) * PIECE, 64))
    return out


def attend_kernel(info, slopes, mine, other, ctx_mine, ctx_other, logsum, rows, ctx, vt, bias):
    spots = piece_places(info)
    cut = info[2]
    for k in range(4):
        span = slice(k * PIECE, (k + 1) * PIECE)
        rows[pl.ds(spots[k], PIECE), :] = mine[span, :]
        rows[pl.ds(spots[4 + k], PIECE), :] = other[span, :]
    fill_bias(bias, slopes, cut)
    vt[...] = rows[:, 256:384].astype(f32).T.astype(bf16)
    for block in range(TOKENS // TILE):
        high = (block + 1) * TILE
        span = slice(block * TILE, high)
        parts = []
        for h in range(2):
            lanes = slice(h * HEAD_DIM, (h + 1) * HEAD_DIM)
            key_lanes = slice(128 + h * HEAD_DIM, 128 + (h + 1) * HEAD_DIM)
            queries = rows[span, lanes] * jnp.asarray(SCALE, bf16)
            scores = scores_t(rows[0:high, key_lanes], queries, bias[h], block, high, cut)
            top = jnp.max(scores, axis=0, keepdims=True)
            weights = jnp.exp(scores - top)
            total = jnp.sum(weights, axis=0, keepdims=True)
            found = dot(vt[lanes, 0:high], weights.astype(bf16))
            parts.append(found * (1.0 / total))
            logsum[h : h + 1, span] = top + jnp.log(total)
        ctx[span, :] = jnp.concatenate(parts, axis=0).T.astype(bf16)
    for k in range(4):
        span = slice(k * PIECE, (k + 1) * PIECE)
        ctx_mine[span, :] = ctx[pl.ds(spots[k], PIECE), :]
        ctx_other[span, :] = ctx[pl.ds(spots[4 + k], PIECE), :]


def attend_back_kernel(
    info, slopes, rows, mine, other, logsum, out_mine, out_other, sums, grad, kt, bias, dq, dk, dv, out
):
    spots = piece_places(info)
    cut = info[2]
    for k in range(4):
        span = slice(k * PIECE, (k + 1) * PIECE)
        grad[pl.ds(spots[k], PIECE), :] = mine[span, :]
        grad[pl.ds(spots[4 + k], PIECE), :] = other[span, :]
    fill_bias(bias, slopes, cut)
    kt[...] = rows[:, 128:256].astype(f32).T.astype(bf16)
    dk[...] = jnp.zeros_like(dk)
    dv[...] = jnp.zeros_like(dv)
    for block in range(TOKENS // TILE):
        high = (block + 1) * TILE
        span = slice(block * TILE, high)
        parts = []
        for h in range(2):
            lanes = slice(h * HEAD_DIM, (h + 1) * HEAD_DIM)
            key_lanes = slice(128 + h * HEAD_DIM, 128 + (h + 1) * HEAD_DIM)
            value_lanes = slice(256 + h * HEAD_DIM, 256 + (h + 1) * HEAD_DIM)
            queries = rows[span, lanes] * jnp.asarray(SCALE, bf16)
            grads = grad[span, lanes]
            scores = scores_t(rows[0:high, key_lanes], queries, bias[h], block, high, cut)
            weights = jnp.exp(scores - logsum[h : h + 1, span])
            d_weights = dot_t(rows[0:high, value_lanes], grads)
            correction = jnp.sum(weights * d_weights, axis=0, keepdims=True)
            d_scores = (weights * (d_weights - correction)).astype(bf16)
            dv[h, 0:high, :] += dot(weights.astype(bf16), grads)
            dk[h, 0:high, :] += dot(d_scores, queries)
            parts.append(dot(kt[lanes, 0:high], d_scores))
        dq[span, :] = (jnp.concatenate(parts, axis=0) * SCALE).T
    out[:, 0:128] = dq[...].astype(bf16)
    out[:, 128:256] = jnp.concatenate([dk[0], dk[1]], axis=1).astype(bf16)
    out[:, 256:384] = jnp.concatenate([dv[0], dv[1]], axis=1).astype(bf16)
    sums[...] = jnp.sum(out[...].astype(f32), axis=0, keepdims=True)
    for k in range(4):
        span = slice(k * PIECE, (k + 1) * PIECE)
        out_mine[span, :] = out[pl.ds(spots[k], PIECE), :]
        out_other[span, :] = out[pl.ds(spots[4 + k], PIECE), :]


smem = pl.BlockSpec(memory_space=pltpu.SMEM)
vmem = pl.BlockSpec(memory_space=pltpu.VMEM)
LIMIT = 40 * 2**20


def attend(info, slopes, mine, other):
    return pl.pallas_call(
        attend_kernel,
        out_shape=(
            jax.ShapeDtypeStruct((HALF, 128), bf16),
            jax.ShapeDtypeStruct((HALF, 128), bf16),
            jax.ShapeDtypeStruct((2, TOKENS), f32),
            jax.ShapeDtypeStruct((TOKENS, 384), bf16),
        ),
        in_specs=[smem, smem, vmem, vmem],
        out_specs=(vmem, vmem, vmem, vmem),
        scratch_shapes=[
            pltpu.VMEM((TOKENS, 128), bf16),
            pltpu.VMEM((128, TOKENS), bf16),
            pltpu.VMEM((2, TOKENS, 128), f32),
        ],
        compiler_params=pltpu.CompilerParams(vmem_limit_bytes=LIMIT),
        cost_estimate=pl.CostEstimate(
            flops=4 * 2 * 1400000 * 64, bytes_accessed=3000000, transcendentals=2800000
        ),
        name="attend",
    )(info, slopes, mine, other)


def attend_back(info, slopes, rows, mine, other, logsum):
    return pl.pallas_call(
        attend_back_kernel,
        out_shape=(
            jax.ShapeDtypeStruct((HALF, 384), bf16),
            jax.ShapeDtypeStruct((HALF, 384), bf16),
            jax.ShapeDtypeStruct((1, 384), f32),
        ),
        in_specs=[smem, smem, vmem, vmem, vmem, vmem],
        out_specs=(vmem, vmem, vmem),
        scratch_shapes=[
            pltpu.VMEM((TOKENS, 128), bf16),
            pltpu.VMEM((128, TOKENS), bf16),
            pltpu.VMEM((2, TOKENS, 128), f32),
            pltpu.VMEM((TOKENS, 128), f32),
            pltpu.VMEM((2, TOKENS, HEAD_DIM), f32),
            pltpu.VMEM((2, TOKENS, HEAD_DIM), f32),
            pltpu.VMEM((TOKENS, 384), bf16),
        ],
        compiler_params=pltpu.CompilerParams(vmem_limit_bytes=LIMIT),
        cost_estimate=pl.CostEstimate(
            flops=10 * 2 * 1400000 * 64, bytes_accessed=5000000, transcendentals=2800000
        ),
        name="attend_back",
    )(info, slopes, rows, mine, other, logsum)


def norm_parts(values):
    average = jnp.mean(values, axis=-1, keepdims=True)
    centered = values - average
    variance = jnp.mean(centered * centered, axis=-1, keepdims=True)
    scale = lax.rsqrt(variance + 1e-05)
    return centered * scale, scale


def norm(values, gain, offset):
    return norm_parts(values)[0] * gain + offset


def norm_back(values, gain, grads):
    unit, scale = norm_parts(values)
    weighted = grads * gain
    mean_one = jnp.mean(weighted, axis=-1, keepdims=True)
    mean_two = jnp.mean(weighted * unit, axis=-1, keepdims=True)
    d_values = scale * (weighted - mean_one - unit * mean_two)
    return d_values, jnp.sum(grads * unit, axis=0), jnp.sum(grads, axis=0)


def gelu(values):
    return jax.nn.gelu(values, approximate=True)


def pack_first_kernel(info, weight, small, out):
    core = info[0]
    rows = pl.ds(pl.multiple_of(core * 64, 64), 64)
    for place in range(8):
        for side in range(2):
            for part in range(3):
                at = part * D + side * 512 + (place % 4) * 128
                to = (side * 3 + part) * 128
                out[place, 0:64, to : to + 128] = weight[0, rows, at : at + 128]
        out[place, 64:80, :] = small[...]


def pack_rest_kernel(info, weight, up, down, project, first, second, rows_first, rows_second):
    core = info[0]
    rows = pl.ds(pl.multiple_of(core * 64, 64), 64)
    for place in range(8):
        for side in range(2):
            at = side * 2048 + (place % 4) * 512
            to = side * 512
            first[place, :, to : to + 512] = up[0, rows, at : at + 512]
            second[place, :, to : to + 512] = up[1, rows, at : at + 512]
            for part in range(3):
                at = part * D + side * 512 + (place % 4) * 128
                to = D + (side * 3 + part) * 128
                second[place, :, to : to + 128] = weight[0, rows, at : at + 128]
    long = pl.ds(pl.multiple_of(core * 256, 64), 256)
    for layer, out in ((0, rows_first), (1, rows_second)):
        out[0:256, :] = down[layer, long, :]
        out[256:320, :] = project[layer, rows, :]


def join_columns_kernel(info, got, other, *outs):
    core = info[0]
    at = 0
    for out in outs:
        width = out.shape[1]
        for place in range(8):
            mine = pl.multiple_of(place * 128 + core * 64, 64)
            theirs = pl.multiple_of(place * 128 + (1 - core) * 64, 64)
            out[pl.ds(mine, 64), :] = got[place, 0:64, at : at + width]
            out[pl.ds(theirs, 64), :] = other[place, 0:64, at : at + width]
        at += width


def join_rows_kernel(info, down, project, got, other, down_out, project_out):
    core, y_hi = info[0], info[3]
    for out, own, size, at in ((down_out, down, 512, 0), (project_out, project, 128, 256)):
        half = size // 2
        out[pl.ds(pl.multiple_of(y_hi * size, 64), size), :] = own[0]
        mine = pl.multiple_of((1 - y_hi) * size + core * half, 64)
        theirs = pl.multiple_of((1 - y_hi) * size + (1 - core) * half, 64)
        out[pl.ds(mine, half), :] = got[at : at + half, :]
        out[pl.ds(theirs, half), :] = other[at : at + half, :]


def layer_block(shape, layer):
    return pl.BlockSpec((1,) + shape, lambda i: (layer, 0, 0))


whole = pl.BlockSpec(memory_space=pltpu.VMEM)
params_one = pltpu.CompilerParams(vmem_limit_bytes=LIMIT)


def pack_first(info, weight, small):
    return pl.pallas_call(
        pack_first_kernel,
        grid=(1,),
        out_shape=jax.ShapeDtypeStruct((8, 80, 768), bf16),
        in_specs=[smem, layer_block((128, 3072), 0), whole],
        out_specs=whole,
        compiler_params=params_one,
        name="pack_first",
    )(info, weight, small)


def pack_rest(info, weight, up, down, project):
    return pl.pallas_call(
        pack_rest_kernel,
        grid=(1,),
        out_shape=(
            jax.ShapeDtypeStruct((8, 64, 1024), bf16),
            jax.ShapeDtypeStruct((8, 64, 1792), bf16),
            jax.ShapeDtypeStruct((320, D), bf16),
            jax.ShapeDtypeStruct((320, D), bf16),
        ),
        in_specs=[smem, layer_block((128, 3072), 1), whole, whole, whole],
        out_specs=(whole,) * 4,
        compiler_params=params_one,
        name="pack_rest",
    )(info, weight, up, down, project)


def join_columns(info, got, other, widths):
    return pl.pallas_call(
        join_columns_kernel,
        out_shape=tuple(jax.ShapeDtypeStruct((D, width), bf16) for width in widths),
        in_specs=[smem, whole, whole],
        out_specs=(whole,) * len(widths),
        compiler_params=params_one,
        name="join_columns",
    )(info, got, other)


def join_rows(info, down, project, layer, got, other):
    return pl.pallas_call(
        join_rows_kernel,
        grid=(1,),
        out_shape=(
            jax.ShapeDtypeStruct((D, D), bf16),
            jax.ShapeDtypeStruct((256, D), bf16),
        ),
        in_specs=[smem, layer_block((512, D), layer), layer_block((128, D), layer), whole, whole],
        out_specs=(whole,) * 2,
        compiler_params=params_one,
        name="join_rows",
    )(info, down, project, got, other)


def to_ctx(value):
    return lax.all_to_all(value, CTX, split_axis=0, concat_axis=0, tiled=True)


def in_order(mine, other, core):
    return jnp.where(
        core == 0,
        jnp.concatenate([mine, other], axis=1),
        jnp.concatenate([other, mine], axis=1),
    )


def columns_at(value, at, width):
    return lax.dynamic_slice_in_dim(value, at * width, width, 1)


def forward(hidden, normed_all, params, info, slopes, core):
    (_, _, w_in, in_bias, project, project_bias) = params[:6]
    (gain_two, offset_two, up, up_bias, down, down_bias) = params[6:]
    projected = (dot(normed_all, w_in) + in_bias).astype(bf16)
    received = swap(columns_at(projected, 1 - core, 384), "core")
    mine = columns_at(projected, core, 384)
    ctx_mine, ctx_other, logsum, rows = attend(info, slopes, mine, received)
    context = in_order(ctx_mine, swap(ctx_other, "core"), core)
    middle = hidden + dot_scatter(context, project, dot) + project_bias
    normed_two = gather_z(norm(middle, gain_two, offset_two).astype(bf16))
    before = dot(normed_two, up) + up_bias
    activated = gelu(before).astype(bf16)
    result = middle + dot_scatter(activated, down, dot) + down_bias
    kept = (hidden, normed_all, logsum, rows, context, middle, normed_two, before, activated)
    return result, kept


def backward(gradient, params, kept, info, slopes, core):
    (gain_one, _, w_in, _, project, _) = params[:6]
    (gain_two, _, up, _, down, _) = params[6:]
    hidden, normed_all, logsum, rows, context, middle, normed_two, before, activated = kept
    grad_low = gradient.astype(bf16)
    grad_down = gather_z(grad_low)
    sum_down = jnp.sum(grad_low.astype(f32), axis=0)
    d_act = dot_t(grad_down, down)
    d_before = jax.vjp(gelu, before)[1](d_act)[0].astype(bf16)
    sum_up = jnp.sum(d_before.astype(f32), axis=0)
    d_normed = dot_scatter(d_before, up, dot_t)
    grad_down, d_before = after((grad_down, d_before), d_before)
    g_down = outer(activated, grad_down).astype(bf16)
    g_up = outer(normed_two, d_before).astype(bf16)
    d_normed, g_down, g_up = after((d_normed, g_down, g_up), g_down, g_up)
    d_values, sum_gain_two, sum_offset_two = norm_back(middle, gain_two, d_normed)
    d_middle = gradient + d_values
    grad_out = d_middle.astype(bf16)
    grad_out_all = gather_z(grad_out)
    sum_project = jnp.sum(grad_out.astype(f32), axis=0)
    d_context = dot_t(grad_out_all, project).astype(bf16)
    received = swap(columns_at(d_context, 1 - core, 128), "core")
    g_project = outer(context, grad_out_all).astype(bf16)
    d_mine, d_other, sums = attend_back(
        info, slopes, rows, columns_at(d_context, core, 128), received, logsum
    )
    d_joined = in_order(d_mine, swap(d_other, "core"), core)
    d_normed_one = dot_scatter(d_joined, w_in, dot_t)
    g_input = outer(normed_all, d_joined).astype(bf16)
    d_normed_one, g_input = after((d_normed_one, g_input), g_input)
    d_hidden, sum_gain_one, sum_offset_one = norm_back(hidden, gain_one, d_normed_one)
    big = (g_down, g_up, g_project, g_input)
    small = (
        sum_gain_one,
        sum_offset_one,
        sum_project,
        sum_gain_two,
        sum_offset_two,
        sum_down,
        sums,
        sum_up,
    )
    return d_middle + d_hidden, big, small


def take(value, at, axis=0):
    return lax.dynamic_index_in_dim(value, at, axis, keepdims=False)


def groups_first(value, shape):
    split = value.reshape(shape)
    order = (1, 0) + tuple(range(2, len(shape)))
    return split.transpose(order)


def pack_outer(g_down, g_up):
    pieces = (
        groups_first(g_down, (2, 16, 32, D)).reshape(16, 64, D),
        groups_first(g_up, (8, 16, 8, D)).reshape(16, 64, D),
    )
    return jnp.concatenate(pieces, axis=-1)


def pack_inner(g_project, g_input):
    pieces = (
        groups_first(g_project, (2, 16, 8, 4, 256)).reshape(16, 64, 256),
        groups_first(g_input, (8, 16, 8, 768)).reshape(16, 64, 768),
    )
    return jnp.concatenate(pieces, axis=-1)


def sum_pairs(value, at, axis):
    return take(value, at).astype(f32) + swap(take(value, 1 - at), axis).astype(f32)


def own_rows(summed, split, y_hi):
    both = sum_pairs(summed.reshape(2, 32, -1), y_hi, "y_hi").astype(bf16)
    columns = both[:, split:].reshape(4, 8, -1)
    columns = lax.all_to_all(columns, "z", split_axis=0, concat_axis=0, tiled=True)
    return jnp.concatenate([both[:, :split], columns.reshape(32, -1)], axis=1)


def sum_steps(pack, place):
    x, y_lo, core = place
    total = sum_pairs(pack.reshape(2, 4, 2, 64, -1), core, "core")
    low = total.astype(bf16)
    total = take(total, x)
    for k in (1, 2, 3):
        total = total + shift_x(take(low, (x + k) % 4), k).astype(f32)
    return sum_pairs(total.astype(bf16), y_lo, "y_lo")


def spread_steps(rows, place):
    x, y_lo, core = place
    other = swap(rows, "y_lo")
    both = jnp.where(y_lo == 0, jnp.stack([rows, other]), jnp.stack([other, rows]))
    blocks = jnp.stack([both] + [shift_x(both, k) for k in (3, 2, 1)])
    blocks = lax.dynamic_slice_in_dim(jnp.concatenate([blocks, blocks]), (4 - x) % 4, 4, 0)
    other = swap(blocks, "core")
    both = jnp.where(core == 0, jnp.stack([blocks, other]), jnp.stack([other, blocks]))
    return both.reshape(16, *rows.shape)


def order_columns(rows, parts):
    split = rows.reshape(16, 4, 8, 2, parts, -1)
    return split.transpose(0, 2, 4, 3, 1, 5).reshape(128, -1)


def unpack_outer(full):
    full = full.astype(f32)
    return full[:, :, :D].reshape(512, D), order_columns(full[:, :, D:], 1)


def unpack_inner(full):
    full = full.astype(f32)
    return full[:, :, :256].reshape(128, D), order_columns(full[:, :, 256:], 3)


def pack_small(small, place, z):
    (gain_one, offset_one, project, gain_two, offset_two, down, sums, up) = small
    vectors = [
        v.reshape(8, 128) for v in (gain_one, offset_one, project, gain_two, offset_two, down)
    ]
    sums = sums.reshape(-1)
    inputs = lax.dynamic_update_slice_in_dim(jnp.zeros((2 * D,), f32), sums[:128], place * 128, 0)
    inputs = lax.dynamic_update_slice_in_dim(inputs, sums[256:], D + place * 128, 0)
    units = lax.dynamic_update_slice_in_dim(
        jnp.zeros((2, 4, 512), f32), up.reshape(2, 1, 512), z, 1
    )
    return jnp.concatenate(
        vectors + [inputs.reshape(8, 256), units.reshape(8, 512)], axis=1
    )


def on_device(
    inputs,
    cotangent,
    segments,
    norm_one_gain,
    norm_one_bias,
    input_weight,
    input_bias,
    project_weight,
    project_bias,
    norm_two_gain,
    norm_two_bias,
    up_weight,
    up_bias,
    down_weight,
    down_bias,
):
    y_hi, z = lax.axis_index("y_hi"), lax.axis_index("z")
    x, y_lo, core = lax.axis_index("x"), lax.axis_index("y_lo"), lax.axis_index("core")
    place = core * 4 + z
    rows_in = regroup(inputs[0], core, y_hi)
    cut = jnp.sum((segments[0] < 2).astype(jnp.int32))
    cut = regroup(jnp.broadcast_to(cut, (1, 128)), core, y_hi)[0, 0]
    info = jnp.stack([core, z, cut, y_hi]).astype(jnp.int32)
    corner = jnp.stack([core, z, y_hi, y_hi]).astype(jnp.int32)
    heads = (place * 2 + jnp.arange(2, dtype=jnp.int32)).astype(f32)
    slopes = jnp.exp2(-8.0 * (heads + 1.0) / HEADS)

    raw_all = gather_z(rows_in)
    small = jnp.concatenate(
        [
            norm_one_gain,
            norm_one_bias,
            project_bias,
            norm_two_gain,
            norm_two_bias,
            down_bias,
            input_bias,
            up_bias,
        ],
        axis=1,
    )
    small = jnp.concatenate([small.reshape(4, 768), jnp.zeros((12, 768), bf16)], axis=0)
    first = to_ctx(pack_first(corner, input_weight, small))
    small = first[:, 64:68].reshape(8, LAYERS, -1).transpose(1, 0, 2).astype(f32)
    (w_first,) = join_columns(corner, first, swap(first[:, :64], "core"), (768,))

    packed = pack_rest(corner, input_weight, up_weight, down_weight, project_weight)
    up_first = to_ctx(packed[0])
    second = to_ctx(packed[1])
    (up_first,) = join_columns(corner, up_first, swap(up_first, "core"), (D,))
    up_second, w_second = join_columns(corner, second, swap(second, "core"), (D, 768))
    w_all = (w_first, w_second)
    up_all = (up_first, up_second)

    layers = []
    for layer in range(LAYERS):
        got = swap(packed[2 + layer], "y_hi")
        down, project = join_rows(
            corner, down_weight, project_weight, layer, got, swap(got, "core")
        )
        vectors = [small[layer, :, i * 128 : (i + 1) * 128].reshape(D) for i in range(6)]
        in_bias = small[layer, :, 768:1024].reshape(2, 2, 4, 128)
        in_bias = lax.dynamic_index_in_dim(in_bias, z, 2, keepdims=False)
        in_bias = jnp.stack([in_bias[0], jnp.zeros((2, 128), f32), in_bias[1]], axis=1)
        unit_bias = small[layer, :, 1024:1536].reshape(2, 4, 512)
        unit_bias = lax.dynamic_index_in_dim(unit_bias, z, 1, keepdims=False).reshape(D)
        layers.append(
            (
                vectors[0],
                vectors[1],
                w_all[layer],
                in_bias.reshape(768),
                project,
                vectors[2],
                vectors[3],
                vectors[4],
                up_all[layer],
                unit_bias,
                down,
                vectors[5],
            )
        )

    hidden = rows_in.astype(f32)
    kept = []
    for layer in range(LAYERS):
        params = layers[layer]
        if layer == 0:
            normed_all = norm(raw_all.astype(f32), params[0], params[1]).astype(bf16)
        else:
            normed_all = gather_z(norm(hidden, params[0], params[1]).astype(bf16))
        hidden, state = forward(hidden, normed_all, params, info, slopes, core)
        kept.append(state)
    gradient = regroup(cotangent[0], core, y_hi).astype(f32)
    slot = (x, y_lo, core)
    finals = [None] * LAYERS
    smalls = [None] * LAYERS
    for layer in (1, 0):
        gradient, big, smalls[layer] = backward(
            gradient, layers[layer], kept[layer], info, slopes, core
        )
        outer_pack = pack_outer(big[0], big[1])
        inner_pack = pack_inner(big[2], big[3])
        if layer == 1:
            outer_sum = lax.psum_scatter(outer_pack, GRP, scatter_dimension=0, tiled=True)
            inner_sum = lax.psum_scatter(inner_pack, GRP, scatter_dimension=0, tiled=True)
            outer_sum = own_rows(outer_sum.reshape(64, -1), D, y_hi)
            inner_sum = own_rows(inner_sum.reshape(64, -1), 256, y_hi)
            both = lax.all_gather(jnp.concatenate([outer_sum, inner_sum], axis=1), GRP)
            finals[1] = unpack_outer(both[:, :, : 2 * D]) + unpack_inner(both[:, :, 2 * D :])
        else:
            outer_sum = own_rows(sum_steps(outer_pack, slot).astype(bf16), D, y_hi)
            inner_sum = own_rows(sum_steps(inner_pack, slot).astype(bf16), 256, y_hi)
            finals[0] = unpack_outer(spread_steps(outer_sum, slot)) + unpack_inner(
                spread_steps(inner_sum, slot)
            )
    packed = jnp.concatenate([pack_small(s, place, z) for s in smalls], axis=1)
    vector = jnp.sum(to_ctx(packed), axis=0)
    vector = jnp.sum(lax.all_gather(vector.reshape(8, -1), GRP, axis=0, tiled=False), axis=0)
    vector = vector.reshape(LAYERS, -1)
    parts = [vector[:, i * 128 : (i + 1) * 128] for i in range(6)]
    both = [jnp.stack([finals[0][i], finals[1][i]]) for i in range(4)]
    return (
        regroup(hidden, core, y_hi)[None],
        regroup(gradient, core, y_hi)[None],
        parts[0],
        parts[1],
        both[3],
        vector[:, 768:1024],
        both[2],
        parts[2],
        parts[3],
        parts[4],
        both[1],
        vector[:, 1024:1536],
        both[0],
        parts[5],
    )


def solution(mesh):
    split = Mesh(mesh.devices.reshape(4, 2, 2, 2, 4), GRP + CTX)
    rows = P(GRP, CTX, None)
    vector = P(None, CTX)
    matrix = P(None, CTX, None)
    weights = (
        vector,
        vector,
        matrix,
        vector,
        matrix,
        vector,
        vector,
        vector,
        matrix,
        vector,
        matrix,
        vector,
    )
    return jax.shard_map(
        on_device,
        mesh=split,
        in_specs=(rows, rows, P(GRP, None)) + weights,
        out_specs=(rows, rows) + weights,
        check_vma=False,
    )
```

```python
import functools

import jax
import jax.numpy as jnp
from jax import lax
from jax.experimental import pallas as pl
from jax.experimental.pallas import tpu as pltpu
from jax.sharding import Mesh
from jax.sharding import PartitionSpec as P

D = 1024
HEADS = 16
HEAD_DIM = 64
FF = 4096
PROMPT = 1024
TOKENS = 1536
PIECE = 192
LAYERS = 2
TILE = 256
HALF = 4 * PIECE
SCALE = HEAD_DIM ** (-0.5)
masked_value = -1e30

GRP = ("x", "y_lo", "core")
CTX = ("y_hi", "z")
bf16 = jnp.bfloat16
f32 = jnp.float32


def shift_z(value, step):
    return lax.ppermute(value, "z", [(i, (i + step) % 4) for i in range(4)])


def shift_x(value, step):
    return lax.ppermute(value, "x", [(i, (i + step) % 4) for i in range(4)])


def swap(value, axis):
    return lax.ppermute(value, axis, [(0, 1), (1, 0)])


def regroup(value, core, y_hi):
    got = lax.ppermute(value, ("core", "y_hi"), [(1, 2), (2, 1)])
    return jnp.where(core == y_hi, value, got)


def after(value, *others):
    return lax.optimization_barrier((value, others))[0]


def beside(send, transfer, given, work):
    send, given = lax.optimization_barrier((send, given))
    return lax.optimization_barrier((transfer(send), work(given)))


def gather_z(rows):
    return jnp.concatenate([rows] + [shift_z(rows, k) for k in (1, 2, 3)], axis=0)


def dot(left, right):
    return jnp.dot(left, right, preferred_element_type=f32)


def dot_t(left, right):
    return lax.dot_general(left, right, (((1,), (1,)), ((), ())), preferred_element_type=f32)


def outer(left, right):
    return lax.dot_general(left, right, (((0,), (0,)), ((), ())), preferred_element_type=f32)


def scatter_parts(others):
    return tuple(
        shift_z(others[(k - 1) * PIECE : k * PIECE], -k) for k in (1, 2, 3)
    )


def sum_parts(own, parts):
    total = own
    for part in parts:
        total = total + part.astype(f32)
    return total


def dot_others(left, weight, product):
    return product(left[PIECE:], weight).astype(bf16)


def dot_own(left, weight, product):
    return product(left[:PIECE], weight)


def tile_mask(block, low, high, cut):
    keys = lax.broadcasted_iota(jnp.int32, (high - low, TILE), 0) + low
    queries = lax.broadcasted_iota(jnp.int32, (high - low, TILE), 1) + block * TILE
    visible = keys <= queries
    if block * TILE >= PROMPT:
        visible = visible & ((keys >= cut) | (queries < cut))
    return visible


def fill_bias(bias, slopes, cut):
    keys = lax.broadcasted_iota(jnp.int32, (TOKENS, 128), 0)
    places = jnp.where(keys >= cut, keys - cut + PROMPT, keys).astype(f32)
    for h in range(2):
        bias[h] = places * slopes[h]


def scores_t(keys, queries, bias, block, high, cut):
    low = min(block * TILE, PROMPT)
    scores = dot_t(keys, queries)
    scores = scores + jnp.concatenate([bias[0:high], bias[0:high]], axis=1)
    tail = jnp.where(tile_mask(block, low, high, cut), scores[low:high], masked_value)
    if low == 0:
        return tail
    return jnp.concatenate([scores[:low], tail], axis=0)


def piece_places(info):
    core, z = info[0], info[1]
    out = []
    for side in range(2):
        half = core if side == 0 else 1 - core
        for k in range(4):
            out.append(pl.multiple_of((half * 4 + ((z - k) & 3)) * PIECE, 64))
    return out


def attend_kernel(info, slopes, mine, other, ctx_mine, ctx_other, logsum, rows, ctx, vt, bias):
    spots = piece_places(info)
    cut = info[2]
    for k in range(4):
        span = slice(k * PIECE, (k + 1) * PIECE)
        rows[pl.ds(spots[k], PIECE), :] = mine[span, :]
        rows[pl.ds(spots[4 + k], PIECE), :] = other[span, :]
    fill_bias(bias, slopes, cut)
    vt[...] = rows[:, 256:384].astype(f32).T.astype(bf16)
    for block in range(TOKENS // TILE):
        high = (block + 1) * TILE
        span = slice(block * TILE, high)
        parts = []
        for h in range(2):
            lanes = slice(h * HEAD_DIM, (h + 1) * HEAD_DIM)
            key_lanes = slice(128 + h * HEAD_DIM, 128 + (h + 1) * HEAD_DIM)
            queries = rows[span, lanes] * jnp.asarray(SCALE, bf16)
            scores = scores_t(rows[0:high, key_lanes], queries, bias[h], block, high, cut)
            top = jnp.max(scores, axis=0, keepdims=True)
            weights = jnp.exp(scores - top)
            total = jnp.sum(weights, axis=0, keepdims=True)
            found = dot(vt[lanes, 0:high], weights.astype(bf16))
            parts.append(found * (1.0 / total))
            logsum[h : h + 1, span] = top + jnp.log(total)
        ctx[span, :] = jnp.concatenate(parts, axis=0).T.astype(bf16)
    for k in range(4):
        span = slice(k * PIECE, (k + 1) * PIECE)
        ctx_mine[span, :] = ctx[pl.ds(spots[k], PIECE), :]
        ctx_other[span, :] = ctx[pl.ds(spots[4 + k], PIECE), :]


def attend_back_kernel(
    info, slopes, rows, mine, other, logsum, out_mine, out_other, sums, grad, kt, bias, dq, dk, dv, out
):
    spots = piece_places(info)
    cut = info[2]
    for k in range(4):
        span = slice(k * PIECE, (k + 1) * PIECE)
        grad[pl.ds(spots[k], PIECE), :] = mine[span, :]
        grad[pl.ds(spots[4 + k], PIECE), :] = other[span, :]
    fill_bias(bias, slopes, cut)
    kt[...] = rows[:, 128:256].astype(f32).T.astype(bf16)
    dk[...] = jnp.zeros_like(dk)
    dv[...] = jnp.zeros_like(dv)
    for block in range(TOKENS // TILE):
        high = (block + 1) * TILE
        span = slice(block * TILE, high)
        parts = []
        for h in range(2):
            lanes = slice(h * HEAD_DIM, (h + 1) * HEAD_DIM)
            key_lanes = slice(128 + h * HEAD_DIM, 128 + (h + 1) * HEAD_DIM)
            value_lanes = slice(256 + h * HEAD_DIM, 256 + (h + 1) * HEAD_DIM)
            queries = rows[span, lanes] * jnp.asarray(SCALE, bf16)
            grads = grad[span, lanes]
            scores = scores_t(rows[0:high, key_lanes], queries, bias[h], block, high, cut)
            weights = jnp.exp(scores - logsum[h : h + 1, span])
            d_weights = dot_t(rows[0:high, value_lanes], grads)
            correction = jnp.sum(weights * d_weights, axis=0, keepdims=True)
            d_scores = (weights * (d_weights - correction)).astype(bf16)
            dv[h, 0:high, :] += dot(weights.astype(bf16), grads)
            dk[h, 0:high, :] += dot(d_scores, queries)
            parts.append(dot(kt[lanes, 0:high], d_scores))
        dq[span, :] = (jnp.concatenate(parts, axis=0) * SCALE).T
    out[:, 0:128] = dq[...].astype(bf16)
    out[:, 128:256] = jnp.concatenate([dk[0], dk[1]], axis=1).astype(bf16)
    out[:, 256:384] = jnp.concatenate([dv[0], dv[1]], axis=1).astype(bf16)
    sums[...] = jnp.sum(out[...].astype(f32), axis=0, keepdims=True)
    for k in range(4):
        span = slice(k * PIECE, (k + 1) * PIECE)
        out_mine[span, :] = out[pl.ds(spots[k], PIECE), :]
        out_other[span, :] = out[pl.ds(spots[4 + k], PIECE), :]


smem = pl.BlockSpec(memory_space=pltpu.SMEM)
vmem = pl.BlockSpec(memory_space=pltpu.VMEM)
LIMIT = 40 * 2**20


def attend(info, slopes, mine, other):
    return pl.pallas_call(
        attend_kernel,
        out_shape=(
            jax.ShapeDtypeStruct((HALF, 128), bf16),
            jax.ShapeDtypeStruct((HALF, 128), bf16),
            jax.ShapeDtypeStruct((2, TOKENS), f32),
            jax.ShapeDtypeStruct((TOKENS, 384), bf16),
        ),
        in_specs=[smem, smem, vmem, vmem],
        out_specs=(vmem, vmem, vmem, vmem),
        scratch_shapes=[
            pltpu.VMEM((TOKENS, 128), bf16),
            pltpu.VMEM((128, TOKENS), bf16),
            pltpu.VMEM((2, TOKENS, 128), f32),
        ],
        compiler_params=pltpu.CompilerParams(vmem_limit_bytes=LIMIT),
        cost_estimate=pl.CostEstimate(
            flops=4 * 2 * 1400000 * 64, bytes_accessed=28000000, transcendentals=2800000
        ),
        name="attend",
    )(info, slopes, mine, other)


def attend_back(info, slopes, rows, mine, other, logsum):
    return pl.pallas_call(
        attend_back_kernel,
        out_shape=(
            jax.ShapeDtypeStruct((HALF, 384), bf16),
            jax.ShapeDtypeStruct((HALF, 384), bf16),
            jax.ShapeDtypeStruct((1, 384), f32),
        ),
        in_specs=[smem, smem, vmem, vmem, vmem, vmem],
        out_specs=(vmem, vmem, vmem),
        scratch_shapes=[
            pltpu.VMEM((TOKENS, 128), bf16),
            pltpu.VMEM((128, TOKENS), bf16),
            pltpu.VMEM((2, TOKENS, 128), f32),
            pltpu.VMEM((TOKENS, 128), f32),
            pltpu.VMEM((2, TOKENS, HEAD_DIM), f32),
            pltpu.VMEM((2, TOKENS, HEAD_DIM), f32),
            pltpu.VMEM((TOKENS, 384), bf16),
        ],
        compiler_params=pltpu.CompilerParams(vmem_limit_bytes=LIMIT),
        cost_estimate=pl.CostEstimate(
            flops=10 * 2 * 1400000 * 64, bytes_accessed=36000000, transcendentals=2800000
        ),
        name="attend_back",
    )(info, slopes, rows, mine, other, logsum)


def norm_parts(values):
    average = jnp.mean(values, axis=-1, keepdims=True)
    centered = values - average
    variance = jnp.mean(centered * centered, axis=-1, keepdims=True)
    scale = lax.rsqrt(variance + 1e-05)
    return centered * scale, scale


def norm(values, gain, offset):
    return norm_parts(values)[0] * gain + offset


def norm_back(values, gain, grads):
    unit, scale = norm_parts(values)
    weighted = grads * gain
    mean_one = jnp.mean(weighted, axis=-1, keepdims=True)
    mean_two = jnp.mean(weighted * unit, axis=-1, keepdims=True)
    d_values = scale * (weighted - mean_one - unit * mean_two)
    return d_values, jnp.sum(grads * unit, axis=0), jnp.sum(grads, axis=0)


def gelu(values):
    return jax.nn.gelu(values, approximate=True)


def pack_first_kernel(info, weight, small, out):
    core = info[0]
    rows = pl.ds(pl.multiple_of(core * 64, 64), 64)
    for place in range(8):
        for side in range(2):
            for part in range(3):
                at = part * D + side * 512 + (place % 4) * 128
                to = (side * 3 + part) * 128
                out[place, 0:64, to : to + 128] = weight[0, rows, at : at + 128]
        out[place, 64:80, :] = small[...]


def pack_rest_kernel(info, weight, up, down, project, first, second, rows_first, rows_second):
    core = info[0]
    rows = pl.ds(pl.multiple_of(core * 64, 64), 64)
    for place in range(8):
        for side in range(2):
            at = side * 2048 + (place % 4) * 512
            to = side * 512
            first[place, :, to : to + 512] = up[0, rows, at : at + 512]
            second[place, :, to : to + 512] = up[1, rows, at : at + 512]
            for part in range(3):
                at = part * D + side * 512 + (place % 4) * 128
                to = D + (side * 3 + part) * 128
                second[place, :, to : to + 128] = weight[0, rows, at : at + 128]
    long = pl.ds(pl.multiple_of(core * 256, 64), 256)
    for layer, out in ((0, rows_first), (1, rows_second)):
        out[0:256, :] = down[layer, long, :]
        out[256:320, :] = project[layer, rows, :]


def join_columns_kernel(info, got, other, *outs):
    core = info[0]
    at = 0
    for out in outs:
        width = out.shape[1]
        for place in range(8):
            mine = pl.multiple_of(place * 128 + core * 64, 64)
            theirs = pl.multiple_of(place * 128 + (1 - core) * 64, 64)
            out[pl.ds(mine, 64), :] = got[place, 0:64, at : at + width]
            out[pl.ds(theirs, 64), :] = other[place, 0:64, at : at + width]
        at += width


def join_rows_kernel(info, down, project, got, other, down_out, project_out):
    core, y_hi = info[0], info[3]
    for out, own, size, at in ((down_out, down, 512, 0), (project_out, project, 128, 256)):
        half = size // 2
        out[pl.ds(pl.multiple_of(y_hi * size, 64), size), :] = own[0]
        mine = pl.multiple_of((1 - y_hi) * size + core * half, 64)
        theirs = pl.multiple_of((1 - y_hi) * size + (1 - core) * half, 64)
        out[pl.ds(mine, half), :] = got[at : at + half, :]
        out[pl.ds(theirs, half), :] = other[at : at + half, :]


def layer_block(shape, layer):
    return pl.BlockSpec((1,) + shape, lambda i: (layer, 0, 0))


whole = pl.BlockSpec(memory_space=pltpu.VMEM)
params_one = pltpu.CompilerParams(vmem_limit_bytes=LIMIT)


def pack_first(info, weight, small):
    return pl.pallas_call(
        pack_first_kernel,
        grid=(1,),
        out_shape=jax.ShapeDtypeStruct((8, 80, 768), bf16),
        in_specs=[smem, layer_block((128, 3072), 0), whole],
        out_specs=whole,
        compiler_params=params_one,
        name="pack_first",
    )(info, weight, small)


def pack_rest(info, weight, up, down, project):
    return pl.pallas_call(
        pack_rest_kernel,
        grid=(1,),
        out_shape=(
            jax.ShapeDtypeStruct((8, 64, 1024), bf16),
            jax.ShapeDtypeStruct((8, 64, 1792), bf16),
            jax.ShapeDtypeStruct((320, D), bf16),
            jax.ShapeDtypeStruct((320, D), bf16),
        ),
        in_specs=[smem, layer_block((128, 3072), 1), whole, whole, whole],
        out_specs=(whole,) * 4,
        compiler_params=params_one,
        name="pack_rest",
    )(info, weight, up, down, project)


def join_columns(info, got, other, widths):
    return pl.pallas_call(
        join_columns_kernel,
        out_shape=tuple(jax.ShapeDtypeStruct((D, width), bf16) for width in widths),
        in_specs=[smem, whole, whole],
        out_specs=(whole,) * len(widths),
        compiler_params=params_one,
        name="join_columns",
    )(info, got, other)


def join_rows(info, down, project, layer, got, other):
    return pl.pallas_call(
        join_rows_kernel,
        grid=(1,),
        out_shape=(
            jax.ShapeDtypeStruct((D, D), bf16),
            jax.ShapeDtypeStruct((256, D), bf16),
        ),
        in_specs=[smem, layer_block((512, D), layer), layer_block((128, D), layer), whole, whole],
        out_specs=(whole,) * 2,
        compiler_params=params_one,
        name="join_rows",
    )(info, down, project, got, other)


def to_ctx(value):
    return lax.all_to_all(value, CTX, split_axis=0, concat_axis=0, tiled=True)


def in_order(mine, other, core):
    return jnp.where(
        core == 0,
        jnp.concatenate([mine, other], axis=1),
        jnp.concatenate([other, mine], axis=1),
    )


def columns_at(value, at, width):
    return lax.dynamic_slice_in_dim(value, at * width, width, 1)


def forward(hidden, normed_all, params, info, slopes, core, side=None):
    (_, _, w_in, in_bias, project, project_bias) = params[:6]
    (gain_two, offset_two, up, up_bias, down, down_bias) = params[6:]
    projected = (dot(normed_all, w_in) + in_bias).astype(bf16)
    received = swap(columns_at(projected, 1 - core, 384), "core")
    mine = columns_at(projected, core, 384)
    side_done = None
    if side is None:
        ctx_mine, ctx_other, logsum, rows = attend(info, slopes, mine, received)
    else:
        side_done, (ctx_mine, ctx_other, logsum, rows) = beside(
            side[0], side[1], (mine, received), lambda v: attend(info, slopes, *v)
        )
    context = in_order(ctx_mine, swap(ctx_other, "core"), core)
    parts, own = beside(
        dot_others(context, project, dot),
        scatter_parts,
        context,
        lambda v: dot_own(v, project, dot),
    )
    middle = hidden + sum_parts(own, parts) + project_bias
    normed_two = gather_z(norm(middle, gain_two, offset_two).astype(bf16))
    before = dot(normed_two, up) + up_bias
    activated = gelu(before).astype(bf16)
    last = (middle, activated)
    kept = (hidden, normed_all, logsum, rows, context, middle, normed_two, before, activated)
    return last, kept, side_done


def last_send(last, params):
    return dot_others(last[1], params[10], dot)


def last_sum(last, params, parts):
    return last[0] + sum_parts(dot_own(last[1], params[10], dot), parts) + params[11]


def backward(gradient, grad_down, params, kept, info, slopes, core, fill):
    (gain_one, _, w_in, _, project, _) = params[:6]
    (gain_two, _, up, _, down, _) = params[6:]
    hidden, normed_all, logsum, rows, context, middle, normed_two, before, activated = kept
    sum_down = jnp.sum(gradient.astype(bf16).astype(f32), axis=0)
    d_act = dot_t(grad_down, down)
    d_before = jax.vjp(gelu, before)[1](d_act)[0].astype(bf16)
    sum_up = jnp.sum(d_before.astype(f32), axis=0)

    def outer_work(given):
        activated, grad_down, normed_two, d_before = given
        own = dot_own(d_before, up, dot_t)
        g_down = outer(activated, grad_down).astype(bf16)
        g_up = outer(normed_two, d_before).astype(bf16)
        return own, g_down, g_up

    parts, (own, g_down, g_up) = beside(
        dot_others(d_before, up, dot_t),
        scatter_parts,
        (activated, grad_down, normed_two, d_before),
        outer_work,
    )
    d_normed = sum_parts(own, parts)
    d_values, sum_gain_two, sum_offset_two = norm_back(middle, gain_two, d_normed)
    d_middle = gradient + d_values
    grad_out = d_middle.astype(bf16)
    sum_project = jnp.sum(grad_out.astype(f32), axis=0)
    grad_out_all, outer_state = beside(grad_out, gather_z, (g_down, g_up), fill["outer"])
    d_context = dot_t(grad_out_all, project).astype(bf16)
    received = swap(columns_at(d_context, 1 - core, 128), "core")
    mine = columns_at(d_context, core, 128)
    attend_done, (d_mine, d_other, sums) = beside(
        fill["attend"][0],
        fill["attend"][1],
        (mine, received),
        lambda v: attend_back(info, slopes, rows, *v, logsum),
    )
    d_joined = in_order(d_mine, swap(d_other, "core"), core)

    def inner_work(given):
        context, grad_out_all, normed_all, d_joined = given
        own = dot_own(d_joined, w_in, dot_t)
        g_input = outer(normed_all, d_joined).astype(bf16)
        g_project = outer(context, grad_out_all).astype(bf16)
        return own, fill["inner"](g_project, g_input)

    parts, (own, inner_state) = beside(
        dot_others(d_joined, w_in, dot_t),
        scatter_parts,
        (context, grad_out_all, normed_all, d_joined),
        inner_work,
    )
    d_normed_one = sum_parts(own, parts)
    d_hidden, sum_gain_one, sum_offset_one = norm_back(hidden, gain_one, d_normed_one)
    small = (
        sum_gain_one,
        sum_offset_one,
        sum_project,
        sum_gain_two,
        sum_offset_two,
        sum_down,
        sums,
        sum_up,
    )
    return d_middle + d_hidden, outer_state, attend_done, inner_state, small


def take(value, at, axis=0):
    return lax.dynamic_index_in_dim(value, at, axis, keepdims=False)


def groups_first(value, shape):
    split = value.reshape(shape)
    order = (1, 0) + tuple(range(2, len(shape)))
    return split.transpose(order)


def pack_outer(g_down, g_up):
    pieces = (
        groups_first(g_down, (2, 16, 32, D)).reshape(16, 64, D),
        groups_first(g_up, (8, 16, 8, D)).reshape(16, 64, D),
    )
    return jnp.concatenate(pieces, axis=-1)


def pack_inner(g_project, g_input):
    pieces = (
        groups_first(g_project, (2, 16, 8, 4, 256)).reshape(16, 64, 256),
        groups_first(g_input, (8, 16, 8, 768)).reshape(16, 64, 768),
    )
    return jnp.concatenate(pieces, axis=-1)


def sum_pairs(value, at, axis):
    return take(value, at).astype(f32) + swap(take(value, 1 - at), axis).astype(f32)


def own_rows(summed, split, y_hi):
    both = sum_pairs(summed.reshape(2, 32, -1), y_hi, "y_hi").astype(bf16)
    columns = both[:, split:].reshape(4, 8, -1)
    columns = lax.all_to_all(columns, "z", split_axis=0, concat_axis=0, tiled=True)
    return jnp.concatenate([both[:, :split], columns.reshape(32, -1)], axis=1)


def project_steps(g_project, place, y_hi):
    x, y_lo, core = place
    pack = g_project.reshape(2, 4, 2, 2, 8, D).transpose(3, 1, 2, 0, 4, 5)
    low = sum_pairs(pack, core, "core").astype(bf16)
    total = take(low, x).astype(f32)
    for k in (1, 2, 3):
        total = total + shift_x(take(low, (x + k) % 4), k).astype(f32)
    low = sum_pairs(total.astype(bf16), y_lo, "y_lo").astype(bf16)
    return sum_pairs(low, y_hi, "y_hi").astype(bf16).reshape(32, 256)


def sum_small(packed, z, y_hi):
    split = packed.reshape(2, 4, -1)
    total = take(split, z, 1)
    for k in (1, 2, 3):
        total = total + shift_z(take(split, (z + k) % 4, 1), k)
    total = take(total, y_hi) + swap(take(total, 1 - y_hi), "y_hi")
    total = total + swap(total, "core")
    total = total + swap(total, "y_lo")
    return total + shift_x(total, 1) + shift_x(total, 2) + shift_x(total, 3)


def order_columns(rows, parts):
    split = rows.reshape(16, 4, 8, 2, parts, -1)
    return split.transpose(0, 2, 4, 3, 1, 5).reshape(128, -1)


def unpack(full):
    full = full.astype(f32)
    return (
        full[:, :, :D].reshape(512, D),
        order_columns(full[:, :, D : 2 * D], 1),
        full[:, :, 2 * D : 2 * D + 256].reshape(128, D),
        order_columns(full[:, :, 2 * D + 256 :], 3),
    )


def pack_small(small, place, z):
    (gain_one, offset_one, project, gain_two, offset_two, down, sums, up) = small
    vectors = [
        v.reshape(8, 128) for v in (gain_one, offset_one, project, gain_two, offset_two, down)
    ]
    sums = sums.reshape(-1)
    inputs = lax.dynamic_update_slice_in_dim(jnp.zeros((2 * D,), f32), sums[:128], place * 128, 0)
    inputs = lax.dynamic_update_slice_in_dim(inputs, sums[256:], D + place * 128, 0)
    units = lax.dynamic_update_slice_in_dim(
        jnp.zeros((2, 4, 512), f32), up.reshape(2, 1, 512), z, 1
    )
    return jnp.concatenate(
        vectors + [inputs.reshape(8, 256), units.reshape(8, 512)], axis=1
    )


def on_device(
    inputs,
    cotangent,
    segments,
    norm_one_gain,
    norm_one_bias,
    input_weight,
    input_bias,
    project_weight,
    project_bias,
    norm_two_gain,
    norm_two_bias,
    up_weight,
    up_bias,
    down_weight,
    down_bias,
):
    y_hi, z = lax.axis_index("y_hi"), lax.axis_index("z")
    x, y_lo, core = lax.axis_index("x"), lax.axis_index("y_lo"), lax.axis_index("core")
    place = core * 4 + z
    rows_in = regroup(inputs[0], core, y_hi)
    cut = jnp.sum((segments[0] < 2).astype(jnp.int32))
    cut = regroup(jnp.broadcast_to(cut, (1, 128)), core, y_hi)[0, 0]
    info = jnp.stack([core, z, cut, y_hi]).astype(jnp.int32)
    corner = jnp.stack([core, z, y_hi, y_hi]).astype(jnp.int32)
    heads = (place * 2 + jnp.arange(2, dtype=jnp.int32)).astype(f32)
    slopes = jnp.exp2(-8.0 * (heads + 1.0) / HEADS)

    raw_all = gather_z(rows_in)
    small = jnp.concatenate(
        [
            norm_one_gain,
            norm_one_bias,
            project_bias,
            norm_two_gain,
            norm_two_bias,
            down_bias,
            input_bias,
            up_bias,
        ],
        axis=1,
    )
    small = jnp.concatenate([small.reshape(4, 768), jnp.zeros((12, 768), bf16)], axis=0)
    first = to_ctx(pack_first(corner, input_weight, small))
    small = first[:, 64:68].reshape(8, LAYERS, -1).transpose(1, 0, 2).astype(f32)
    (w_first,) = join_columns(corner, first, swap(first[:, :64], "core"), (768,))

    packed = pack_rest(corner, input_weight, up_weight, down_weight, project_weight)
    up_first = to_ctx(packed[0])
    second = to_ctx(packed[1])
    (up_first,) = join_columns(corner, up_first, swap(up_first, "core"), (D,))
    up_second, w_second = join_columns(corner, second, swap(second, "core"), (D, 768))
    w_all = (w_first, w_second)
    up_all = (up_first, up_second)

    layers = []
    for layer in range(LAYERS):
        got = swap(packed[2 + layer], "y_hi")
        down, project = join_rows(
            corner, down_weight, project_weight, layer, got, swap(got, "core")
        )
        vectors = [small[layer, :, i * 128 : (i + 1) * 128].reshape(D) for i in range(6)]
        in_bias = small[layer, :, 768:1024].reshape(2, 2, 4, 128)
        in_bias = lax.dynamic_index_in_dim(in_bias, z, 2, keepdims=False)
        in_bias = jnp.stack([in_bias[0], jnp.zeros((2, 128), f32), in_bias[1]], axis=1)
        unit_bias = small[layer, :, 1024:1536].reshape(2, 4, 512)
        unit_bias = lax.dynamic_index_in_dim(unit_bias, z, 1, keepdims=False).reshape(D)
        layers.append(
            (
                vectors[0],
                vectors[1],
                w_all[layer],
                in_bias.reshape(768),
                project,
                vectors[2],
                vectors[3],
                vectors[4],
                up_all[layer],
                unit_bias,
                down,
                vectors[5],
            )
        )

    slot = (x, y_lo, core)
    gradient = regroup(cotangent[0], core, y_hi)
    hidden = rows_in.astype(f32)
    normed_all = norm(raw_all.astype(f32), layers[0][0], layers[0][1]).astype(bf16)
    last, kept_0, grad_down = forward(
        hidden, normed_all, layers[0], info, slopes, core, (gradient, gather_z)
    )
    gradient = gradient.astype(f32)
    hidden = last_sum(last, layers[0], scatter_parts(last_send(last, layers[0])))
    normed_all = gather_z(norm(hidden, layers[1][0], layers[1][1]).astype(bf16))
    last, kept_1, _ = forward(hidden, normed_all, layers[1], info, slopes, core)

    def grp_sum(pack):
        return lax.psum_scatter(pack, GRP, scatter_dimension=0, tiled=True).reshape(64, -1)

    fill = {
        "outer": lambda v: pack_outer(*v),
        "attend": (last_send(last, layers[1]), scatter_parts),
        "inner": pack_inner,
    }
    gradient, outer_pack, parts, inner_pack, small_1 = backward(
        gradient, grad_down, layers[1], kept_1, info, slopes, core, fill
    )
    output = last_sum(last, layers[1], parts)
    outer_1 = grp_sum(outer_pack)
    inner_1 = grp_sum(inner_pack)

    grad_down, output = beside(
        gradient.astype(bf16), gather_z, output, lambda v: v + 0.0
    )

    def core_sum(given):
        pack = pack_outer(*given).reshape(8, 2, 64, 2 * D)
        return take(pack, core, 1), take(pack, 1 - core, 1)

    def outer_start(given):
        keep, send = given
        return keep.astype(f32) + swap(send, "core").astype(f32)

    fill = {
        "outer": core_sum,
        "attend": (jnp.zeros((8, 128), f32), lambda v: v),
        "inner": lambda g_project, g_input: (
            project_steps(g_project, slot, y_hi),
            groups_first(g_input, (8, 16, 8, 768)).reshape(128, 8, 768),
        ),
    }
    gradient, outer_0, _, (project_0, input_0), small_0 = backward(
        gradient, grad_down, layers[0], kept_0, info, slopes, core, fill
    )
    outer_0 = outer_start(outer_0).astype(bf16)
    outer_0 = lax.all_to_all(outer_0, ("x", "y_lo"), split_axis=0, concat_axis=0, tiled=True)
    outer_0 = own_rows(jnp.sum(outer_0.astype(f32), axis=0).astype(bf16), D, y_hi)
    outer_0 = lax.all_gather(jnp.concatenate([outer_0, project_0], axis=1), GRP)
    input_0 = lax.all_to_all(input_0, GRP + CTX, split_axis=0, concat_axis=0, tiled=True)
    input_0 = jnp.sum(input_0.reshape(32, 32, 768).astype(f32), axis=0).astype(bf16)
    input_0 = lax.all_gather(input_0, GRP)
    final_0 = unpack(jnp.concatenate([outer_0, input_0], axis=2))
    inner_1 = own_rows(inner_1, 256, y_hi)
    outer_1 = own_rows(outer_1, D, y_hi)
    final_1 = unpack(lax.all_gather(jnp.concatenate([outer_1, inner_1], axis=1), GRP))
    packed = jnp.concatenate([pack_small(s, place, z) for s in (small_0, small_1)], axis=1)
    vector = sum_small(packed, z, y_hi).reshape(LAYERS, -1)
    parts = [vector[:, i * 128 : (i + 1) * 128] for i in range(6)]
    both = [jnp.stack([final_0[i], final_1[i]]) for i in range(4)]
    return (
        regroup(output, core, y_hi)[None],
        regroup(gradient, core, y_hi)[None],
        parts[0],
        parts[1],
        both[3],
        vector[:, 768:1024],
        both[2],
        parts[2],
        parts[3],
        parts[4],
        both[1],
        vector[:, 1024:1536],
        both[0],
        parts[5],
    )


def solution(mesh):
    split = Mesh(mesh.devices.reshape(4, 2, 2, 2, 4), GRP + CTX)
    rows = P(GRP, CTX, None)
    vector = P(None, CTX)
    matrix = P(None, CTX, None)
    weights = (
        vector,
        vector,
        matrix,
        vector,
        matrix,
        vector,
        vector,
        vector,
        matrix,
        vector,
        matrix,
        vector,
    )
    return jax.shard_map(
        on_device,
        mesh=split,
        in_specs=(rows, rows, P(GRP, None)) + weights,
        out_specs=(rows, rows) + weights,
        check_vma=False,
    )
```

```python
import functools

import jax
import jax.numpy as jnp
from jax import lax
from jax.experimental import pallas as pl
from jax.experimental.pallas import tpu as pltpu
from jax.sharding import Mesh
from jax.sharding import PartitionSpec as P

D = 1024
HEADS = 16
HEAD_DIM = 64
FF = 4096
PROMPT = 1024
TOKENS = 1536
PIECE = 192
LAYERS = 2
TILE = 256
HALF = 4 * PIECE
SCALE = HEAD_DIM ** (-0.5)
masked_value = -1e30

GRP = ("x", "y_lo", "core")
CTX = ("y_hi", "z")
bf16 = jnp.bfloat16
f32 = jnp.float32


def shift_z(value, step):
    return lax.ppermute(value, "z", [(i, (i + step) % 4) for i in range(4)])


def shift_x(value, step):
    return lax.ppermute(value, "x", [(i, (i + step) % 4) for i in range(4)])


def swap(value, axis):
    return lax.ppermute(value, axis, [(0, 1), (1, 0)])


def regroup(value, core, y_hi):
    got = lax.ppermute(value, ("core", "y_hi"), [(1, 2), (2, 1)])
    return jnp.where(core == y_hi, value, got)


def after(value, *others):
    return lax.optimization_barrier((value, others))[0]


def beside(send, transfer, given, work):
    send, given = lax.optimization_barrier((send, given))
    return lax.optimization_barrier((transfer(send), work(given)))


def gather_z(rows):
    return jnp.concatenate([rows] + [shift_z(rows, k) for k in (1, 2, 3)], axis=0)


def dot(left, right):
    return jnp.dot(left, right, preferred_element_type=f32)


def dot_t(left, right):
    return lax.dot_general(left, right, (((1,), (1,)), ((), ())), preferred_element_type=f32)


def outer(left, right):
    return lax.dot_general(left, right, (((0,), (0,)), ((), ())), preferred_element_type=f32)


def scatter_parts(others):
    return tuple(
        shift_z(others[(k - 1) * PIECE : k * PIECE], -k) for k in (1, 2, 3)
    )


def sum_parts(own, parts):
    total = own
    for part in parts:
        total = total + part.astype(f32)
    return total


def dot_others(left, weight, product):
    return product(left[PIECE:], weight).astype(bf16)


def dot_own(left, weight, product):
    return product(left[:PIECE], weight)


def tile_mask(block, low, high, cut):
    keys = lax.broadcasted_iota(jnp.int32, (high - low, TILE), 0) + low
    queries = lax.broadcasted_iota(jnp.int32, (high - low, TILE), 1) + block * TILE
    visible = keys <= queries
    if block * TILE >= PROMPT:
        visible = visible & ((keys >= cut) | (queries < cut))
    return visible


def fill_bias(bias, slopes, cut):
    keys = lax.broadcasted_iota(jnp.int32, (TOKENS, 128), 0)
    places = jnp.where(keys >= cut, keys - cut + PROMPT, keys).astype(f32)
    for h in range(2):
        bias[h] = places * slopes[h]


def scores_t(keys, queries, bias, block, high, cut):
    low = min(block * TILE, PROMPT)
    scores = dot_t(keys, queries)
    scores = scores + jnp.concatenate([bias[0:high], bias[0:high]], axis=1)
    tail = jnp.where(tile_mask(block, low, high, cut), scores[low:high], masked_value)
    if low == 0:
        return tail
    return jnp.concatenate([scores[:low], tail], axis=0)


def piece_places(info):
    core, z = info[0], info[1]
    out = []
    for side in range(2):
        half = core if side == 0 else 1 - core
        for k in range(4):
            out.append(pl.multiple_of((half * 4 + ((z - k) & 3)) * PIECE, 64))
    return out


def attend_kernel(info, slopes, mine, other, ctx_mine, ctx_other, logsum, rows, ctx, vt, bias):
    spots = piece_places(info)
    cut = info[2]
    for k in range(4):
        span = slice(k * PIECE, (k + 1) * PIECE)
        rows[pl.ds(spots[k], PIECE), :] = mine[span, :]
        rows[pl.ds(spots[4 + k], PIECE), :] = other[span, :]
    fill_bias(bias, slopes, cut)
    vt[...] = rows[:, 256:384].astype(f32).T.astype(bf16)
    for block in range(TOKENS // TILE):
        high = (block + 1) * TILE
        span = slice(block * TILE, high)
        parts = []
        for h in range(2):
            lanes = slice(h * HEAD_DIM, (h + 1) * HEAD_DIM)
            key_lanes = slice(128 + h * HEAD_DIM, 128 + (h + 1) * HEAD_DIM)
            queries = rows[span, lanes] * jnp.asarray(SCALE, bf16)
            scores = scores_t(rows[0:high, key_lanes], queries, bias[h], block, high, cut)
            top = jnp.max(scores, axis=0, keepdims=True)
            weights = jnp.exp(scores - top)
            total = jnp.sum(weights, axis=0, keepdims=True)
            found = dot(vt[lanes, 0:high], weights.astype(bf16))
            parts.append(found * (1.0 / total))
            logsum[h : h + 1, span] = top + jnp.log(total)
        ctx[span, :] = jnp.concatenate(parts, axis=0).T.astype(bf16)
    for k in range(4):
        span = slice(k * PIECE, (k + 1) * PIECE)
        ctx_mine[span, :] = ctx[pl.ds(spots[k], PIECE), :]
        ctx_other[span, :] = ctx[pl.ds(spots[4 + k], PIECE), :]


def attend_back_kernel(
    info, slopes, rows, mine, other, logsum, out_mine, out_other, sums, grad, kt, bias, dq, dk, dv, out
):
    spots = piece_places(info)
    cut = info[2]
    for k in range(4):
        span = slice(k * PIECE, (k + 1) * PIECE)
        grad[pl.ds(spots[k], PIECE), :] = mine[span, :]
        grad[pl.ds(spots[4 + k], PIECE), :] = other[span, :]
    fill_bias(bias, slopes, cut)
    kt[...] = rows[:, 128:256].astype(f32).T.astype(bf16)
    dk[...] = jnp.zeros_like(dk)
    dv[...] = jnp.zeros_like(dv)
    for block in range(TOKENS // TILE):
        high = (block + 1) * TILE
        span = slice(block * TILE, high)
        parts = []
        for h in range(2):
            lanes = slice(h * HEAD_DIM, (h + 1) * HEAD_DIM)
            key_lanes = slice(128 + h * HEAD_DIM, 128 + (h + 1) * HEAD_DIM)
            value_lanes = slice(256 + h * HEAD_DIM, 256 + (h + 1) * HEAD_DIM)
            queries = rows[span, lanes] * jnp.asarray(SCALE, bf16)
            grads = grad[span, lanes]
            scores = scores_t(rows[0:high, key_lanes], queries, bias[h], block, high, cut)
            weights = jnp.exp(scores - logsum[h : h + 1, span])
            d_weights = dot_t(rows[0:high, value_lanes], grads)
            correction = jnp.sum(weights * d_weights, axis=0, keepdims=True)
            d_scores = (weights * (d_weights - correction)).astype(bf16)
            dv[h, 0:high, :] += dot(weights.astype(bf16), grads)
            dk[h, 0:high, :] += dot(d_scores, queries)
            parts.append(dot(kt[lanes, 0:high], d_scores))
        dq[span, :] = (jnp.concatenate(parts, axis=0) * SCALE).T
    out[:, 0:128] = dq[...].astype(bf16)
    out[:, 128:256] = jnp.concatenate([dk[0], dk[1]], axis=1).astype(bf16)
    out[:, 256:384] = jnp.concatenate([dv[0], dv[1]], axis=1).astype(bf16)
    sums[...] = jnp.sum(out[...].astype(f32), axis=0, keepdims=True)
    for k in range(4):
        span = slice(k * PIECE, (k + 1) * PIECE)
        out_mine[span, :] = out[pl.ds(spots[k], PIECE), :]
        out_other[span, :] = out[pl.ds(spots[4 + k], PIECE), :]


smem = pl.BlockSpec(memory_space=pltpu.SMEM)
vmem = pl.BlockSpec(memory_space=pltpu.VMEM)
LIMIT = 40 * 2**20


def attend(info, slopes, mine, other):
    return pl.pallas_call(
        attend_kernel,
        out_shape=(
            jax.ShapeDtypeStruct((HALF, 128), bf16),
            jax.ShapeDtypeStruct((HALF, 128), bf16),
            jax.ShapeDtypeStruct((2, TOKENS), f32),
            jax.ShapeDtypeStruct((TOKENS, 384), bf16),
        ),
        in_specs=[smem, smem, vmem, vmem],
        out_specs=(vmem, vmem, vmem, vmem),
        scratch_shapes=[
            pltpu.VMEM((TOKENS, 128), bf16),
            pltpu.VMEM((128, TOKENS), bf16),
            pltpu.VMEM((2, TOKENS, 128), f32),
        ],
        compiler_params=pltpu.CompilerParams(vmem_limit_bytes=LIMIT),
        cost_estimate=pl.CostEstimate(
            flops=1000000, bytes_accessed=1000000, transcendentals=0
        ),
        name="attend",
    )(info, slopes, mine, other)


def attend_back(info, slopes, rows, mine, other, logsum):
    return pl.pallas_call(
        attend_back_kernel,
        out_shape=(
            jax.ShapeDtypeStruct((HALF, 384), bf16),
            jax.ShapeDtypeStruct((HALF, 384), bf16),
            jax.ShapeDtypeStruct((1, 384), f32),
        ),
        in_specs=[smem, smem, vmem, vmem, vmem, vmem],
        out_specs=(vmem, vmem, vmem),
        scratch_shapes=[
            pltpu.VMEM((TOKENS, 128), bf16),
            pltpu.VMEM((128, TOKENS), bf16),
            pltpu.VMEM((2, TOKENS, 128), f32),
            pltpu.VMEM((TOKENS, 128), f32),
            pltpu.VMEM((2, TOKENS, HEAD_DIM), f32),
            pltpu.VMEM((2, TOKENS, HEAD_DIM), f32),
            pltpu.VMEM((TOKENS, 384), bf16),
        ],
        compiler_params=pltpu.CompilerParams(vmem_limit_bytes=LIMIT),
        cost_estimate=pl.CostEstimate(
            flops=1000000, bytes_accessed=1000000, transcendentals=0
        ),
        name="attend_back",
    )(info, slopes, rows, mine, other, logsum)


def norm_parts(values):
    average = jnp.mean(values, axis=-1, keepdims=True)
    centered = values - average
    variance = jnp.mean(centered * centered, axis=-1, keepdims=True)
    scale = lax.rsqrt(variance + 1e-05)
    return centered * scale, scale


def norm(values, gain, offset):
    return norm_parts(values)[0] * gain + offset


def norm_back(values, gain, grads):
    unit, scale = norm_parts(values)
    weighted = grads * gain
    mean_one = jnp.mean(weighted, axis=-1, keepdims=True)
    mean_two = jnp.mean(weighted * unit, axis=-1, keepdims=True)
    d_values = scale * (weighted - mean_one - unit * mean_two)
    return d_values, jnp.sum(grads * unit, axis=0), jnp.sum(grads, axis=0)


def gelu(values):
    return jax.nn.gelu(values, approximate=True)


def pack_first_kernel(info, weight, small, out):
    rows = slice(0, 64)
    for place in range(8):
        for side in range(2):
            for part in range(3):
                at = part * D + side * 512 + (place % 4) * 128
                to = (side * 3 + part) * 128
                out[place, 0:64, to : to + 128] = weight[0, rows, at : at + 128]
        out[place, 64:80, :] = small[...]


def pack_rest_kernel(info, weight, up, down, project, first, second, rows_first, rows_second):
    core = info[0]
    rows = pl.ds(pl.multiple_of(core * 64, 64), 64)
    for place in range(8):
        for side in range(2):
            at = side * 2048 + (place % 4) * 512
            to = side * 512
            first[place, :, to : to + 512] = up[0, rows, at : at + 512]
            second[place, :, to : to + 512] = up[1, rows, at : at + 512]
            for part in range(3):
                at = part * D + side * 512 + (place % 4) * 128
                to = D + (side * 3 + part) * 128
                second[place, :, to : to + 128] = weight[0, rows, at : at + 128]
    long = pl.ds(pl.multiple_of(core * 256, 64), 256)
    for layer, out in ((0, rows_first), (1, rows_second)):
        out[0:256, :] = down[layer, long, :]
        out[256:320, :] = project[layer, rows, :]


def join_columns_kernel(info, got, other, *outs):
    core = info[0]
    at = 0
    for out in outs:
        width = out.shape[1]
        for place in range(8):
            mine = pl.multiple_of(place * 128 + core * 64, 64)
            theirs = pl.multiple_of(place * 128 + (1 - core) * 64, 64)
            out[pl.ds(mine, 64), :] = got[place, 0:64, at : at + width]
            out[pl.ds(theirs, 64), :] = other[place, 0:64, at : at + width]
        at += width


def join_rows_kernel(info, down, project, got, other, down_out, project_out):
    core, y_hi = info[0], info[3]
    for out, own, size, at in ((down_out, down, 512, 0), (project_out, project, 128, 256)):
        half = size // 2
        out[pl.ds(pl.multiple_of(y_hi * size, 64), size), :] = own[0]
        mine = pl.multiple_of((1 - y_hi) * size + core * half, 64)
        theirs = pl.multiple_of((1 - y_hi) * size + (1 - core) * half, 64)
        out[pl.ds(mine, half), :] = got[at : at + half, :]
        out[pl.ds(theirs, half), :] = other[at : at + half, :]


def layer_block(shape, layer):
    return pl.BlockSpec((1,) + shape, lambda i: (layer, 0, 0))


whole = pl.BlockSpec(memory_space=pltpu.VMEM)
params_one = pltpu.CompilerParams(vmem_limit_bytes=LIMIT)


def pack_first(info, weight, small):
    return pl.pallas_call(
        pack_first_kernel,
        grid_spec=pltpu.PrefetchScalarGridSpec(
            num_scalar_prefetch=1,
            grid=(1,),
            in_specs=[
                pl.BlockSpec((1, 64, 3072), lambda i, info: (0, info[0], 0)),
                pl.BlockSpec((16, 768), lambda i, info: (0, 0)),
            ],
            out_specs=pl.BlockSpec((8, 80, 768), lambda i, info: (0, 0, 0)),
        ),
        out_shape=jax.ShapeDtypeStruct((8, 80, 768), bf16),
        compiler_params=params_one,
        name="pack_first",
    )(info, weight, small)


def read_small_kernel(info, got, vectors, in_bias, unit_bias):
    z = info[1]
    for layer in range(LAYERS):
        for member in range(6):
            lanes = slice(member * 128, (member + 1) * 128)
            for place in range(8):
                vectors[layer * 6 + member : layer * 6 + member + 1, place * 128 : (place + 1) * 128] = (
                    got[place, 64 + 2 * layer : 65 + 2 * layer, lanes].astype(f32)
                )
        row = slice(65 + 2 * layer, 66 + 2 * layer)
        here = slice(layer, layer + 1)
        for side in range(2):
            at = side * 384
            lanes = pl.ds(pl.multiple_of((z & 1) * 128, 128), 128)
            owner = side * 2 + (z >> 1)
            in_bias[here, at : at + 128] = got[owner, row, lanes].astype(f32)
            in_bias[here, at + 128 : at + 256] = jnp.zeros((1, 128), f32)
            in_bias[here, at + 256 : at + 384] = got[owner + 4, row, lanes].astype(f32)
            unit_bias[here, side * 512 : (side + 1) * 512] = got[side * 4 + z, row, 256:768].astype(f32)


def read_small(info, got):
    return pl.pallas_call(
        read_small_kernel,
        out_shape=(
            jax.ShapeDtypeStruct((12, D), f32),
            jax.ShapeDtypeStruct((LAYERS, 768), f32),
            jax.ShapeDtypeStruct((LAYERS, D), f32),
        ),
        in_specs=[smem, whole],
        out_specs=(whole,) * 3,
        compiler_params=params_one,
        name="read_small",
    )(info, got)


def pack_rest(info, weight, up, down, project):
    return pl.pallas_call(
        pack_rest_kernel,
        grid=(1,),
        out_shape=(
            jax.ShapeDtypeStruct((8, 64, 1024), bf16),
            jax.ShapeDtypeStruct((8, 64, 1792), bf16),
            jax.ShapeDtypeStruct((320, D), bf16),
            jax.ShapeDtypeStruct((320, D), bf16),
        ),
        in_specs=[smem, layer_block((128, 3072), 1), whole, whole, whole],
        out_specs=(whole,) * 4,
        compiler_params=params_one,
        name="pack_rest",
    )(info, weight, up, down, project)


def join_columns(info, got, other, widths):
    return pl.pallas_call(
        join_columns_kernel,
        out_shape=tuple(jax.ShapeDtypeStruct((D, width), bf16) for width in widths),
        in_specs=[smem, whole, whole],
        out_specs=(whole,) * len(widths),
        compiler_params=params_one,
        name="join_columns",
    )(info, got, other)


def join_rows(info, down, project, layer, got, other):
    return pl.pallas_call(
        join_rows_kernel,
        grid=(1,),
        out_shape=(
            jax.ShapeDtypeStruct((D, D), bf16),
            jax.ShapeDtypeStruct((256, D), bf16),
        ),
        in_specs=[smem, layer_block((512, D), layer), layer_block((128, D), layer), whole, whole],
        out_specs=(whole,) * 2,
        compiler_params=params_one,
        name="join_rows",
    )(info, down, project, got, other)


def to_ctx(value):
    return lax.all_to_all(value, CTX, split_axis=0, concat_axis=0, tiled=True)


def in_order(mine, other, core):
    return jnp.where(
        core == 0,
        jnp.concatenate([mine, other], axis=1),
        jnp.concatenate([other, mine], axis=1),
    )


def columns_at(value, at, width):
    return lax.dynamic_slice_in_dim(value, at * width, width, 1)


def forward(hidden, normed_all, params, info, slopes, core, side):
    (_, _, w_in, in_bias, project, project_bias) = params[:6]
    (gain_two, offset_two, up, up_bias, down, down_bias) = params[6:]

    def attention(normed_all):
        projected = (dot(normed_all, w_in) + in_bias).astype(bf16)
        received = swap(columns_at(projected, 1 - core, 384), "core")
        mine = columns_at(projected, core, 384)
        ctx_mine, ctx_other, logsum, rows = attend(info, slopes, mine, received)
        return in_order(ctx_mine, swap(ctx_other, "core"), core), logsum, rows

    side_done, (context, logsum, rows) = beside(side[0], side[1], normed_all, attention)
    parts, own = beside(
        dot_others(context, project, dot),
        scatter_parts,
        context,
        lambda v: dot_own(v, project, dot),
    )
    middle = hidden + sum_parts(own, parts) + project_bias
    normed_two = gather_z(norm(middle, gain_two, offset_two).astype(bf16))
    before = dot(normed_two, up) + up_bias
    activated = gelu(before).astype(bf16)
    last = (middle, activated)
    kept = (hidden, normed_all, logsum, rows, context, middle, normed_two, before, activated)
    return last, kept, side_done


def last_send(last, params):
    return dot_others(last[1], params[10], dot)


def last_sum(last, params, parts):
    return last[0] + sum_parts(dot_own(last[1], params[10], dot), parts) + params[11]


def backward(gradient, grad_down, params, kept, info, slopes, core, fill):
    (gain_one, _, w_in, _, project, _) = params[:6]
    (gain_two, _, up, _, down, _) = params[6:]
    hidden, normed_all, logsum, rows, context, middle, normed_two, before, activated = kept
    sum_down = jnp.sum(gradient.astype(bf16).astype(f32), axis=0)
    d_act = dot_t(grad_down, down)
    d_before = jax.vjp(gelu, before)[1](d_act)[0].astype(bf16)
    sum_up = jnp.sum(d_before.astype(f32), axis=0)

    def outer_work(given):
        activated, grad_down, normed_two, d_before = given
        own = dot_own(d_before, up, dot_t)
        g_down = outer(activated, grad_down).astype(bf16)
        g_up = outer(normed_two, d_before).astype(bf16)
        return own, g_down, g_up

    parts, (own, g_down, g_up) = beside(
        dot_others(d_before, up, dot_t),
        scatter_parts,
        (activated, grad_down, normed_two, d_before),
        outer_work,
    )
    d_normed = sum_parts(own, parts)
    d_values, sum_gain_two, sum_offset_two = norm_back(middle, gain_two, d_normed)
    d_middle = gradient + d_values
    grad_out = d_middle.astype(bf16)
    sum_project = jnp.sum(grad_out.astype(f32), axis=0)
    grad_out_all, outer_state = beside(grad_out, gather_z, (g_down, g_up), fill["outer"])

    def attention(grad_out_all):
        d_context = dot_t(grad_out_all, project).astype(bf16)
        received = swap(columns_at(d_context, 1 - core, 128), "core")
        mine = columns_at(d_context, core, 128)
        d_mine, d_other, sums = attend_back(info, slopes, rows, mine, received, logsum)
        return in_order(d_mine, swap(d_other, "core"), core), sums

    def inner_work(given):
        context, grad_out_all, normed_all, d_joined = given
        own = dot_own(d_joined, w_in, dot_t)
        g_input = outer(normed_all, d_joined).astype(bf16)
        g_project = outer(context, grad_out_all).astype(bf16)
        return own, fill["inner"](g_project, g_input)

    def inner_part(given):
        context, grad_out_all, normed_all = given
        early, (d_joined, sums) = beside(
            fill["early"][0], fill["early"][1], grad_out_all, attention
        )
        return early, sums, beside(
            dot_others(d_joined, w_in, dot_t),
            scatter_parts,
            (context, grad_out_all, normed_all, d_joined),
            inner_work,
        )

    late_send, late_transfer = fill["late"](outer_state)
    late, (early, sums, (parts, (own, inner_state))) = beside(
        late_send, late_transfer, (context, grad_out_all, normed_all), inner_part
    )
    d_normed_one = sum_parts(own, parts)
    d_hidden, sum_gain_one, sum_offset_one = norm_back(hidden, gain_one, d_normed_one)
    small = (
        sum_gain_one,
        sum_offset_one,
        sum_project,
        sum_gain_two,
        sum_offset_two,
        sum_down,
        sums,
        sum_up,
    )
    return d_middle + d_hidden, outer_state, early, late, inner_state, small


def take(value, at, axis=0):
    return lax.dynamic_index_in_dim(value, at, axis, keepdims=False)


def groups_first(value, shape):
    split = value.reshape(shape)
    order = (1, 0) + tuple(range(2, len(shape)))
    return split.transpose(order)


def pack_outer(g_down, g_up):
    pieces = (
        groups_first(g_down, (2, 16, 32, D)).reshape(16, 64, D),
        groups_first(g_up, (8, 16, 8, D)).reshape(16, 64, D),
    )
    return jnp.concatenate(pieces, axis=-1)


def pack_inner(g_project, g_input):
    pieces = (
        groups_first(g_project, (2, 16, 8, 4, 256)).reshape(16, 64, 256),
        groups_first(g_input, (8, 16, 8, 768)).reshape(16, 64, 768),
    )
    return jnp.concatenate(pieces, axis=-1)


def sum_pairs(value, at, axis):
    return take(value, at).astype(f32) + swap(take(value, 1 - at), axis).astype(f32)


def own_rows(summed, split, y_hi, z):
    both = sum_pairs(summed.reshape(2, 32, -1), y_hi, "y_hi").astype(bf16)
    columns = both[:, split:].reshape(4, 8, -1)
    blocks = [take(columns, z)] + [shift_z(take(columns, (z + 4 - k) % 4), 4 - k) for k in (1, 2, 3)]
    blocks = jnp.stack(blocks + blocks)
    columns = lax.dynamic_slice_in_dim(blocks, (4 - z) % 4, 4, 0)
    return jnp.concatenate([both[:, :split], columns.reshape(32, -1)], axis=1)


def project_steps(g_project, place, y_hi):
    x, y_lo, core = place
    pack = g_project.reshape(2, 4, 2, 2, 8, D).transpose(3, 1, 2, 0, 4, 5)
    low = sum_pairs(pack, core, "core").astype(bf16)
    total = take(low, x).astype(f32)
    for k in (1, 2, 3):
        total = total + shift_x(take(low, (x + k) % 4), k).astype(f32)
    low = sum_pairs(total.astype(bf16), y_lo, "y_lo").astype(bf16)
    return sum_pairs(low, y_hi, "y_hi").astype(bf16).reshape(32, 256)


def sum_small(packed, z, y_hi):
    split = packed.reshape(2, 4, -1)
    total = take(split, z, 1)
    for k in (1, 2, 3):
        total = total + shift_z(take(split, (z + k) % 4, 1), k)
    axes = ("y_lo", "y_hi")
    own, other = take(total, y_hi), take(total, 1 - y_hi)
    moves = ((own, [2, 3, 0, 1]), (other, [1, 0, 3, 2]), (other, [3, 2, 1, 0]))
    for value, to in moves:
        own = own + lax.ppermute(value, axes, list(enumerate(to)))
    own = own + shift_x(own, 1) + shift_x(own, 2) + shift_x(own, 3)
    return own + swap(own, "core")


def unpack_outer_kernel(first, second, down, up):
    for layer, full in ((0, first), (1, second)):
        for g in range(16):
            down[layer, g * 32 : (g + 1) * 32, :] = full[g, :, 0:D].astype(f32)
            for four in range(4):
                rows = full[g, four * 8 : (four + 1) * 8, D : 2 * D].astype(f32)
                for side in range(2):
                    at = side * 2048 + four * 512
                    up[layer, g * 8 : (g + 1) * 8, at : at + 512] = rows[
                        :, side * 512 : (side + 1) * 512
                    ]


def unpack_inner_kernel(first, second, inputs, *, at_one, at_two):
    for layer, full, at in ((0, first, at_one), (1, second, at_two)):
        for g in range(16):
            for four in range(4):
                rows = full[g, four * 8 : (four + 1) * 8, at : at + 768].astype(f32)
                for side in range(2):
                    for part in range(3):
                        to = part * D + side * 512 + four * 128
                        inputs[layer, g * 8 : (g + 1) * 8, to : to + 128] = rows[
                            :, (side * 3 + part) * 128 : (side * 3 + part + 1) * 128
                        ]


def unpack_outer(first, second):
    return pl.pallas_call(
        unpack_outer_kernel,
        out_shape=(
            jax.ShapeDtypeStruct((LAYERS, 512, D), f32),
            jax.ShapeDtypeStruct((LAYERS, 128, FF), f32),
        ),
        in_specs=[whole, whole],
        out_specs=(whole, whole),
        compiler_params=params_one,
        name="unpack_outer",
    )(first, second)


def unpack_inner(first, second, at_one, at_two):
    return pl.pallas_call(
        functools.partial(unpack_inner_kernel, at_one=at_one, at_two=at_two),
        out_shape=jax.ShapeDtypeStruct((LAYERS, 128, 3072), f32),
        in_specs=[whole, whole],
        out_specs=whole,
        compiler_params=params_one,
        name="unpack_inner",
    )(first, second)


def pack_small(small, place, z):
    (gain_one, offset_one, project, gain_two, offset_two, down, sums, up) = small
    vectors = [
        v.reshape(8, 128) for v in (gain_one, offset_one, project, gain_two, offset_two, down)
    ]
    sums = sums.reshape(-1)
    inputs = lax.dynamic_update_slice_in_dim(jnp.zeros((2 * D,), f32), sums[:128], place * 128, 0)
    inputs = lax.dynamic_update_slice_in_dim(inputs, sums[256:], D + place * 128, 0)
    units = lax.dynamic_update_slice_in_dim(
        jnp.zeros((2, 4, 512), f32), up.reshape(2, 1, 512), z, 1
    )
    return jnp.concatenate(
        vectors + [inputs.reshape(8, 256), units.reshape(8, 512)], axis=1
    )


def on_device(
    inputs,
    cotangent,
    segments,
    norm_one_gain,
    norm_one_bias,
    input_weight,
    input_bias,
    project_weight,
    project_bias,
    norm_two_gain,
    norm_two_bias,
    up_weight,
    up_bias,
    down_weight,
    down_bias,
):
    y_hi, z = lax.axis_index("y_hi"), lax.axis_index("z")
    x, y_lo, core = lax.axis_index("x"), lax.axis_index("y_lo"), lax.axis_index("core")
    place = core * 4 + z
    rows_in = regroup(inputs[0], core, y_hi)
    cut = jnp.sum((segments[0] < 2).astype(jnp.int32))
    cut = regroup(jnp.broadcast_to(cut, (1, 128)), core, y_hi)[0, 0]
    info = jnp.stack([core, z, cut, y_hi]).astype(jnp.int32)
    corner = jnp.stack([core, z, y_hi, y_hi]).astype(jnp.int32)
    heads = (place * 2 + jnp.arange(2, dtype=jnp.int32)).astype(f32)
    slopes = jnp.exp2(-8.0 * (heads + 1.0) / HEADS)

    small = jnp.concatenate(
        [
            norm_one_gain,
            norm_one_bias,
            project_bias,
            norm_two_gain,
            norm_two_bias,
            down_bias,
            input_bias,
            up_bias,
        ],
        axis=1,
    )
    small = jnp.concatenate([small.reshape(4, 768), jnp.zeros((12, 768), bf16)], axis=0)
    first = pack_first(corner, input_weight, small)
    rows_in, first = lax.optimization_barrier((rows_in, first))
    first = to_ctx(first)
    raw_all = gather_z(rows_in)
    vectors, in_bias, unit_bias = read_small(corner, first)
    (w_first,) = join_columns(corner, first, swap(first, "core"), (768,))

    packed = pack_rest(corner, input_weight, up_weight, down_weight, project_weight)
    up_first = to_ctx(packed[0])
    (up_first,) = join_columns(corner, up_first, swap(up_first, "core"), (D,))

    def layer_rows(layer):
        got = swap(packed[2 + layer], "y_hi")
        return join_rows(corner, down_weight, project_weight, layer, got, swap(got, "core"))

    def layer_params(layer, w_in, up, rows):
        down, project = rows
        vector = [vectors[layer * 6 + i] for i in range(6)]
        return (
            vector[0],
            vector[1],
            w_in,
            in_bias[layer],
            project,
            vector[2],
            vector[3],
            vector[4],
            up,
            unit_bias[layer],
            down,
            vector[5],
        )

    params_0 = layer_params(0, w_first, up_first, layer_rows(0))
    slot = (x, y_lo, core)
    gradient = regroup(cotangent[0], core, y_hi)
    hidden = rows_in.astype(f32)
    normed_all = norm(raw_all.astype(f32), params_0[0], params_0[1]).astype(bf16)
    last, kept_0, second = forward(
        hidden, normed_all, params_0, info, slopes, core, (packed[1], to_ctx)
    )
    up_second, w_second = join_columns(corner, second, swap(second, "core"), (D, 768))
    params_1 = layer_params(1, w_second, up_second, layer_rows(1))
    hidden = last_sum(last, params_0, scatter_parts(last_send(last, params_0)))
    normed_all = gather_z(norm(hidden, params_1[0], params_1[1]).astype(bf16))
    last, kept_1, grad_down = forward(
        hidden, normed_all, params_1, info, slopes, core, (gradient, gather_z)
    )
    gradient = gradient.astype(f32)
    nothing = (jnp.zeros((8, 128), f32), lambda v: v)

    fill = {
        "outer": lambda v: pack_outer(*v),
        "late": lambda state: nothing,
        "early": (last_send(last, params_1), scatter_parts),
        "inner": pack_inner,
    }
    gradient, outer_pack, parts, _, inner_pack, small_1 = backward(
        gradient, grad_down, params_1, kept_1, info, slopes, core, fill
    )
    output = last_sum(last, params_1, parts)
    pack = jnp.concatenate([outer_pack, inner_pack], axis=-1)

    def grp_sum(pack):
        return lax.psum_scatter(pack, GRP, scatter_dimension=0, tiled=True).reshape(64, -1)

    sums_1 = grp_sum(pack)
    grad_down, (output, pack) = beside(
        gradient.astype(bf16), gather_z, (output, pack), lambda v: v
    )

    def core_sum(given):
        split = pack_outer(*given).reshape(8, 2, 64, 2 * D)
        keep, send = take(split, core, 1), take(split, 1 - core, 1)
        return (keep.astype(f32) + swap(send, "core").astype(f32)).astype(bf16)

    def to_xy(value):
        return lax.all_to_all(value, ("x", "y_lo"), split_axis=0, concat_axis=0, tiled=True)

    def own_one(summed):
        outer_1 = own_rows(summed[:, : 2 * D], D, y_hi, z)
        inner_1 = own_rows(summed[:, 2 * D :], 256, y_hi, z)
        return lax.all_gather(jnp.concatenate([outer_1, inner_1], axis=1), GRP)

    fill = {
        "outer": core_sum,
        "late": lambda state: (state, to_xy),
        "early": (sums_1, lambda v: v),
        "inner": lambda g_project, g_input: (
            g_project,
            groups_first(g_input, (8, 16, 8, 768)).reshape(128, 8, 768),
        ),
    }
    gradient, _, sums_1, outer_0, (g_project, input_0), small_0 = backward(
        gradient, grad_down, params_0, kept_0, info, slopes, core, fill
    )
    input_0 = lax.all_to_all(input_0, GRP + CTX, split_axis=0, concat_axis=0, tiled=True)
    full_1 = own_one(sums_1)
    project_0 = project_steps(g_project, slot, y_hi)
    outer_0 = own_rows(jnp.sum(outer_0.astype(f32), axis=0).astype(bf16), D, y_hi, z)
    full_0 = lax.all_gather(jnp.concatenate([outer_0, project_0], axis=1), GRP)
    g_down, g_up = unpack_outer(full_0, full_1)
    g_project = jnp.stack(
        [full[:, :, 2 * D : 2 * D + 256].reshape(128, D) for full in (full_0, full_1)]
    ).astype(f32)
    packed = jnp.concatenate([pack_small(s, place, z) for s in (small_0, small_1)], axis=1)
    vector = sum_small(packed, z, y_hi).reshape(LAYERS, -1)
    input_0 = jnp.sum(input_0.reshape(32, 32, 768).astype(f32), axis=0).astype(bf16)
    input_0, g_down, g_up = lax.optimization_barrier((input_0, g_down, g_up))
    input_0 = lax.all_gather(input_0, GRP)
    g_input = unpack_inner(input_0, full_1, 0, 2 * D + 256)
    parts = [vector[:, i * 128 : (i + 1) * 128] for i in range(6)]
    return (
        regroup(output, core, y_hi)[None],
        regroup(gradient, core, y_hi)[None],
        parts[0],
        parts[1],
        g_input,
        vector[:, 768:1024],
        g_project,
        parts[2],
        parts[3],
        parts[4],
        g_up,
        vector[:, 1024:1536],
        g_down,
        parts[5],
    )


def solution(mesh):
    split = Mesh(mesh.devices.reshape(4, 2, 2, 2, 4), GRP + CTX)
    rows = P(GRP, CTX, None)
    vector = P(None, CTX)
    matrix = P(None, CTX, None)
    weights = (
        vector,
        vector,
        matrix,
        vector,
        matrix,
        vector,
        vector,
        vector,
        matrix,
        vector,
        matrix,
        vector,
    )
    return jax.shard_map(
        on_device,
        mesh=split,
        in_specs=(rows, rows, P(GRP, None)) + weights,
        out_specs=(rows, rows) + weights,
        check_vma=False,
    )
```

```python
import math

import jax
import jax.numpy as jnp
from jax import lax
from jax.experimental import pallas as pl
from jax.experimental.pallas import tpu as pltpu
from jax.sharding import Mesh
from jax.sharding import PartitionSpec as P

D = 1024
HEADS = 16
HEAD_DIM = 64
FF = 4096
PROMPT = 1024
TOKENS = 1536
PIECE = 192
LAYERS = 2
TILE = 256
HALF = 4 * PIECE
SCALE = HEAD_DIM ** (-0.5)
masked_value = -1e30

GRP = ("x", "y_lo", "core")
CTX = ("y_hi", "z")
bf16 = jnp.bfloat16
f32 = jnp.float32


def shift_z(value, step):
    return lax.ppermute(value, "z", [(i, (i + step) % 4) for i in range(4)])


def shift_x(value, step):
    return lax.ppermute(value, "x", [(i, (i + step) % 4) for i in range(4)])


def swap(value, axis):
    return lax.ppermute(value, axis, [(0, 1), (1, 0)])


def regroup(value, core, y_hi):
    got = lax.ppermute(value, ("core", "y_hi"), [(1, 2), (2, 1)])
    return jnp.where(core == y_hi, value, got)


def after(value, *others):
    return lax.optimization_barrier((value, others))[0]


def beside(send, transfer, given, work):
    send, given = lax.optimization_barrier((send, given))
    return lax.optimization_barrier((transfer(send), work(given)))


def gather_z(rows):
    return jnp.concatenate([rows] + [shift_z(rows, k) for k in (1, 2, 3)], axis=0)


def dot(left, right):
    return jnp.dot(left, right, preferred_element_type=f32)


def dot_t(left, right):
    return lax.dot_general(left, right, (((1,), (1,)), ((), ())), preferred_element_type=f32)


def outer(left, right):
    return lax.dot_general(left, right, (((0,), (0,)), ((), ())), preferred_element_type=f32)


def scatter_parts(others):
    return tuple(
        shift_z(others[(k - 1) * PIECE : k * PIECE], -k) for k in (1, 2, 3)
    )


def sum_parts(own, parts):
    total = own
    for part in parts:
        total = total + part.astype(f32)
    return total


def dot_others(left, weight, product):
    return product(left[PIECE:], weight).astype(bf16)


def dot_own(left, weight, product):
    return product(left[:PIECE], weight)


def tile_mask(block, low, high, cut):
    keys = lax.broadcasted_iota(jnp.int32, (high - low, TILE), 0) + low
    queries = lax.broadcasted_iota(jnp.int32, (high - low, TILE), 1) + block * TILE
    visible = keys <= queries
    if block * TILE >= PROMPT:
        visible = visible & ((keys >= cut) | (queries < cut))
    return visible


def fill_bias(bias, slopes, cut):
    keys = lax.broadcasted_iota(jnp.int32, (TOKENS, 128), 0)
    places = jnp.where(keys >= cut, keys - cut + PROMPT, keys).astype(f32)
    for h in range(2):
        bias[h] = places * slopes[h]


def scores_t(keys, queries, bias, block, high, cut):
    low = min(block * TILE, PROMPT)
    scores = dot_t(keys, queries)
    scores = scores + jnp.concatenate([bias[0:high], bias[0:high]], axis=1)
    tail = jnp.where(tile_mask(block, low, high, cut), scores[low:high], masked_value)
    if low == 0:
        return tail
    return jnp.concatenate([scores[:low], tail], axis=0)


def piece_places(info):
    core, z = info[0], info[1]
    out = []
    for side in range(2):
        half = core if side == 0 else 1 - core
        for k in range(4):
            out.append(pl.multiple_of((half * 4 + ((z - k) & 3)) * PIECE, 64))
    return out


def attend_kernel(info, slopes, mine, other, ctx_mine, ctx_other, logsum, rows, ctx, vt, bias):
    spots = piece_places(info)
    cut = info[2]
    for k in range(4):
        span = slice(k * PIECE, (k + 1) * PIECE)
        rows[pl.ds(spots[k], PIECE), :] = mine[span, :]
        rows[pl.ds(spots[4 + k], PIECE), :] = other[span, :]
    fill_bias(bias, slopes, cut)
    vt[...] = rows[:, 256:384].astype(f32).T.astype(bf16)
    for block in range(TOKENS // TILE):
        high = (block + 1) * TILE
        span = slice(block * TILE, high)
        parts = []
        for h in range(2):
            lanes = slice(h * HEAD_DIM, (h + 1) * HEAD_DIM)
            key_lanes = slice(128 + h * HEAD_DIM, 128 + (h + 1) * HEAD_DIM)
            queries = rows[span, lanes] * jnp.asarray(SCALE, bf16)
            scores = scores_t(rows[0:high, key_lanes], queries, bias[h], block, high, cut)
            top = jnp.max(scores, axis=0, keepdims=True)
            weights = jnp.exp(scores - top)
            total = jnp.sum(weights, axis=0, keepdims=True)
            found = dot(vt[lanes, 0:high], weights.astype(bf16))
            parts.append(found * (1.0 / total))
            logsum[h : h + 1, span] = top + jnp.log(total)
        ctx[span, :] = jnp.concatenate(parts, axis=0).T.astype(bf16)
    for k in range(4):
        span = slice(k * PIECE, (k + 1) * PIECE)
        ctx_mine[span, :] = ctx[pl.ds(spots[k], PIECE), :]
        ctx_other[span, :] = ctx[pl.ds(spots[4 + k], PIECE), :]


def attend_back_kernel(
    info, slopes, rows, mine, other, logsum, out_mine, out_other, sums, grad, kt, bias, dq, dk, dv, out
):
    spots = piece_places(info)
    cut = info[2]
    for k in range(4):
        span = slice(k * PIECE, (k + 1) * PIECE)
        grad[pl.ds(spots[k], PIECE), :] = mine[span, :]
        grad[pl.ds(spots[4 + k], PIECE), :] = other[span, :]
    fill_bias(bias, slopes, cut)
    kt[...] = rows[:, 128:256].astype(f32).T.astype(bf16)
    dk[...] = jnp.zeros_like(dk)
    dv[...] = jnp.zeros_like(dv)
    for block in range(TOKENS // TILE):
        high = (block + 1) * TILE
        span = slice(block * TILE, high)
        parts = []
        for h in range(2):
            lanes = slice(h * HEAD_DIM, (h + 1) * HEAD_DIM)
            key_lanes = slice(128 + h * HEAD_DIM, 128 + (h + 1) * HEAD_DIM)
            value_lanes = slice(256 + h * HEAD_DIM, 256 + (h + 1) * HEAD_DIM)
            queries = rows[span, lanes] * jnp.asarray(SCALE, bf16)
            grads = grad[span, lanes]
            scores = scores_t(rows[0:high, key_lanes], queries, bias[h], block, high, cut)
            weights = jnp.exp(scores - logsum[h : h + 1, span])
            d_weights = dot_t(rows[0:high, value_lanes], grads)
            correction = jnp.sum(weights * d_weights, axis=0, keepdims=True)
            d_scores = (weights * (d_weights - correction)).astype(bf16)
            dv[h, 0:high, :] += dot(weights.astype(bf16), grads)
            dk[h, 0:high, :] += dot(d_scores, queries)
            parts.append(dot(kt[lanes, 0:high], d_scores))
        dq[span, :] = (jnp.concatenate(parts, axis=0) * SCALE).T
    out[:, 0:128] = dq[...].astype(bf16)
    out[:, 128:256] = jnp.concatenate([dk[0], dk[1]], axis=1).astype(bf16)
    out[:, 256:384] = jnp.concatenate([dv[0], dv[1]], axis=1).astype(bf16)
    sums[...] = jnp.sum(out[...].astype(f32), axis=0, keepdims=True)
    for k in range(4):
        span = slice(k * PIECE, (k + 1) * PIECE)
        out_mine[span, :] = out[pl.ds(spots[k], PIECE), :]
        out_other[span, :] = out[pl.ds(spots[4 + k], PIECE), :]


smem = pl.BlockSpec(memory_space=pltpu.SMEM)
vmem = pl.BlockSpec(memory_space=pltpu.VMEM)
LIMIT = 40 * 2**20


def attend(info, slopes, mine, other):
    return pl.pallas_call(
        attend_kernel,
        out_shape=(
            jax.ShapeDtypeStruct((HALF, 128), bf16),
            jax.ShapeDtypeStruct((HALF, 128), bf16),
            jax.ShapeDtypeStruct((2, TOKENS), f32),
            jax.ShapeDtypeStruct((TOKENS, 384), bf16),
        ),
        in_specs=[smem, smem, vmem, vmem],
        out_specs=(vmem, vmem, vmem, vmem),
        scratch_shapes=[
            pltpu.VMEM((TOKENS, 128), bf16),
            pltpu.VMEM((128, TOKENS), bf16),
            pltpu.VMEM((2, TOKENS, 128), f32),
        ],
        compiler_params=pltpu.CompilerParams(vmem_limit_bytes=LIMIT),
        cost_estimate=pl.CostEstimate(
            flops=1000000, bytes_accessed=36000000, transcendentals=0
        ),
        name="attend",
    )(info, slopes, mine, other)


def attend_back(info, slopes, rows, mine, other, logsum):
    return pl.pallas_call(
        attend_back_kernel,
        out_shape=(
            jax.ShapeDtypeStruct((HALF, 384), bf16),
            jax.ShapeDtypeStruct((HALF, 384), bf16),
            jax.ShapeDtypeStruct((1, 384), f32),
        ),
        in_specs=[smem, smem, vmem, vmem, vmem, vmem],
        out_specs=(vmem, vmem, vmem),
        scratch_shapes=[
            pltpu.VMEM((TOKENS, 128), bf16),
            pltpu.VMEM((128, TOKENS), bf16),
            pltpu.VMEM((2, TOKENS, 128), f32),
            pltpu.VMEM((TOKENS, 128), f32),
            pltpu.VMEM((2, TOKENS, HEAD_DIM), f32),
            pltpu.VMEM((2, TOKENS, HEAD_DIM), f32),
            pltpu.VMEM((TOKENS, 384), bf16),
        ],
        compiler_params=pltpu.CompilerParams(vmem_limit_bytes=LIMIT),
        cost_estimate=pl.CostEstimate(
            flops=1000000, bytes_accessed=48000000, transcendentals=0
        ),
        name="attend_back",
    )(info, slopes, rows, mine, other, logsum)


def norm_parts(values):
    average = jnp.mean(values, axis=-1, keepdims=True)
    centered = values - average
    variance = jnp.mean(centered * centered, axis=-1, keepdims=True)
    scale = lax.rsqrt(variance + 1e-05)
    return centered * scale, scale


def norm(values, gain, offset):
    return norm_parts(values)[0] * gain + offset


def norm_back(values, gain, grads):
    unit, scale = norm_parts(values)
    weighted = grads * gain
    mean_one = jnp.mean(weighted, axis=-1, keepdims=True)
    mean_two = jnp.mean(weighted * unit, axis=-1, keepdims=True)
    d_values = scale * (weighted - mean_one - unit * mean_two)
    return d_values, jnp.sum(grads * unit, axis=0), jnp.sum(grads, axis=0)


def gelu(values):
    return jax.nn.gelu(values, approximate=True)


PAIR = 2 * PIECE


def wide_down(weight, down):
    for place in range(8):
        for side in range(2):
            at = place * 128 + side * 64
            down[place * 64 : (place + 1) * 64, side * 512 : (side + 1) * 512] = weight[
                0, at : at + 64, 512:1024
            ]


def gelu_parts(u):
    k = math.sqrt(2.0 / math.pi)
    square = u * u
    t = jnp.tanh(k * u * (1.0 + 0.044715 * square))
    half = 0.5 * (1.0 + t)
    slope = half + 0.5 * u * (1.0 - t * t) * (k * (1.0 + 3.0 * 0.044715 * square))
    return u * half, slope


def wide_forward_kernel(rows, weight, bias, own, other, before, down, total):
    step = pl.program_id(0)
    wide_down(weight, down)
    u = dot(rows[...], weight[0, :, 0:512]) + bias[0]
    before[0] = u
    activated = gelu_parts(u)[0].astype(bf16)
    part = dot(activated, down[...])

    @pl.when(step == 0)
    def _():
        total[...] = part

    @pl.when(step > 0)
    def _():
        total[...] += part

    @pl.when(step == 3)
    def _():
        own[...] = total[0:PIECE, :]
        other[...] = total[PIECE:PAIR, :].astype(bf16)


def wide_forward(rows, weight, bias):
    fixed = lambda shape: pl.BlockSpec(shape, lambda i: (0,) * len(shape))
    each = lambda *shape: pl.BlockSpec((1,) + shape, lambda i: (i, 0, 0))
    return pl.pallas_call(
        wide_forward_kernel,
        grid=(4,),
        out_shape=(
            jax.ShapeDtypeStruct((PIECE, D), f32),
            jax.ShapeDtypeStruct((PIECE, D), bf16),
            jax.ShapeDtypeStruct((4, PAIR, 512), f32),
        ),
        in_specs=[fixed((PAIR, D)), each(D, D), each(1, 512)],
        out_specs=(fixed((PIECE, D)), fixed((PIECE, D)), each(PAIR, 512)),
        scratch_shapes=[pltpu.VMEM((512, D), bf16), pltpu.VMEM((PAIR, D), f32)],
        compiler_params=pltpu.CompilerParams(vmem_limit_bytes=58 * 2**20),
        cost_estimate=pl.CostEstimate(
            flops=4 * PAIR * 2048 * D, bytes_accessed=20000000, transcendentals=0
        ),
        name="wide_forward",
    )(rows, weight, bias)


def wide_back_kernel(grads, rows, before, weight, own, other, sums, pack, down, total):
    step = pl.program_id(0)
    wide_down(weight, down)
    activated, slope = gelu_parts(before[0])
    d_before = (dot_t(grads[...], down[...]) * slope).astype(bf16)
    sums[0] = jnp.sum(d_before.astype(f32), axis=0, keepdims=True)
    part = dot_t(d_before, weight[0, :, 0:512])
    g_up = outer(rows[...], d_before).astype(bf16)
    g_down = outer(activated.astype(bf16), grads[...]).astype(bf16)
    for place in range(8):
        for side in range(2):
            at = place * 128 + side * 64
            pack[0, side, place, :, 0:512] = g_up[at : at + 64, :]
            pack[0, side, place, :, 512:1024] = g_down[
                place * 64 : (place + 1) * 64, side * 512 : (side + 1) * 512
            ]

    @pl.when(step == 0)
    def _():
        total[...] = part

    @pl.when(step > 0)
    def _():
        total[...] += part

    @pl.when(step == 3)
    def _():
        own[...] = total[0:PIECE, :]
        other[...] = total[PIECE:PAIR, :].astype(bf16)


def wide_back(grads, rows, before, weight):
    fixed = lambda shape: pl.BlockSpec(shape, lambda i: (0,) * len(shape))
    each = lambda *shape: pl.BlockSpec((1,) + shape, lambda i: (i,) + (0,) * len(shape))
    return pl.pallas_call(
        wide_back_kernel,
        grid=(4,),
        out_shape=(
            jax.ShapeDtypeStruct((PIECE, D), f32),
            jax.ShapeDtypeStruct((PIECE, D), bf16),
            jax.ShapeDtypeStruct((4, 1, 512), f32),
            jax.ShapeDtypeStruct((4, 2, 8, 64, D), bf16),
        ),
        in_specs=[fixed((PAIR, D)), fixed((PAIR, D)), each(PAIR, 512), each(D, D)],
        out_specs=(fixed((PIECE, D)), fixed((PIECE, D)), each(1, 512), each(2, 8, 64, D)),
        scratch_shapes=[pltpu.VMEM((512, D), bf16), pltpu.VMEM((PAIR, D), f32)],
        compiler_params=pltpu.CompilerParams(vmem_limit_bytes=58 * 2**20),
        cost_estimate=pl.CostEstimate(
            flops=10 * PAIR * 2048 * D, bytes_accessed=40000000, transcendentals=0
        ),
        name="wide_back",
    )(grads, rows, before, weight)


QUARTER = 16


def pack_first_kernel(info, weight, small, out):
    for place in range(8):
        for side in range(2):
            for part in range(3):
                at = part * D + side * 512 + (place % 4) * 128
                to = (side * 3 + part) * 128
                out[place, 0:16, to : to + 128] = weight[0, :, at : at + 128]
        out[place, 16:32, :] = small[...]


def pack_rest_kernel(info, weight, up, down, project, first, second, rows, wide):
    core, x = info[0], info[4]
    at_row = pl.ds(pl.multiple_of(core * 64 + x * 16, 16), 16)
    for place in range(8):
        for side in range(2):
            at = side * 2048 + (place % 4) * 512
            to = side * 512
            first[place, :, to : to + 512] = up[0, at_row, at : at + 512]
            for part in range(3):
                at = part * D + side * 512 + (place % 4) * 128
                to = (side * 3 + part) * 128
                second[place, :, to : to + 128] = weight[0, at_row, at : at + 128]
    long = pl.ds(pl.multiple_of(core * 256 + x * 64, 64), 64)
    rows[0:64, :] = down[0, long, :]
    rows[64:80, :] = project[0, at_row, :]
    rows[80:96, :] = project[1, at_row, :]
    wide[0:64, 512:1024] = down[1, long, 0:512]
    wide[64:128, 512:1024] = down[1, long, 512:1024]
    for place in range(8):
        pair = pl.ds(pl.multiple_of(place * 512 + core * 256 + (x >> 1) * 128, 128), 128)
        found = up[1, :, pair].astype(f32)
        found = jnp.where(x % 2 == 0, found[:, 0:64], found[:, 64:128])
        wide[:, place * 64 : (place + 1) * 64] = found.astype(bf16)


def join_columns_kernel(info, mine, other, out):
    core, x = info[0], info[4]
    for pieces, half in ((mine, core), (other, 1 - core)):
        for k in range(4):
            for place in range(8):
                at = place * 128 + half * 64 + ((x - k) & 3) * 16
                out[pl.ds(pl.multiple_of(at, 16), 16), :] = pieces[k, place * 16 : (place + 1) * 16, :]


def join_rows_kernel(info, down, project, mine, other, down_out, project_out, project_next):
    core, x, y_hi = info[0], info[4], info[2]
    down_out[pl.ds(pl.multiple_of(y_hi * 512, 64), 512), :] = down[0]
    own = pl.ds(pl.multiple_of(y_hi * 128, 64), 128)
    project_out[own, :] = project[0]
    project_next[own, :] = project[1]
    for pieces, half in ((mine, core), (other, 1 - core)):
        for k in range(4):
            quarter = (x - k) & 3
            at = (1 - y_hi) * 512 + half * 256 + quarter * 64
            down_out[pl.ds(pl.multiple_of(at, 64), 64), :] = pieces[k, 0:64, :]
            at = pl.ds(pl.multiple_of((1 - y_hi) * 128 + half * 64 + quarter * 16, 16), 16)
            project_out[at, :] = pieces[k, 64:80, :]
            project_next[at, :] = pieces[k, 80:96, :]


def read_small_kernel(info, got, vectors, in_bias, unit_bias):
    z = info[1]
    for layer in range(LAYERS):
        for member in range(6):
            lanes = slice(member * 128, (member + 1) * 128)
            row = layer * 6 + member
            for place in range(8):
                vectors[row : row + 1, place * 128 : (place + 1) * 128] = got[
                    place, 16 + 2 * layer : 17 + 2 * layer, lanes
                ].astype(f32)
        row = slice(17 + 2 * layer, 18 + 2 * layer)
        here = slice(layer, layer + 1)
        for side in range(2):
            at = side * 384
            lanes = pl.ds(pl.multiple_of((z & 1) * 128, 128), 128)
            owner = side * 2 + (z >> 1)
            in_bias[here, at : at + 128] = got[owner, row, lanes].astype(f32)
            in_bias[here, at + 128 : at + 256] = jnp.zeros((1, 128), f32)
            in_bias[here, at + 256 : at + 384] = got[owner + 4, row, lanes].astype(f32)
            unit_bias[here, side * 512 : (side + 1) * 512] = got[side * 4 + z, row, 256:768].astype(f32)


def layer_block(shape, layer):
    return pl.BlockSpec((1,) + shape, lambda i: (layer, 0, 0))


whole = pl.BlockSpec(memory_space=pltpu.VMEM)
params_one = pltpu.CompilerParams(vmem_limit_bytes=LIMIT)


def pack_first(row_block, weight, small):
    return pl.pallas_call(
        pack_first_kernel,
        grid_spec=pltpu.PrefetchScalarGridSpec(
            num_scalar_prefetch=1,
            grid=(1,),
            in_specs=[
                pl.BlockSpec((1, 16, 3072), lambda i, info: (0, info[0], 0)),
                pl.BlockSpec((16, 768), lambda i, info: (0, 0)),
            ],
            out_specs=pl.BlockSpec((8, 32, 768), lambda i, info: (0, 0, 0)),
        ),
        out_shape=jax.ShapeDtypeStruct((8, 32, 768), bf16),
        compiler_params=params_one,
        name="pack_first",
    )(row_block, weight, small)


def pack_rest(info, weight, up, down, project):
    return pl.pallas_call(
        pack_rest_kernel,
        grid=(1,),
        out_shape=(
            jax.ShapeDtypeStruct((8, 16, 1024), bf16),
            jax.ShapeDtypeStruct((8, 16, 768), bf16),
            jax.ShapeDtypeStruct((96, D), bf16),
            jax.ShapeDtypeStruct((128, D), bf16),
        ),
        in_specs=[smem, layer_block((128, 3072), 1), whole, whole, whole],
        out_specs=(whole,) * 4,
        compiler_params=params_one,
        name="pack_rest",
    )(info, weight, up, down, project)


def read_small(info, got):
    return pl.pallas_call(
        read_small_kernel,
        out_shape=(
            jax.ShapeDtypeStruct((12, D), f32),
            jax.ShapeDtypeStruct((LAYERS, 768), f32),
            jax.ShapeDtypeStruct((LAYERS, D), f32),
        ),
        in_specs=[smem, whole],
        out_specs=(whole,) * 3,
        compiler_params=params_one,
        name="read_small",
    )(info, got)


def gather_x(piece):
    return jnp.stack([piece] + [shift_x(piece, k) for k in (1, 2, 3)])


def join_columns(info, mine, other):
    return pl.pallas_call(
        join_columns_kernel,
        out_shape=jax.ShapeDtypeStruct((D, mine.shape[2]), bf16),
        in_specs=[smem, whole, whole],
        out_specs=whole,
        compiler_params=params_one,
        name="join_columns",
    )(info, mine, other)


def join_rows(info, down, project, mine, other):
    return pl.pallas_call(
        join_rows_kernel,
        grid=(1,),
        out_shape=(
            jax.ShapeDtypeStruct((D, D), bf16),
            jax.ShapeDtypeStruct((256, D), bf16),
            jax.ShapeDtypeStruct((256, D), bf16),
        ),
        in_specs=[smem, layer_block((512, D), 0), whole, whole, whole],
        out_specs=(whole,) * 3,
        compiler_params=params_one,
        name="join_rows",
    )(info, down, project, mine, other)


def to_ctx(value):
    return lax.all_to_all(value, CTX, split_axis=0, concat_axis=0, tiled=True)


def in_order(mine, other, core):
    return jnp.where(
        core == 0,
        jnp.concatenate([mine, other], axis=1),
        jnp.concatenate([other, mine], axis=1),
    )


def columns_at(value, at, width):
    return lax.dynamic_slice_in_dim(value, at * width, width, 1)


def forward_attention(normed_all, w_in, in_bias, info, slopes, core, side):
    def attention(normed_all):
        projected = (dot(normed_all, w_in) + in_bias).astype(bf16)
        received = swap(columns_at(projected, 1 - core, 384), "core")
        mine = columns_at(projected, core, 384)
        ctx_mine, ctx_other, logsum, rows = attend(info, slopes, mine, received)
        return in_order(ctx_mine, swap(ctx_other, "core"), core), logsum, rows

    side_done, (context, logsum, rows) = beside(side[0], side[1], normed_all, attention)
    return context, logsum, rows, side_done


def forward_middle(hidden, context, params):
    (project, project_bias, gain_two, offset_two) = params[4:8]
    parts, own = beside(
        dot_others(context, project, dot),
        scatter_parts,
        context,
        lambda v: dot_own(v, project, dot),
    )
    middle = hidden + sum_parts(own, parts) + project_bias
    return middle, norm(middle, gain_two, offset_two).astype(bf16)


def with_rows(middle, normed):
    return middle, gather_z(normed)


def last_send(last, params):
    return dot_others(last[1], params[10], dot)


def last_sum(last, params, parts):
    return last[0] + sum_parts(dot_own(last[1], params[10], dot), parts) + params[11]


def backward_two(grad_down, params, kept, core):
    (up, _, down, _) = params[8:]
    normed_two, before, activated = kept[6:]
    d_act = dot_t(grad_down, down)
    d_before = jax.vjp(gelu, before)[1](d_act)[0].astype(bf16)
    sum_up = jnp.sum(d_before.astype(f32), axis=0)

    def work_two(given):
        activated, grad_down, normed_two, d_before = given
        own = dot_own(d_before, up, dot_t)
        g_down = outer(activated, grad_down).astype(bf16)
        g_up = outer(normed_two, d_before).astype(bf16)
        return own, core_sum(pack_outer(g_down, g_up), core)

    parts, (own, summed) = beside(
        dot_others(d_before, up, dot_t),
        scatter_parts,
        (activated, grad_down, normed_two, d_before),
        work_two,
    )
    return sum_parts(own, parts), summed, sum_up


def backward(gradient, d_normed, sum_up, params, kept, info, slopes, core, across, one):
    (gain_one, _, w_in, _, project, _, gain_two) = params[:7]
    hidden, normed_all, logsum, rows, context, middle = kept[:6]
    sum_down = jnp.sum(gradient.astype(bf16).astype(f32), axis=0)
    d_values, sum_gain_two, sum_offset_two = norm_back(middle, gain_two, d_normed)
    d_middle = gradient + d_values
    grad_out = d_middle.astype(bf16)
    sum_project = jnp.sum(grad_out.astype(f32), axis=0)

    def attention(grad_out):
        grad_out_all = gather_z(grad_out)
        d_context = dot_t(grad_out_all, project).astype(bf16)
        received = swap(columns_at(d_context, 1 - core, 128), "core")
        mine = columns_at(d_context, core, 128)
        d_mine, d_other, sums = attend_back(info, slopes, rows, mine, received, logsum)
        return in_order(d_mine, swap(d_other, "core"), core), sums, grad_out_all

    crossed, (d_joined, sums, grad_out_all) = beside(across[0], across[1], grad_out, attention)

    def work_one(given):
        context, grad_out_all, normed_all, d_joined, crossed = given
        own = dot_own(d_joined, w_in, dot_t)
        g_input = outer(normed_all, d_joined).astype(bf16)
        g_project = outer(context, grad_out_all).astype(bf16)
        return own, one(crossed, g_input, g_project)

    parts, (own, done_one) = beside(
        dot_others(d_joined, w_in, dot_t),
        scatter_parts,
        (context, grad_out_all, normed_all, d_joined, crossed),
        work_one,
    )

    def finish(given):
        own, parts = given
        d_normed_one = sum_parts(own, parts)
        d_hidden, sum_gain_one, sum_offset_one = norm_back(hidden, gain_one, d_normed_one)
        small = (
            sum_gain_one,
            sum_offset_one,
            sum_project,
            sum_gain_two,
            sum_offset_two,
            sum_down,
            sums,
            sum_up,
        )
        return d_middle + d_hidden, small

    return (own, parts), finish, done_one


def take(value, at, axis=0):
    return lax.dynamic_index_in_dim(value, at, axis, keepdims=False)


def groups_first(value, shape):
    split = value.reshape(shape)
    order = (1, 0) + tuple(range(2, len(shape)))
    return split.transpose(order)


def core_sum(pack, core):
    split = pack.reshape(8, 2, 64, -1)
    keep, send = take(split, core, 1), take(split, 1 - core, 1)
    return (keep.astype(f32) + swap(send, "core").astype(f32)).astype(bf16)


def pack_outer(g_down, g_up):
    pieces = (
        groups_first(g_down, (2, 16, 32, D)).reshape(16, 64, D),
        groups_first(g_up, (8, 16, 8, D)).reshape(16, 64, D),
    )
    return jnp.concatenate(pieces, axis=-1)


def pack_inner(g_project, g_input):
    project = g_project.reshape(2, 16, 8, 4, 256).transpose(1, 0, 3, 2, 4).reshape(16, 64, 256)
    return jnp.concatenate(
        [project, groups_first(g_input, (8, 16, 8, 768)).reshape(16, 64, 768)], axis=-1
    )


def to_xy(value):
    return lax.all_to_all(value, ("x", "y_lo"), split_axis=0, concat_axis=0, tiled=True)


def sum_pairs(value, at, axis):
    return take(value, at).astype(f32) + swap(take(value, 1 - at), axis).astype(f32)


def spread_z(both, z):
    columns = both.reshape(4, 8, -1)
    blocks = [take(columns, z)] + [shift_z(take(columns, (z + 4 - k) % 4), 4 - k) for k in (1, 2, 3)]
    blocks = jnp.stack(blocks + blocks)
    return lax.dynamic_slice_in_dim(blocks, (4 - z) % 4, 4, 0).reshape(32, -1)


def y_rows(summed, y_hi):
    return sum_pairs(summed.reshape(2, 32, -1), y_hi, "y_hi").astype(bf16)


def across_y(own, to_hi, to_lo, to_both):
    axes = ("y_lo", "y_hi")
    total = own.astype(f32)
    for value, to in ((to_hi, [1, 0, 3, 2]), (to_lo, [2, 3, 0, 1]), (to_both, [3, 2, 1, 0])):
        total = total + lax.ppermute(value, axes, list(enumerate(to))).astype(f32)
    return total


def inner_core(pack, core):
    split = pack.reshape(4, 2, 2, 64, 1024)
    keep, send = take(split, core, 2), take(split, 1 - core, 2)
    return (keep.astype(f32) + swap(send, "core").astype(f32)).astype(bf16)


def inner_x(low, x):
    total = take(low, x).astype(f32)
    for k in (1, 2, 3):
        total = total + shift_x(take(low, (x + k) % 4), k).astype(f32)
    return total.astype(bf16)


def inner_y(low, y_lo, y_hi):
    split = low.reshape(2, 2, 32, 1024)
    piece = lambda a, b: take(take(split, a), b)
    return across_y(
        piece(y_lo, y_hi),
        piece(y_lo, 1 - y_hi),
        piece(1 - y_lo, y_hi),
        piece(1 - y_lo, 1 - y_hi),
    ).astype(bf16)


def inner_z(both, z):
    return jnp.concatenate([both[:, :256], spread_z(both[:, 256:], z)], axis=1)


def small_z(packed, z):
    split = packed.reshape(2, 4, -1)
    total = take(split, z, 1)
    for k in (1, 2, 3):
        total = total + shift_z(take(split, (z + k) % 4, 1), k)
    return total


def small_y(total, y_hi):
    own, other = take(total, y_hi), take(total, 1 - y_hi)
    return across_y(own, other, own, other)


def small_x(total):
    return total + shift_x(total, 1) + shift_x(total, 2) + shift_x(total, 3)


def unpack_outer_kernel(first, second, down, up):
    for g in range(16):
        down[0, g * 32 : (g + 1) * 32, :] = first[g, :, 0:D].astype(f32)
        for four in range(4):
            rows = first[g, four * 8 : (four + 1) * 8, D : 2 * D].astype(f32)
            for side in range(2):
                at = side * 2048 + four * 512
                up[0, g * 8 : (g + 1) * 8, at : at + 512] = rows[:, side * 512 : (side + 1) * 512]
    for pair in range(2):
        for y_lo in range(2):
            for core in range(2):
                low = second[(pair * 2) * 4 + y_lo * 2 + core].astype(f32)
                high = second[(pair * 2 + 1) * 4 + y_lo * 2 + core].astype(f32)
                for x, block in ((pair * 2, low), (pair * 2 + 1, high)):
                    at = core * 256 + x * 64
                    down[1, at : at + 64, y_lo * 512 : (y_lo + 1) * 512] = block[:, 512:1024]
                for place in range(8):
                    lanes = slice(place * 64, (place + 1) * 64)
                    at = place * 512 + core * 256 + pair * 128
                    up[1, y_lo * 64 : (y_lo + 1) * 64, at : at + 128] = jnp.concatenate(
                        [low[:, lanes], high[:, lanes]], axis=1
                    )


def place_inner(block, layer, row, inputs, project):
    rows = pl.ds(row, 8)
    for four in range(4):
        part_rows = block[four * 8 : (four + 1) * 8, :].astype(f32)
        project[layer, rows, four * 256 : (four + 1) * 256] = part_rows[:, 0:256]
        for side in range(2):
            for part in range(3):
                to = part * D + side * 512 + four * 128
                at = 256 + (side * 3 + part) * 128
                inputs[layer, rows, to : to + 128] = part_rows[:, at : at + 128]


def unpack_inner_kernel(info, mine, other, second, inputs, project):
    core, x, y_lo = info[0], info[4], info[5]
    for pieces, half in ((mine, core), (other, 1 - core)):
        for k in range(4):
            for side in range(2):
                low = y_lo if side == 0 else 1 - y_lo
                g = (((x - k) & 3) * 2 + low) * 2 + half
                place_inner(pieces[k, side], 0, pl.multiple_of(g * 8, 8), inputs, project)
    for g in range(16):
        place_inner(second[g, :, 2048:3072], 1, g * 8, inputs, project)


def unpack_outer(first, second):
    return pl.pallas_call(
        unpack_outer_kernel,
        out_shape=(
            jax.ShapeDtypeStruct((LAYERS, 512, D), f32),
            jax.ShapeDtypeStruct((LAYERS, 128, FF), f32),
        ),
        in_specs=[whole, whole],
        out_specs=(whole, whole),
        compiler_params=params_one,
        name="unpack_outer",
    )(first, second)


def unpack_inner(info, mine, other, second):
    return pl.pallas_call(
        unpack_inner_kernel,
        out_shape=(
            jax.ShapeDtypeStruct((LAYERS, 128, 3072), f32),
            jax.ShapeDtypeStruct((LAYERS, 128, D), f32),
        ),
        in_specs=[smem, whole, whole, whole],
        out_specs=(whole, whole),
        compiler_params=params_one,
        name="unpack_inner",
    )(info, mine, other, second)


def pack_small(small, place):
    (gain_one, offset_one, project, gain_two, offset_two, down, sums, up) = small
    vectors = [
        v.reshape(8, 128) for v in (gain_one, offset_one, project, gain_two, offset_two, down)
    ]
    sums = sums.reshape(-1)
    inputs = lax.dynamic_update_slice_in_dim(jnp.zeros((2 * D,), f32), sums[:128], place * 128, 0)
    inputs = lax.dynamic_update_slice_in_dim(inputs, sums[256:], D + place * 128, 0)
    return jnp.concatenate(vectors + [inputs.reshape(8, 256), up], axis=1)


def on_device(
    inputs,
    cotangent,
    segments,
    norm_one_gain,
    norm_one_bias,
    input_weight,
    input_bias,
    project_weight,
    project_bias,
    norm_two_gain,
    norm_two_bias,
    up_weight,
    up_bias,
    down_weight,
    down_bias,
):
    y_hi, z = lax.axis_index("y_hi"), lax.axis_index("z")
    x, y_lo, core = lax.axis_index("x"), lax.axis_index("y_lo"), lax.axis_index("core")
    place = core * 4 + z
    rows_in = regroup(inputs[0], core, y_hi)
    cut = jnp.sum((segments[0] < 2).astype(jnp.int32))
    cut = regroup(jnp.broadcast_to(cut, (1, 128)), core, y_hi)[0, 0]
    info = jnp.stack([core, z, cut, y_hi]).astype(jnp.int32)
    corner = jnp.stack([core, z, y_hi, core * 4 + x, x, y_lo]).astype(jnp.int32)
    heads = (place * 2 + jnp.arange(2, dtype=jnp.int32)).astype(f32)
    slopes = jnp.exp2(-8.0 * (heads + 1.0) / HEADS)

    small = jnp.concatenate(
        [
            norm_one_gain,
            norm_one_bias,
            project_bias,
            norm_two_gain,
            norm_two_bias,
            down_bias,
            input_bias,
            up_bias,
        ],
        axis=1,
    )
    small = jnp.concatenate([small.reshape(4, 768), jnp.zeros((12, 768), bf16)], axis=0)
    first = pack_first(corner[3:4], input_weight, small)
    rows_in, first = lax.optimization_barrier((rows_in, first))
    first = to_ctx(first)
    raw_all = gather_z(rows_in)
    corner_late, first = lax.optimization_barrier((corner, first))
    first, raw_all = lax.optimization_barrier((first, raw_all))
    vectors, in_bias, unit_bias = read_small(corner, first)
    w_first = gather_x(first[:, 0:16].reshape(128, 768))
    w_first = join_columns(corner, w_first, swap(w_first, "core"))
    up_zero, second, rows, wide = pack_rest(
        corner_late, input_weight, up_weight, down_weight, project_weight
    )
    wide = lax.all_gather(wide, CTX, axis=0, tiled=True)
    rows_zero = swap(rows, "y_hi")
    vector = [vectors[i] for i in range(12)]
    nothing = (jnp.zeros((8, 128), f32), lambda v: v)
    unit_wide = first[:, 19:20, 256:768].reshape(8, 2, 4, 64)
    unit_wide = lax.dynamic_index_in_dim(unit_wide, core, 1, keepdims=False)
    unit_wide = unit_wide.transpose(1, 0, 2).reshape(4, 1, 512).astype(f32)
    hidden = rows_in.astype(f32)
    normed_all = norm(raw_all.astype(f32), vectors[0], vectors[1]).astype(bf16)
    context, logsum, rows_kept, (up_zero, pieces) = forward_attention(
        normed_all,
        w_first,
        in_bias[0],
        info,
        slopes,
        core,
        ((up_zero, rows_zero), lambda v: (to_ctx(v[0]), gather_x(v[1]))),
    )
    down_zero, project_zero, project_one = join_rows(
        corner, down_weight, project_weight, pieces, swap(pieces, "core")
    )
    params_0 = (
        vector[0],
        vector[1],
        w_first,
        in_bias[0],
        project_zero,
        vector[2],
        vector[3],
        vector[4],
    )
    wide, context = lax.optimization_barrier((wide, context))
    wide = lax.all_gather(wide, "x")
    (up_zero, second), (middle, normed_two) = beside(
        (up_zero.reshape(128, D), second),
        lambda v: (gather_x(v[0]), to_ctx(v[1])),
        (hidden, context),
        lambda v: with_rows(*forward_middle(*v, params_0)),
    )
    up_zero = join_columns(corner, up_zero, swap(up_zero, "core"))
    params_0 = params_0 + (up_zero, unit_bias[0], down_zero, vector[5])
    before = dot(normed_two, up_zero) + unit_bias[0]
    activated = gelu(before).astype(bf16)
    last = (middle, activated)
    kept_0 = (hidden, normed_all, logsum, rows_kept, context, middle, normed_two, before, activated)
    w_second = gather_x(second.reshape(128, 768))
    w_second = join_columns(corner, w_second, swap(w_second, "core"))
    hidden = last_sum(last, params_0, scatter_parts(last_send(last, params_0)))
    params_1 = (
        vector[6],
        vector[7],
        w_second,
        in_bias[1],
        project_one,
        vector[8],
        vector[9],
        vector[10],
    )
    normed_all = gather_z(norm(hidden, vector[6], vector[7]).astype(bf16))
    gradient = regroup(cotangent[0], core, y_hi)
    context, logsum, rows_kept, grad_other = forward_attention(
        normed_all, w_second, in_bias[1], info, slopes, core, (gradient, lambda v: swap(v, "core"))
    )
    middle, normed_two = forward_middle(hidden, context, params_1)
    pair_rows = jnp.concatenate([normed_two, swap(normed_two, "core")])
    own, other, before = wide_forward(pair_rows, wide, unit_wide)
    output = middle + (own + swap(other, "core").astype(f32)) + vector[11]
    kept_1 = (hidden, normed_all, logsum, rows_kept, context, middle)
    own, other, sum_up, wide_grads = wide_back(
        jnp.concatenate([gradient, grad_other]), pair_rows, before, wide
    )
    d_normed = own + swap(other, "core").astype(f32)
    wide_grads = lax.psum_scatter(wide_grads, "x", scatter_dimension=0, tiled=True)[0]
    units = lax.dynamic_update_slice_in_dim(
        jnp.zeros((8, 2, 4, 64), f32), sum_up.reshape(4, 8, 64).transpose(1, 0, 2)[:, None], core, 1
    )
    gradient = gradient.astype(f32)

    left, finish, inner_1 = backward(
        gradient,
        d_normed,
        units.reshape(8, 512),
        params_1,
        kept_1,
        info,
        slopes,
        core,
        nothing,
        lambda crossed, g_input, g_project: pack_inner(g_project, g_input),
    )
    gradient, small_1 = finish(left)
    grad_down = gather_z(gradient.astype(bf16))
    grad_down, wide_grads, inner_1 = lax.optimization_barrier((grad_down, wide_grads, inner_1))
    inner_1 = lax.psum_scatter(inner_1, GRP, scatter_dimension=0, tiled=True)[0]

    def to_owners(value):
        axes = ("y_lo",) + CTX
        return lax.all_to_all(value, axes, split_axis=0, concat_axis=0, tiled=True)

    wide_grads, (d_normed, summed, sum_up) = beside(
        wide_grads.reshape(16, 64, D),
        to_owners,
        grad_down,
        lambda v: backward_two(v, params_0, kept_0, core),
    )
    wide_grads = lax.all_gather(jnp.sum(wide_grads.astype(f32), axis=0).astype(bf16), GRP)
    units = lax.dynamic_update_slice_in_dim(
        jnp.zeros((2, 4, 512), f32), sum_up.reshape(2, 1, 512), z, 1
    )

    def work_one(got, g_input, g_project):
        low = inner_core(pack_inner(g_project, g_input), core)
        both = jnp.concatenate([jnp.sum(got.astype(f32), axis=0).astype(bf16), inner_1], axis=1)
        both = y_rows(both, y_hi)
        spread = spread_z(jnp.concatenate([both[:, D : 2 * D], both[:, 2 * D + 256 :]], axis=1), z)
        both = jnp.concatenate(
            [both[:, :D], spread[:, :D], both[:, 2 * D : 2 * D + 256], spread[:, D:]], axis=1
        )
        return low, both

    left, finish, (low, both) = backward(
        gradient,
        d_normed,
        units.reshape(8, 512),
        params_0,
        kept_0,
        info,
        slopes,
        core,
        (summed, to_xy),
        work_one,
    )
    low, (gradient, small_0) = beside(low, lambda v: inner_x(v, x), left, finish)
    full = lax.all_gather(both, GRP)
    packed = jnp.concatenate([pack_small(s, place) for s in (small_0, small_1)], axis=1)
    low, packed = beside(
        low, lambda v: inner_y(v, y_lo, y_hi), packed, lambda v: small_z(v, z)
    )
    low, (packed, gradient) = beside(
        low,
        lambda v: inner_z(v, z),
        (packed, gradient),
        lambda v: (small_y(v[0], y_hi), regroup(v[1], core, y_hi)),
    )
    low, packed = beside(low, lambda v: jnp.stack([v, swap(v, "y_lo")]), packed, small_x)
    low, packed = beside(low, gather_x, packed, lambda v: v + swap(v, "core"))
    g_input, g_project = unpack_inner(corner, low, swap(low, "core"), full)
    g_down, g_up = unpack_outer(full, wide_grads)
    vector = packed.reshape(LAYERS, -1)
    parts = [vector[:, i * 128 : (i + 1) * 128] for i in range(6)]
    return (
        regroup(output, core, y_hi)[None],
        gradient[None],
        parts[0],
        parts[1],
        g_input,
        vector[:, 768:1024],
        g_project,
        parts[2],
        parts[3],
        parts[4],
        g_up,
        vector[:, 1024:1536],
        g_down,
        parts[5],
    )


def solution(mesh):
    split = Mesh(mesh.devices.reshape(4, 2, 2, 2, 4), GRP + CTX)
    rows = P(GRP, CTX, None)
    vector = P(None, CTX)
    matrix = P(None, CTX, None)
    weights = (
        vector,
        vector,
        matrix,
        vector,
        matrix,
        vector,
        vector,
        vector,
        matrix,
        vector,
        matrix,
        vector,
    )
    return jax.shard_map(
        on_device,
        mesh=split,
        in_specs=(rows, rows, P(GRP, None)) + weights,
        out_specs=(rows, rows) + weights,
        check_vma=False,
    )
```

```python
import math

import jax
import jax.numpy as jnp
from jax import lax
from jax.experimental import pallas as pl
from jax.experimental.pallas import tpu as pltpu
from jax.sharding import Mesh
from jax.sharding import PartitionSpec as P

D = 1024
HEADS = 16
HEAD_DIM = 64
FF = 4096
PROMPT = 1024
TOKENS = 1536
PIECE = 192
LAYERS = 2
TILE = 256
HALF = 4 * PIECE
SCALE = HEAD_DIM ** (-0.5)
masked_value = -1e30

GRP = ("x", "y_lo", "core")
CTX = ("y_hi", "z")
bf16 = jnp.bfloat16
f32 = jnp.float32


def shift_z(value, step):
    return lax.ppermute(value, "z", [(i, (i + step) % 4) for i in range(4)])


def shift_x(value, step):
    return lax.ppermute(value, "x", [(i, (i + step) % 4) for i in range(4)])


def swap(value, axis):
    return lax.ppermute(value, axis, [(0, 1), (1, 0)])


def regroup(value, core, y_hi):
    got = lax.ppermute(value, ("core", "y_hi"), [(1, 2), (2, 1)])
    return jnp.where(core == y_hi, value, got)


def after(value, *others):
    return lax.optimization_barrier((value, others))[0]


def beside(send, transfer, given, work):
    send, given = lax.optimization_barrier((send, given))
    return lax.optimization_barrier((transfer(send), work(given)))


def gather_z(rows):
    return jnp.concatenate([rows] + [shift_z(rows, k) for k in (1, 2, 3)], axis=0)


def dot(left, right):
    return jnp.dot(left, right, preferred_element_type=f32)


def dot_t(left, right):
    return lax.dot_general(left, right, (((1,), (1,)), ((), ())), preferred_element_type=f32)


def outer(left, right):
    return lax.dot_general(left, right, (((0,), (0,)), ((), ())), preferred_element_type=f32)


def scatter_parts(others):
    return tuple(
        shift_z(others[(k - 1) * PIECE : k * PIECE], -k) for k in (1, 2, 3)
    )


def sum_parts(own, parts):
    total = own
    for part in parts:
        total = total + part.astype(f32)
    return total


def dot_others(left, weight, product):
    return product(left[PIECE:], weight).astype(bf16)


def dot_own(left, weight, product):
    return product(left[:PIECE], weight)


def tile_mask(block, low, high, cut):
    keys = lax.broadcasted_iota(jnp.int32, (high - low, TILE), 0) + low
    queries = lax.broadcasted_iota(jnp.int32, (high - low, TILE), 1) + block * TILE
    visible = keys <= queries
    if block * TILE >= PROMPT:
        visible = visible & ((keys >= cut) | (queries < cut))
    return visible


def fill_bias(bias, slopes, cut):
    keys = lax.broadcasted_iota(jnp.int32, (TOKENS, 128), 0)
    places = jnp.where(keys >= cut, keys - cut + PROMPT, keys).astype(f32)
    for h in range(2):
        bias[h] = places * slopes[h]


def scores_t(keys, queries, bias, block, high, cut):
    low = min(block * TILE, PROMPT)
    scores = dot_t(keys, queries)
    scores = scores + jnp.concatenate([bias[0:high], bias[0:high]], axis=1)
    tail = jnp.where(tile_mask(block, low, high, cut), scores[low:high], masked_value)
    if low == 0:
        return tail
    return jnp.concatenate([scores[:low], tail], axis=0)


def piece_places(info):
    core, z = info[0], info[1]
    out = []
    for side in range(2):
        half = core if side == 0 else 1 - core
        for k in range(4):
            out.append(pl.multiple_of((half * 4 + ((z - k) & 3)) * PIECE, 64))
    return out


def attend_kernel(info, slopes, mine, other, ctx_mine, ctx_other, logsum, rows, ctx, vt, bias):
    spots = piece_places(info)
    cut = info[2]
    for k in range(4):
        span = slice(k * PIECE, (k + 1) * PIECE)
        rows[pl.ds(spots[k], PIECE), :] = mine[span, :]
        rows[pl.ds(spots[4 + k], PIECE), :] = other[span, :]
    fill_bias(bias, slopes, cut)
    vt[...] = rows[:, 256:384].astype(f32).T.astype(bf16)
    for block in range(TOKENS // TILE):
        high = (block + 1) * TILE
        span = slice(block * TILE, high)
        parts = []
        for h in range(2):
            lanes = slice(h * HEAD_DIM, (h + 1) * HEAD_DIM)
            key_lanes = slice(128 + h * HEAD_DIM, 128 + (h + 1) * HEAD_DIM)
            queries = rows[span, lanes] * jnp.asarray(SCALE, bf16)
            scores = scores_t(rows[0:high, key_lanes], queries, bias[h], block, high, cut)
            top = jnp.max(scores, axis=0, keepdims=True)
            weights = jnp.exp(scores - top)
            total = jnp.sum(weights, axis=0, keepdims=True)
            found = dot(vt[lanes, 0:high], weights.astype(bf16))
            parts.append(found * (1.0 / total))
            logsum[h : h + 1, span] = top + jnp.log(total)
        ctx[span, :] = jnp.concatenate(parts, axis=0).T.astype(bf16)
    for k in range(4):
        span = slice(k * PIECE, (k + 1) * PIECE)
        ctx_mine[span, :] = ctx[pl.ds(spots[k], PIECE), :]
        ctx_other[span, :] = ctx[pl.ds(spots[4 + k], PIECE), :]


def attend_back_kernel(
    info, slopes, rows, mine, other, logsum, out_mine, out_other, sums, grad, kt, bias, dq, dk, dv, out
):
    spots = piece_places(info)
    cut = info[2]
    for k in range(4):
        span = slice(k * PIECE, (k + 1) * PIECE)
        grad[pl.ds(spots[k], PIECE), :] = mine[span, :]
        grad[pl.ds(spots[4 + k], PIECE), :] = other[span, :]
    fill_bias(bias, slopes, cut)
    kt[...] = rows[:, 128:256].astype(f32).T.astype(bf16)
    dk[...] = jnp.zeros_like(dk)
    dv[...] = jnp.zeros_like(dv)
    for block in range(TOKENS // TILE):
        high = (block + 1) * TILE
        span = slice(block * TILE, high)
        parts = []
        for h in range(2):
            lanes = slice(h * HEAD_DIM, (h + 1) * HEAD_DIM)
            key_lanes = slice(128 + h * HEAD_DIM, 128 + (h + 1) * HEAD_DIM)
            value_lanes = slice(256 + h * HEAD_DIM, 256 + (h + 1) * HEAD_DIM)
            queries = rows[span, lanes] * jnp.asarray(SCALE, bf16)
            grads = grad[span, lanes]
            scores = scores_t(rows[0:high, key_lanes], queries, bias[h], block, high, cut)
            weights = jnp.exp(scores - logsum[h : h + 1, span])
            d_weights = dot_t(rows[0:high, value_lanes], grads)
            correction = jnp.sum(weights * d_weights, axis=0, keepdims=True)
            d_scores = (weights * (d_weights - correction)).astype(bf16)
            dv[h, 0:high, :] += dot(weights.astype(bf16), grads)
            dk[h, 0:high, :] += dot(d_scores, queries)
            parts.append(dot(kt[lanes, 0:high], d_scores))
        dq[span, :] = (jnp.concatenate(parts, axis=0) * SCALE).T
    out[:, 0:128] = dq[...].astype(bf16)
    out[:, 128:256] = jnp.concatenate([dk[0], dk[1]], axis=1).astype(bf16)
    out[:, 256:384] = jnp.concatenate([dv[0], dv[1]], axis=1).astype(bf16)
    sums[...] = jnp.sum(out[...].astype(f32), axis=0, keepdims=True)
    for k in range(4):
        span = slice(k * PIECE, (k + 1) * PIECE)
        out_mine[span, :] = out[pl.ds(spots[k], PIECE), :]
        out_other[span, :] = out[pl.ds(spots[4 + k], PIECE), :]


smem = pl.BlockSpec(memory_space=pltpu.SMEM)
vmem = pl.BlockSpec(memory_space=pltpu.VMEM)
LIMIT = 40 * 2**20


def attend(info, slopes, mine, other):
    return pl.pallas_call(
        attend_kernel,
        out_shape=(
            jax.ShapeDtypeStruct((HALF, 128), bf16),
            jax.ShapeDtypeStruct((HALF, 128), bf16),
            jax.ShapeDtypeStruct((2, TOKENS), f32),
            jax.ShapeDtypeStruct((TOKENS, 384), bf16),
        ),
        in_specs=[smem, smem, vmem, vmem],
        out_specs=(vmem, vmem, vmem, vmem),
        scratch_shapes=[
            pltpu.VMEM((TOKENS, 128), bf16),
            pltpu.VMEM((128, TOKENS), bf16),
            pltpu.VMEM((2, TOKENS, 128), f32),
        ],
        compiler_params=pltpu.CompilerParams(vmem_limit_bytes=LIMIT),
        cost_estimate=pl.CostEstimate(
            flops=1000000, bytes_accessed=36000000, transcendentals=0
        ),
        name="attend",
    )(info, slopes, mine, other)


def attend_back(info, slopes, rows, mine, other, logsum):
    return pl.pallas_call(
        attend_back_kernel,
        out_shape=(
            jax.ShapeDtypeStruct((HALF, 384), bf16),
            jax.ShapeDtypeStruct((HALF, 384), bf16),
            jax.ShapeDtypeStruct((1, 384), f32),
        ),
        in_specs=[smem, smem, vmem, vmem, vmem, vmem],
        out_specs=(vmem, vmem, vmem),
        scratch_shapes=[
            pltpu.VMEM((TOKENS, 128), bf16),
            pltpu.VMEM((128, TOKENS), bf16),
            pltpu.VMEM((2, TOKENS, 128), f32),
            pltpu.VMEM((TOKENS, 128), f32),
            pltpu.VMEM((2, TOKENS, HEAD_DIM), f32),
            pltpu.VMEM((2, TOKENS, HEAD_DIM), f32),
            pltpu.VMEM((TOKENS, 384), bf16),
        ],
        compiler_params=pltpu.CompilerParams(vmem_limit_bytes=LIMIT),
        cost_estimate=pl.CostEstimate(
            flops=1000000, bytes_accessed=48000000, transcendentals=0
        ),
        name="attend_back",
    )(info, slopes, rows, mine, other, logsum)


def norm_parts(values):
    average = jnp.mean(values, axis=-1, keepdims=True)
    centered = values - average
    variance = jnp.mean(centered * centered, axis=-1, keepdims=True)
    scale = lax.rsqrt(variance + 1e-05)
    return centered * scale, scale


def norm(values, gain, offset):
    return norm_parts(values)[0] * gain + offset


def norm_back(values, gain, grads):
    unit, scale = norm_parts(values)
    weighted = grads * gain
    mean_one = jnp.mean(weighted, axis=-1, keepdims=True)
    mean_two = jnp.mean(weighted * unit, axis=-1, keepdims=True)
    d_values = scale * (weighted - mean_one - unit * mean_two)
    return d_values, jnp.sum(grads * unit, axis=0), jnp.sum(grads, axis=0)


def gelu(values):
    return jax.nn.gelu(values, approximate=True)


PAIR = 2 * PIECE


def wide_down(weight, down):
    for place in range(8):
        for side in range(2):
            at = place * 128 + side * 64
            down[place * 64 : (place + 1) * 64, side * 512 : (side + 1) * 512] = weight[
                0, at : at + 64, 512:1024
            ]


def gelu_parts(u):
    k = math.sqrt(2.0 / math.pi)
    square = u * u
    t = jnp.tanh(k * u * (1.0 + 0.044715 * square))
    half = 0.5 * (1.0 + t)
    slope = half + 0.5 * u * (1.0 - t * t) * (k * (1.0 + 3.0 * 0.044715 * square))
    return u * half, slope


def wide_kernel(
    rows_own, rows_other, grads_own, grads_other, weight, bias,
    out_own, out_other, d_own, d_other, sums, pack,
    rows, grads, down, total, d_total,
):
    step = pl.program_id(0)

    @pl.when(step == 0)
    def _():
        rows[0:PIECE, :] = rows_own[...]
        rows[PIECE:PAIR, :] = rows_other[...]
        grads[0:PIECE, :] = grads_own[...]
        grads[PIECE:PAIR, :] = grads_other[...]

    wide_down(weight, down)
    up = weight[0, :, 0:512]
    activated, slope = gelu_parts(dot(rows[...], up) + bias[0])
    activated = activated.astype(bf16)
    d_before = (dot_t(grads[...], down[...]) * slope).astype(bf16)
    sums[0] = jnp.sum(d_before.astype(f32), axis=0, keepdims=True)
    part = dot(activated, down[...])
    d_part = dot_t(d_before, up)
    g_up = outer(rows[...], d_before).astype(bf16)
    g_down = outer(activated, grads[...]).astype(bf16)
    for place in range(8):
        for side in range(2):
            at = place * 128 + side * 64
            pack[0, side, place, :, 0:512] = g_up[at : at + 64, :]
            pack[0, side, place, :, 512:1024] = g_down[
                place * 64 : (place + 1) * 64, side * 512 : (side + 1) * 512
            ]

    @pl.when(step == 0)
    def _():
        total[...] = part
        d_total[...] = d_part

    @pl.when(step > 0)
    def _():
        total[...] += part
        d_total[...] += d_part

    @pl.when(step == 3)
    def _():
        out_own[...] = total[0:PIECE, :]
        out_other[...] = total[PIECE:PAIR, :].astype(bf16)
        d_own[...] = d_total[0:PIECE, :]
        d_other[...] = d_total[PIECE:PAIR, :].astype(bf16)


def wide_part(rows_own, rows_other, grads_own, grads_other, weight, bias):
    fixed = pl.BlockSpec((PIECE, D), lambda i: (0, 0))
    each = lambda *shape: pl.BlockSpec((1,) + shape, lambda i: (i,) + (0,) * len(shape))
    return pl.pallas_call(
        wide_kernel,
        grid=(4,),
        out_shape=(
            jax.ShapeDtypeStruct((PIECE, D), f32),
            jax.ShapeDtypeStruct((PIECE, D), bf16),
            jax.ShapeDtypeStruct((PIECE, D), f32),
            jax.ShapeDtypeStruct((PIECE, D), bf16),
            jax.ShapeDtypeStruct((4, 1, 512), f32),
            jax.ShapeDtypeStruct((4, 2, 8, 64, D), bf16),
        ),
        in_specs=[fixed] * 4 + [each(D, D), each(1, 512)],
        out_specs=(fixed,) * 4 + (each(1, 512), each(2, 8, 64, D)),
        scratch_shapes=[
            pltpu.VMEM((PAIR, D), bf16),
            pltpu.VMEM((PAIR, D), bf16),
            pltpu.VMEM((512, D), bf16),
            pltpu.VMEM((PAIR, D), f32),
            pltpu.VMEM((PAIR, D), f32),
        ],
        compiler_params=pltpu.CompilerParams(vmem_limit_bytes=58 * 2**20),
        cost_estimate=pl.CostEstimate(
            flops=14 * PAIR * 2048 * D, bytes_accessed=50000000, transcendentals=0
        ),
        name="wide_part",
    )(rows_own, rows_other, grads_own, grads_other, weight, bias)


QUARTER = 16


def pack_first_kernel(info, weight, small, out):
    for place in range(8):
        for side in range(2):
            for part in range(3):
                at = part * D + side * 512 + (place % 4) * 128
                to = (side * 3 + part) * 128
                out[place, 0:16, to : to + 128] = weight[0, :, at : at + 128]
        out[place, 16:32, :] = small[...]


def pack_rest_kernel(info, weight, up, down, project, first, second, rows, wide):
    core, x = info[0], info[4]
    half = pl.ds(pl.multiple_of(core * 64, 64), 64)
    for place in range(8):
        for side in range(2):
            at = side * 2048 + (place % 4) * 512
            to = side * 512
            first[place, :, to : to + 512] = up[0, half, at : at + 512]
            for part in range(3):
                at = part * D + side * 512 + (place % 4) * 128
                to = (side * 3 + part) * 128
                second[place, :, to : to + 128] = weight[0, half, at : at + 128]
    at_row = pl.ds(pl.multiple_of(core * 64 + x * 16, 16), 16)
    long = pl.ds(pl.multiple_of(core * 256 + x * 64, 64), 64)
    rows[0:64, :] = down[0, long, :]
    rows[64:80, :] = project[0, at_row, :]
    rows[80:96, :] = project[1, at_row, :]
    wide[0:64, 512:1024] = down[1, long, 0:512]
    wide[64:128, 512:1024] = down[1, long, 512:1024]
    for place in range(8):
        pair = pl.ds(pl.multiple_of(place * 512 + core * 256 + (x >> 1) * 128, 128), 128)
        found = up[1, :, pair].astype(f32)
        found = jnp.where(x % 2 == 0, found[:, 0:64], found[:, 64:128])
        wide[:, place * 64 : (place + 1) * 64] = found.astype(bf16)


def join_halves_kernel(info, mine, other, *outs):
    core = info[0]
    for pieces, half in ((mine, core), (other, 1 - core)):
        for place in range(8):
            at = pl.ds(pl.multiple_of(place * 128 + half * 64, 64), 64)
            column = 0
            for out in outs:
                width = out.shape[1]
                out[at, :] = pieces[place, :, column : column + width]
                column += width


def join_halves(info, mine, other, widths):
    return pl.pallas_call(
        join_halves_kernel,
        out_shape=tuple(jax.ShapeDtypeStruct((D, width), bf16) for width in widths),
        in_specs=[smem, whole, whole],
        out_specs=(whole,) * len(widths),
        compiler_params=params_one,
        name="join_halves",
    )(info, mine, other)


def join_columns_kernel(info, mine, other, out):
    core, x = info[0], info[4]
    for pieces, half in ((mine, core), (other, 1 - core)):
        for k in range(4):
            for place in range(8):
                at = place * 128 + half * 64 + ((x - k) & 3) * 16
                out[pl.ds(pl.multiple_of(at, 16), 16), :] = pieces[k, place * 16 : (place + 1) * 16, :]


def join_down_kernel(info, down, mine, other, down_out):
    core, x, y_hi = info[0], info[4], info[2]
    down_out[pl.ds(pl.multiple_of(y_hi * 512, 64), 512), :] = down[0]
    for pieces, half in ((mine, core), (other, 1 - core)):
        for k in range(4):
            at = (1 - y_hi) * 512 + half * 256 + ((x - k) & 3) * 64
            down_out[pl.ds(pl.multiple_of(at, 64), 64), :] = pieces[k, 0:64, :]


def join_project_kernel(info, project, mine, other, first, second):
    core, x, y_hi = info[0], info[4], info[2]
    own = pl.ds(pl.multiple_of(y_hi * 128, 64), 128)
    first[own, :] = project[0]
    second[own, :] = project[1]
    for pieces, half in ((mine, core), (other, 1 - core)):
        for k in range(4):
            at = (1 - y_hi) * 128 + half * 64 + ((x - k) & 3) * 16
            at = pl.ds(pl.multiple_of(at, 16), 16)
            first[at, :] = pieces[k, 64:80, :]
            second[at, :] = pieces[k, 80:96, :]


def read_small_kernel(info, got, vectors, in_bias, unit_bias):
    z = info[1]
    for layer in range(LAYERS):
        for member in range(6):
            lanes = slice(member * 128, (member + 1) * 128)
            row = layer * 6 + member
            for place in range(8):
                vectors[row : row + 1, place * 128 : (place + 1) * 128] = got[
                    place, 16 + 2 * layer : 17 + 2 * layer, lanes
                ].astype(f32)
        row = slice(17 + 2 * layer, 18 + 2 * layer)
        here = slice(layer, layer + 1)
        for side in range(2):
            at = side * 384
            lanes = pl.ds(pl.multiple_of((z & 1) * 128, 128), 128)
            owner = side * 2 + (z >> 1)
            in_bias[here, at : at + 128] = got[owner, row, lanes].astype(f32)
            in_bias[here, at + 128 : at + 256] = jnp.zeros((1, 128), f32)
            in_bias[here, at + 256 : at + 384] = got[owner + 4, row, lanes].astype(f32)
            unit_bias[here, side * 512 : (side + 1) * 512] = got[side * 4 + z, row, 256:768].astype(f32)


def layer_block(shape, layer):
    return pl.BlockSpec((1,) + shape, lambda i: (layer, 0, 0))


whole = pl.BlockSpec(memory_space=pltpu.VMEM)
params_one = pltpu.CompilerParams(vmem_limit_bytes=LIMIT)


def pack_first(row_block, weight, small):
    return pl.pallas_call(
        pack_first_kernel,
        grid_spec=pltpu.PrefetchScalarGridSpec(
            num_scalar_prefetch=1,
            grid=(1,),
            in_specs=[
                pl.BlockSpec((1, 16, 3072), lambda i, info: (0, info[0], 0)),
                pl.BlockSpec((16, 768), lambda i, info: (0, 0)),
            ],
            out_specs=pl.BlockSpec((8, 32, 768), lambda i, info: (0, 0, 0)),
        ),
        out_shape=jax.ShapeDtypeStruct((8, 32, 768), bf16),
        compiler_params=params_one,
        name="pack_first",
    )(row_block, weight, small)


def pack_rest(info, weight, up, down, project):
    return pl.pallas_call(
        pack_rest_kernel,
        grid=(1,),
        out_shape=(
            jax.ShapeDtypeStruct((8, 64, 1024), bf16),
            jax.ShapeDtypeStruct((8, 64, 768), bf16),
            jax.ShapeDtypeStruct((96, D), bf16),
            jax.ShapeDtypeStruct((128, D), bf16),
        ),
        in_specs=[smem, layer_block((128, 3072), 1), whole, whole, whole],
        out_specs=(whole,) * 4,
        compiler_params=params_one,
        name="pack_rest",
    )(info, weight, up, down, project)


def read_small(info, got):
    return pl.pallas_call(
        read_small_kernel,
        out_shape=(
            jax.ShapeDtypeStruct((12, D), f32),
            jax.ShapeDtypeStruct((LAYERS, 768), f32),
            jax.ShapeDtypeStruct((LAYERS, D), f32),
        ),
        in_specs=[smem, whole],
        out_specs=(whole,) * 3,
        compiler_params=params_one,
        name="read_small",
    )(info, got)


def gather_x(piece):
    return jnp.stack([piece] + [shift_x(piece, k) for k in (1, 2, 3)])


def join_columns(info, mine, other):
    return pl.pallas_call(
        join_columns_kernel,
        out_shape=jax.ShapeDtypeStruct((D, mine.shape[2]), bf16),
        in_specs=[smem, whole, whole],
        out_specs=whole,
        compiler_params=params_one,
        name="join_columns",
    )(info, mine, other)


def join_down(info, down, mine, other):
    return pl.pallas_call(
        join_down_kernel,
        grid=(1,),
        out_shape=jax.ShapeDtypeStruct((D, D), bf16),
        in_specs=[smem, layer_block((512, D), 0), whole, whole],
        out_specs=whole,
        compiler_params=params_one,
        name="join_down",
    )(info, down, mine, other)


def join_project(info, project, mine, other):
    return pl.pallas_call(
        join_project_kernel,
        out_shape=(jax.ShapeDtypeStruct((256, D), bf16),) * 2,
        in_specs=[smem, whole, whole, whole],
        out_specs=(whole,) * 2,
        compiler_params=params_one,
        name="join_project",
    )(info, project, mine, other)


def to_ctx(value):
    return lax.all_to_all(value, CTX, split_axis=0, concat_axis=0, tiled=True)


def in_order(mine, other, core):
    return jnp.where(
        core == 0,
        jnp.concatenate([mine, other], axis=1),
        jnp.concatenate([other, mine], axis=1),
    )


def columns_at(value, at, width):
    return lax.dynamic_slice_in_dim(value, at * width, width, 1)


def forward_attention(normed_all, w_in, in_bias, info, slopes, core, side):
    def attention(normed_all):
        projected = (dot(normed_all, w_in) + in_bias).astype(bf16)
        received = swap(columns_at(projected, 1 - core, 384), "core")
        mine = columns_at(projected, core, 384)
        ctx_mine, ctx_other, logsum, rows = attend(info, slopes, mine, received)
        return in_order(ctx_mine, swap(ctx_other, "core"), core), logsum, rows

    side_done, (context, logsum, rows) = beside(side[0], side[1], normed_all, attention)
    return context, logsum, rows, side_done


def forward_middle(hidden, context, params, given=None, work=lambda v: None):
    (project, project_bias, gain_two, offset_two) = params[4:8]
    parts, (own, done) = beside(
        dot_others(context, project, dot),
        scatter_parts,
        (context, given),
        lambda v: (dot_own(v[0], project, dot), work(v[1])),
    )
    middle = hidden + sum_parts(own, parts) + project_bias
    return middle, norm(middle, gain_two, offset_two).astype(bf16), done


def last_send(last, params):
    return dot_others(last[1], params[10], dot)


def last_own(last, params):
    return last[0] + dot_own(last[1], params[10], dot) + params[11]


def backward_two(grad_down, d_before, params, kept, core):
    up = params[8]
    normed_two, _, activated = kept[6:]
    sum_up = jnp.sum(d_before.astype(f32), axis=0)

    def work_two(given):
        activated, grad_down, normed_two, d_before = given
        own = dot_own(d_before, up, dot_t)
        g_down = outer(activated, grad_down).astype(bf16)
        g_up = outer(normed_two, d_before).astype(bf16)
        return own, (g_down, g_up)

    parts, (own, grads) = beside(
        dot_others(d_before, up, dot_t),
        scatter_parts,
        (activated, grad_down, normed_two, d_before),
        work_two,
    )
    return sum_parts(own, parts), grads, sum_up


def backward(gradient, d_normed, sum_up, params, kept, info, slopes, core, across, more):
    (gain_one, _, w_in, _, project, _, gain_two) = params[:7]
    hidden, normed_all, logsum, rows, context, middle = kept[:6]
    sum_down = jnp.sum(gradient.astype(bf16).astype(f32), axis=0)

    d_values, sum_gain_two, sum_offset_two = norm_back(middle, gain_two, d_normed)
    d_middle = gradient + d_values
    grad_out = d_middle.astype(bf16)
    grad_out_all, (sum_project, crossed) = beside(
        grad_out,
        gather_z,
        (grad_out, across[0]),
        lambda v: (jnp.sum(v[0].astype(f32), axis=0), across[1](v[1])),
    )

    def attention(grad_out_all):
        d_context = dot_t(grad_out_all, project).astype(bf16)
        received = swap(columns_at(d_context, 1 - core, 128), "core")
        mine = columns_at(d_context, core, 128)
        d_mine, d_other, sums = attend_back(info, slopes, rows, mine, received, logsum)
        return in_order(d_mine, swap(d_other, "core"), core), sums

    def attention_more(grad_out_all):
        d_joined, sums = attention(grad_out_all)
        return d_joined, sums, more(d_joined, sums, (sum_project, sum_gain_two, sum_offset_two, sum_down, sums, sum_up))

    crossed, (d_joined, sums, done_more) = beside(
        across[2](crossed, context, grad_out_all), across[3], grad_out_all, attention_more
    )

    def g_input():
        return outer(normed_all, d_joined).astype(bf16)

    def scatter(work):
        parts, (own, done) = beside(
            dot_others(d_joined, w_in, dot_t),
            scatter_parts,
            d_joined,
            lambda v: (dot_own(v, w_in, dot_t), work()),
        )
        return (own, parts), done

    vectors = (sum_project, sum_gain_two, sum_offset_two, sum_down, sums, sum_up)
    def finish(given):
        own, parts = given
        d_normed_one = sum_parts(own, parts)
        d_hidden, sum_gain_one, sum_offset_one = norm_back(hidden, gain_one, d_normed_one)
        return d_middle + d_hidden, (sum_gain_one, sum_offset_one)

    return crossed, vectors, done_more, g_input, grad_out_all, scatter, finish


def take(value, at, axis=0):
    return lax.dynamic_index_in_dim(value, at, axis, keepdims=False)


def groups_first(value, shape):
    split = value.reshape(shape)
    order = (1, 0) + tuple(range(2, len(shape)))
    return split.transpose(order)


def core_sum(pack, core):
    split = pack.reshape(8, 2, 64, -1)
    keep, send = take(split, core, 1), take(split, 1 - core, 1)
    return (keep.astype(f32) + swap(send, "core").astype(f32)).astype(bf16)


def pack_outer(g_down, g_up):
    pieces = (
        groups_first(g_down, (2, 16, 32, D)).reshape(16, 64, D),
        groups_first(g_up, (8, 16, 8, D)).reshape(16, 64, D),
    )
    return jnp.concatenate(pieces, axis=-1)


def pack_inner(g_project, g_input):
    project = g_project.reshape(2, 16, 8, 4, 256).transpose(1, 0, 3, 2, 4).reshape(16, 64, 256)
    return jnp.concatenate(
        [project, groups_first(g_input, (8, 16, 8, 768)).reshape(16, 64, 768)], axis=-1
    )


def to_xy(value):
    return lax.all_to_all(value, ("x", "y_lo"), split_axis=0, concat_axis=0, tiled=True)


def sum_pairs(value, at, axis):
    return take(value, at).astype(f32) + swap(take(value, 1 - at), axis).astype(f32)


def spread_z(both, z):
    columns = both.reshape(4, 8, -1)
    blocks = [take(columns, z)] + [shift_z(take(columns, (z + 4 - k) % 4), 4 - k) for k in (1, 2, 3)]
    blocks = jnp.stack(blocks + blocks)
    return lax.dynamic_slice_in_dim(blocks, (4 - z) % 4, 4, 0).reshape(32, -1)


def y_rows(summed, y_hi):
    return sum_pairs(summed.reshape(2, 32, -1), y_hi, "y_hi").astype(bf16)


def across_y(own, to_hi, to_lo, to_both):
    axes = ("y_lo", "y_hi")
    total = own.astype(f32)
    for value, to in ((to_hi, [1, 0, 3, 2]), (to_lo, [2, 3, 0, 1]), (to_both, [3, 2, 1, 0])):
        total = total + lax.ppermute(value, axes, list(enumerate(to))).astype(f32)
    return total


def inner_core(pack, core):
    split = pack.reshape(4, 2, 2, 64, -1)
    keep, send = take(split, core, 2), take(split, 1 - core, 2)
    return (keep.astype(f32) + swap(send, "core").astype(f32)).astype(bf16)


def inner_x(low, x):
    total = take(low, x).astype(f32)
    for k in (1, 2, 3):
        total = total + shift_x(take(low, (x + k) % 4), k).astype(f32)
    return total.astype(bf16)


def inner_y(low, y_lo, y_hi):
    split = low.reshape(2, 2, 32, -1)
    piece = lambda a, b: take(take(split, a), b)
    return across_y(
        piece(y_lo, y_hi),
        piece(y_lo, 1 - y_hi),
        piece(1 - y_lo, y_hi),
        piece(1 - y_lo, 1 - y_hi),
    ).astype(bf16)


def inner_z(both, z):
    return jnp.concatenate([both[:, :256], spread_z(both[:, 256:], z)], axis=1)


def small_z(packed, z):
    split = packed.reshape(2, 4, -1)
    total = take(split, z, 1)
    for k in (1, 2, 3):
        total = total + shift_z(take(split, (z + k) % 4, 1), k)
    return total


def small_y(total, y_hi):
    own, other = take(total, y_hi), take(total, 1 - y_hi)
    return across_y(own, other, own, other)


def small_x(total):
    return total + shift_x(total, 1) + shift_x(total, 2) + shift_x(total, 3)


def unpack_outer_kernel(first, second, down, up):
    for g in range(16):
        down[0, g * 32 : (g + 1) * 32, :] = first[g, :, 0:D].astype(f32)
        for four in range(4):
            rows = first[g, four * 8 : (four + 1) * 8, D : 2 * D].astype(f32)
            for side in range(2):
                at = side * 2048 + four * 512
                up[0, g * 8 : (g + 1) * 8, at : at + 512] = rows[:, side * 512 : (side + 1) * 512]
    for pair in range(2):
        for y_lo in range(2):
            for core in range(2):
                low = second[(pair * 2) * 4 + y_lo * 2 + core].astype(f32)
                high = second[(pair * 2 + 1) * 4 + y_lo * 2 + core].astype(f32)
                for x, block in ((pair * 2, low), (pair * 2 + 1, high)):
                    at = core * 256 + x * 64
                    down[1, at : at + 64, y_lo * 512 : (y_lo + 1) * 512] = block[:, 512:1024]
                for place in range(8):
                    lanes = slice(place * 64, (place + 1) * 64)
                    at = place * 512 + core * 256 + pair * 128
                    up[1, y_lo * 64 : (y_lo + 1) * 64, at : at + 128] = jnp.concatenate(
                        [low[:, lanes], high[:, lanes]], axis=1
                    )


def place_input(block, layer, row, inputs):
    rows = pl.ds(row, 8)
    for four in range(4):
        part_rows = block[four * 8 : (four + 1) * 8, :].astype(f32)
        for side in range(2):
            for part in range(3):
                to = part * D + side * 512 + four * 128
                at = (side * 3 + part) * 128
                inputs[layer, rows, to : to + 128] = part_rows[:, at : at + 128]


def unpack_inner_kernel(full, inputs, project):
    for g in range(16):
        place_input(full[g, :, 3328:4096], 0, g * 8, inputs)
        place_input(full[g, :, 2560:3328], 1, g * 8, inputs)
        for layer, at in ((0, 2048), (1, 2304)):
            block = full[g, :, at : at + 256].astype(f32)
            for four in range(4):
                project[layer, g * 8 : (g + 1) * 8, four * 256 : (four + 1) * 256] = block[
                    four * 8 : (four + 1) * 8, :
                ]


def unpack_outer(first, second):
    return pl.pallas_call(
        unpack_outer_kernel,
        out_shape=(
            jax.ShapeDtypeStruct((LAYERS, 512, D), f32),
            jax.ShapeDtypeStruct((LAYERS, 128, FF), f32),
        ),
        in_specs=[whole, whole],
        out_specs=(whole, whole),
        compiler_params=params_one,
        name="unpack_outer",
    )(first, second)


def unpack_inner(full):
    return pl.pallas_call(
        unpack_inner_kernel,
        out_shape=(
            jax.ShapeDtypeStruct((LAYERS, 128, 3072), f32),
            jax.ShapeDtypeStruct((LAYERS, 128, D), f32),
        ),
        in_specs=[whole],
        out_specs=(whole, whole),
        compiler_params=params_one,
        name="unpack_inner",
    )(full)


def pack_tail_kernel(
    info, g_input, gain, offset, project, gain_two, offset_two, down, sums, up, second, out
):
    core, z = info[0], info[1]
    out[:, :, :, 768:896] = jnp.zeros((16, 8, 8, 128), bf16)
    for owner in range(8):
        for g in range(16):
            at = owner * 128 + g * 8
            out[g, owner, :, 0:768] = g_input[at : at + 8, :]
        for block, vector in enumerate((gain, offset, project, gain_two, offset_two, down)):
            row = vector[0:1, owner * 128 : (owner + 1) * 128]
            out[block // 2, owner, block % 2 : block % 2 + 1, 768:896] = row.astype(bf16)
        for block in range(12):
            row = second[owner : owner + 1, block * 128 : (block + 1) * 128]
            to = 12 + block
            out[to // 2, owner, to % 2 : to % 2 + 1, 768:896] = row.astype(bf16)
    place = core * 4 + z
    for part, base in ((0, 0), (2, 4)):
        for odd in range(2):
            row = sums[0:1, part * 128 : (part + 1) * 128]
            row = jnp.where(place % 2 == odd, row, 0.0).astype(bf16)
            out[3, base + (place >> 1), odd : odd + 1, 768:896] = row
    for side in range(2):
        for block in range(4):
            row = up[0:1, side * 512 + block * 128 : side * 512 + (block + 1) * 128].astype(bf16)
            out[4 + block // 2, side * 4 + z, block % 2 : block % 2 + 1, 768:896] = row


def pack_tail(info, g_input, mixed, vectors, second):
    rows = [v.reshape(1, -1) for v in mixed + vectors]
    out = pl.pallas_call(
        pack_tail_kernel,
        out_shape=jax.ShapeDtypeStruct((16, 8, 8, 896), bf16),
        in_specs=[smem] + [whole] * 10,
        out_specs=whole,
        compiler_params=params_one,
        name="pack_tail",
    )(info, g_input, *rows, second)
    return out.reshape(128, 8, 896)


def pack_small(small, place):
    (gain_one, offset_one, project, gain_two, offset_two, down, sums, up) = small
    vectors = [
        v.reshape(8, 128) for v in (gain_one, offset_one, project, gain_two, offset_two, down)
    ]
    sums = sums.reshape(-1)
    inputs = lax.dynamic_update_slice_in_dim(jnp.zeros((2 * D,), f32), sums[:128], place * 128, 0)
    inputs = lax.dynamic_update_slice_in_dim(inputs, sums[256:], D + place * 128, 0)
    return jnp.concatenate(vectors + [inputs.reshape(8, 256), up], axis=1)


def on_device(
    inputs,
    cotangent,
    segments,
    norm_one_gain,
    norm_one_bias,
    input_weight,
    input_bias,
    project_weight,
    project_bias,
    norm_two_gain,
    norm_two_bias,
    up_weight,
    up_bias,
    down_weight,
    down_bias,
):
    y_hi, z = lax.axis_index("y_hi"), lax.axis_index("z")
    x, y_lo, core = lax.axis_index("x"), lax.axis_index("y_lo"), lax.axis_index("core")
    place = core * 4 + z
    rows_in = regroup(inputs[0], core, y_hi)
    cut = jnp.sum((segments[0] < 2).astype(jnp.int32))
    cut = regroup(jnp.broadcast_to(cut, (1, 128)), core, y_hi)[0, 0]
    info = jnp.stack([core, z, cut, y_hi]).astype(jnp.int32)
    corner = jnp.stack([core, z, y_hi, core * 4 + x, x, y_lo]).astype(jnp.int32)
    heads = (place * 2 + jnp.arange(2, dtype=jnp.int32)).astype(f32)
    slopes = jnp.exp2(-8.0 * (heads + 1.0) / HEADS)

    small = jnp.concatenate(
        [
            norm_one_gain,
            norm_one_bias,
            project_bias,
            norm_two_gain,
            norm_two_bias,
            down_bias,
            input_bias,
            up_bias,
        ],
        axis=1,
    )
    small = jnp.concatenate([small.reshape(4, 768), jnp.zeros((12, 768), bf16)], axis=0)
    first = pack_first(corner[3:4], input_weight, small)
    (raw_all, first), (up_zero, second, rows, wide) = beside(
        (rows_in, first),
        lambda v: (gather_z(v[0]), to_ctx(v[1])),
        corner,
        lambda v: pack_rest(v, input_weight, up_weight, down_weight, project_weight),
    )

    def first_norm(given):
        first, raw_all = given
        vectors, in_bias, unit_bias = read_small(corner, first)
        unit = norm_parts(raw_all.astype(f32))[0]
        normed_all = (unit * vectors[0] + vectors[1]).astype(bf16)
        return vectors, in_bias, unit_bias, normed_all, unit.astype(bf16)

    def first_weight(given):
        first, raw_all, rows = given
        (w_first, rows), parts = beside(
            (first[:, 0:16].reshape(128, 768), rows),
            lambda v: (gather_x(v[0]), swap(v[1], "y_hi")),
            (first, raw_all),
            first_norm,
        )
        return join_columns(corner, w_first, swap(w_first, "core")), rows, parts

    up_zero, (w_first, rows, (vectors, in_bias, unit_bias, normed_all, unit_all)) = beside(
        up_zero, to_ctx, (first, raw_all, rows), first_weight
    )
    wide = lax.all_gather(wide, CTX, axis=0, tiled=True)
    vector = [vectors[i] for i in range(12)]
    nothing = (jnp.zeros((8, 128), f32), lambda v: v, lambda v, *more: v, lambda v: v)
    unit_wide = first[:, 19:20, 256:768].reshape(8, 2, 4, 64)
    unit_wide = lax.dynamic_index_in_dim(unit_wide, core, 1, keepdims=False)
    unit_wide = unit_wide.transpose(1, 0, 2).reshape(4, 1, 512).astype(f32)
    hidden = rows_in.astype(f32)
    context, logsum, rows_kept, (pieces, second) = forward_attention(
        normed_all,
        w_first,
        in_bias[0],
        info,
        slopes,
        core,
        ((rows, second), lambda v: (gather_x(v[0]), to_ctx(v[1]))),
    )
    other = swap(pieces, "core")
    project_zero, project_one = join_project(corner, project_weight, pieces, other)
    context, wide = lax.optimization_barrier((context, wide))
    params_0 = (
        vector[0],
        vector[1],
        w_first,
        in_bias[0],
        project_zero,
        vector[2],
        vector[3],
        vector[4],
    )

    def fetch_other(halves, width):
        return join_halves(corner, halves, swap(halves, "core"), (width,))[0]

    middle, normed, up_zero = forward_middle(
        hidden, context, params_0, up_zero, lambda v: fetch_other(v, D)
    )
    wide = lax.all_gather(after(wide, normed), "x")
    normed_two, (w_second, down_zero) = beside(
        normed,
        gather_z,
        (second, pieces, other),
        lambda v: (fetch_other(v[0], 768), join_down(corner, down_weight, v[1], v[2])),
    )
    params_0 = params_0 + (up_zero, unit_bias[0], down_zero, vector[5])
    before = dot(normed_two, up_zero) + unit_bias[0]
    activated = gelu(before).astype(bf16)
    last = (middle, activated)
    kept_0 = (hidden, normed_all, logsum, rows_kept, context, middle, normed_two, before, activated)
    parts, hidden = beside(
        last_send(last, params_0), scatter_parts, last, lambda v: last_own(v, params_0)
    )
    hidden = sum_parts(hidden, parts)
    normed_all = gather_z(norm(hidden, vector[6], vector[7]).astype(bf16))
    params_1 = (
        vector[6],
        vector[7],
        w_second,
        in_bias[1],
        project_one,
        vector[8],
        vector[9],
        vector[10],
    )
    gradient = regroup(cotangent[0], core, y_hi)
    context, logsum, rows_kept, grad_other = forward_attention(
        normed_all, w_second, in_bias[1], info, slopes, core, (gradient, lambda v: swap(v, "core"))
    )
    middle, normed_two, _ = forward_middle(hidden, context, params_1)
    own, other, d_own, d_other, sum_up, wide_grads = wide_part(
        normed_two, swap(normed_two, "core"), gradient, grad_other, wide, unit_wide
    )
    d_normed = d_own + swap(d_other, "core").astype(f32)
    output = middle + (own + swap(other, "core").astype(f32)) + vector[11]
    kept_1 = (hidden, normed_all, logsum, rows_kept, context, middle)
    wide_grads = lax.psum_scatter(wide_grads, "x", scatter_dimension=0, tiled=True)[0]
    units = lax.dynamic_update_slice_in_dim(
        jnp.zeros((8, 2, 4, 64), f32), sum_up.reshape(4, 8, 64).transpose(1, 0, 2)[:, None], core, 1
    )
    gradient = gradient.astype(f32)

    _, vectors_1, _, g_input, grad_out_all, scatter, finish = backward(
        gradient,
        d_normed,
        units.reshape(8, 512),
        params_1,
        kept_1,
        info,
        slopes,
        core,
        nothing,
        lambda *given: None,
    )
    left, inner_1 = scatter(
        lambda: pack_inner(outer(context, grad_out_all).astype(bf16), g_input())
    )
    gradient, norm_sums = finish(left)
    packed_1 = pack_small(norm_sums + vectors_1, place)
    grad_down, wide_grads = beside(
        gradient.astype(bf16),
        gather_z,
        wide_grads,
        lambda v: sum_pairs(v, y_lo, "y_lo").astype(bf16),
    )
    inner_1, wide_grads = lax.optimization_barrier((inner_1, wide_grads))
    inner_1 = lax.psum_scatter(inner_1, GRP, scatter_dimension=0, tiled=True)[0]
    wide_grads, d_before = beside(
        wide_grads,
        to_ctx,
        (grad_down, kept_0[7]),
        lambda v: jax.vjp(gelu, v[1])[1](dot_t(v[0], params_0[10]))[0].astype(bf16),
    )
    d_normed, grads, sum_up = backward_two(grad_down, d_before, params_0, kept_0, core)
    wide_grads = lax.all_gather(jnp.sum(wide_grads.astype(f32), axis=0).astype(bf16), GRP)

    def with_project(summed, context, grad_out_all):
        g_project = outer(context, grad_out_all).astype(bf16)
        rows = g_project.reshape(2, 16, 8, 4, 256).transpose(1, 0, 3, 2, 4).reshape(16, 64, 256)
        return jnp.concatenate([summed, core_sum(rows, core)], axis=-1)

    def tail_pack(d_joined, sums, vectors):
        w_in = params_0[2].astype(f32)
        gain = jnp.sum(outer(unit_all, d_joined) * w_in, axis=1)
        offset = jnp.sum(d_joined.astype(f32), axis=0, keepdims=True)
        offset = jnp.sum(offset * w_in, axis=1)
        g_input = outer(kept_0[1], d_joined).astype(bf16)
        return pack_tail(info, g_input, (gain, offset), vectors, packed_1)

    crossed, _, low, _, _, scatter, finish = backward(
        gradient,
        d_normed,
        sum_up,
        params_0,
        kept_0,
        info,
        slopes,
        core,
        (grads, lambda v: core_sum(pack_outer(*v), core), with_project, to_xy),
        tail_pack,
    )

    def to_all(value):
        return lax.all_to_all(value, GRP + CTX, split_axis=0, concat_axis=0, tiled=True)

    def outer_rows(given):
        crossed, inner_1 = given
        both = jnp.sum(crossed.astype(f32), axis=0).astype(bf16)
        both = y_rows(jnp.concatenate([both, inner_1], axis=1), y_hi)
        at = 2 * D + 512
        spread = spread_z(jnp.concatenate([both[:, D : 2 * D], both[:, at:]], axis=1), z)
        return [both[:, :D], spread[:, :D], both[:, 2 * D : at], spread[:, D:]]

    low, (both, wide_grads) = beside(
        low, to_all, (crossed, inner_1, wide_grads), lambda v: (outer_rows(v[:2]), v[2])
    )
    left, _ = scatter(lambda: None)
    gradient = regroup(finish(left)[0], core, y_hi)
    low = low.reshape(32, 32, 896).astype(f32)
    vector = jnp.sum(low[:, :, 768:].reshape(128, 8, 128), axis=0)
    vector = jnp.pad(vector, ((0, 24), (0, 0)))
    low = jnp.sum(low[:, :, :768], axis=0)
    low = jnp.concatenate([low, vector], axis=1).astype(bf16)
    full = lax.all_gather(jnp.concatenate(both + [low], axis=1), GRP)
    vector = full[0:12, 0:2, 4096:4224].astype(f32)
    g_input, g_project = unpack_inner(full)
    g_down, g_up = unpack_outer(full, wide_grads)
    packed = vector.reshape(LAYERS * 1536)
    vector = packed.reshape(LAYERS, -1)
    parts = [vector[:, i * 128 : (i + 1) * 128] for i in range(6)]
    return (
        regroup(output, core, y_hi)[None],
        gradient[None],
        parts[0],
        parts[1],
        g_input,
        vector[:, 768:1024],
        g_project,
        parts[2],
        parts[3],
        parts[4],
        g_up,
        vector[:, 1024:1536],
        g_down,
        parts[5],
    )


def solution(mesh):
    split = Mesh(mesh.devices.reshape(4, 2, 2, 2, 4), GRP + CTX)
    rows = P(GRP, CTX, None)
    vector = P(None, CTX)
    matrix = P(None, CTX, None)
    weights = (
        vector,
        vector,
        matrix,
        vector,
        matrix,
        vector,
        vector,
        vector,
        matrix,
        vector,
        matrix,
        vector,
    )
    return jax.shard_map(
        on_device,
        mesh=split,
        in_specs=(rows, rows, P(GRP, None)) + weights,
        out_specs=(rows, rows) + weights,
        check_vma=False,
    )
```

```python
import math

import jax
import jax.numpy as jnp
from jax import lax
from jax.experimental import pallas as pl
from jax.experimental.pallas import tpu as pltpu
from jax.sharding import Mesh
from jax.sharding import PartitionSpec as P

D = 1024
HEADS = 16
HEAD_DIM = 64
FF = 4096
PROMPT = 1024
TOKENS = 1536
PIECE = 192
LAYERS = 2
TILE = 256
HALF = 4 * PIECE
SCALE = HEAD_DIM ** (-0.5)
masked_value = -1e30

GRP = ("x", "y_lo", "core")
CTX = ("y_hi", "z")
bf16 = jnp.bfloat16
f32 = jnp.float32


def shift_z(value, step):
    return lax.ppermute(value, "z", [(i, (i + step) % 4) for i in range(4)])


def shift_x(value, step):
    return lax.ppermute(value, "x", [(i, (i + step) % 4) for i in range(4)])


def swap(value, axis):
    return lax.ppermute(value, axis, [(0, 1), (1, 0)])


def regroup(value, core, y_hi):
    got = lax.ppermute(value, ("core", "y_hi"), [(1, 2), (2, 1)])
    return jnp.where(core == y_hi, value, got)


def after(value, *others):
    return lax.optimization_barrier((value, others))[0]


def beside(send, transfer, given, work):
    send, given = lax.optimization_barrier((send, given))
    return lax.optimization_barrier((transfer(send), work(given)))


def gather_z(rows):
    half = rows.shape[0] // 2
    first, second = rows[:half], rows[half:]
    first_left, second_right = shift_z(first, 1), shift_z(second, 3)
    second_left, first_right = shift_z(second, 1), shift_z(first, 3)
    first_left, second_right = lax.optimization_barrier((first_left, second_right))
    first_far, second_far = shift_z(first_left, 1), shift_z(second_right, 3)
    return jnp.concatenate(
        [rows, first_left, second_left, first_far, second_far, first_right, second_right], axis=0
    )


def dot(left, right):
    return jnp.dot(left, right, preferred_element_type=f32)


def dot_t(left, right):
    return lax.dot_general(left, right, (((1,), (1,)), ((), ())), preferred_element_type=f32)


def outer(left, right):
    return lax.dot_general(left, right, (((0,), (0,)), ((), ())), preferred_element_type=f32)


def scatter_parts(others):
    return tuple(
        shift_z(others[(k - 1) * PIECE : k * PIECE], -k) for k in (1, 2, 3)
    )


def sum_parts(own, parts):
    total = own
    for part in parts:
        total = total + part.astype(f32)
    return total


def dot_others(left, weight, product):
    return product(left[PIECE:], weight).astype(bf16)


def dot_own(left, weight, product):
    return product(left[:PIECE], weight)


def tile_mask(block, low, high, cut):
    keys = lax.broadcasted_iota(jnp.int32, (high - low, TILE), 0) + low
    queries = lax.broadcasted_iota(jnp.int32, (high - low, TILE), 1) + block * TILE
    visible = keys <= queries
    if block * TILE >= PROMPT:
        visible = visible & ((keys >= cut) | (queries < cut))
    return visible


def fill_bias(bias, slopes, cut):
    keys = lax.broadcasted_iota(jnp.int32, (TOKENS, 128), 0)
    places = jnp.where(keys >= cut, keys - cut + PROMPT, keys).astype(f32)
    for h in range(2):
        bias[h] = places * slopes[h]


def scores_t(keys, queries, bias, block, high, cut):
    low = min(block * TILE, PROMPT)
    scores = dot_t(keys, queries)
    scores = scores + jnp.concatenate([bias[0:high], bias[0:high]], axis=1)
    tail = jnp.where(tile_mask(block, low, high, cut), scores[low:high], masked_value)
    if low == 0:
        return tail
    return jnp.concatenate([scores[:low], tail], axis=0)


def piece_places(info):
    core, z = info[0], info[1]
    out = []
    for side in range(2):
        half = core if side == 0 else 1 - core
        for k in range(4):
            out.append(pl.multiple_of((half * 4 + ((z - k) & 3)) * PIECE, 64))
    return out


def attend_kernel(info, slopes, mine, other, ctx_mine, ctx_other, logsum, rows, ctx, vt, bias):
    spots = piece_places(info)
    cut = info[2]
    for k in range(4):
        span = slice(k * PIECE, (k + 1) * PIECE)
        rows[pl.ds(spots[k], PIECE), :] = mine[span, :]
        rows[pl.ds(spots[4 + k], PIECE), :] = other[span, :]
    fill_bias(bias, slopes, cut)
    vt[...] = rows[:, 256:384].astype(f32).T.astype(bf16)
    for block in range(TOKENS // TILE):
        high = (block + 1) * TILE
        span = slice(block * TILE, high)
        parts = []
        for h in range(2):
            lanes = slice(h * HEAD_DIM, (h + 1) * HEAD_DIM)
            key_lanes = slice(128 + h * HEAD_DIM, 128 + (h + 1) * HEAD_DIM)
            queries = rows[span, lanes] * jnp.asarray(SCALE, bf16)
            scores = scores_t(rows[0:high, key_lanes], queries, bias[h], block, high, cut)
            top = jnp.max(scores, axis=0, keepdims=True)
            weights = jnp.exp(scores - top)
            total = jnp.sum(weights, axis=0, keepdims=True)
            found = dot(vt[lanes, 0:high], weights.astype(bf16))
            parts.append(found * (1.0 / total))
            logsum[h : h + 1, span] = top + jnp.log(total)
        ctx[span, :] = jnp.concatenate(parts, axis=0).T.astype(bf16)
    for k in range(4):
        span = slice(k * PIECE, (k + 1) * PIECE)
        ctx_mine[span, :] = ctx[pl.ds(spots[k], PIECE), :]
        ctx_other[span, :] = ctx[pl.ds(spots[4 + k], PIECE), :]


def attend_back_kernel(
    info, slopes, rows, mine, other, logsum, out_mine, out_other, sums, grad, kt, bias, dq, dk, dv, out
):
    spots = piece_places(info)
    cut = info[2]
    for k in range(4):
        span = slice(k * PIECE, (k + 1) * PIECE)
        grad[pl.ds(spots[k], PIECE), :] = mine[span, :]
        grad[pl.ds(spots[4 + k], PIECE), :] = other[span, :]
    fill_bias(bias, slopes, cut)
    kt[...] = rows[:, 128:256].astype(f32).T.astype(bf16)
    dk[...] = jnp.zeros_like(dk)
    dv[...] = jnp.zeros_like(dv)
    for block in range(TOKENS // TILE):
        high = (block + 1) * TILE
        span = slice(block * TILE, high)
        parts = []
        for h in range(2):
            lanes = slice(h * HEAD_DIM, (h + 1) * HEAD_DIM)
            key_lanes = slice(128 + h * HEAD_DIM, 128 + (h + 1) * HEAD_DIM)
            value_lanes = slice(256 + h * HEAD_DIM, 256 + (h + 1) * HEAD_DIM)
            queries = rows[span, lanes] * jnp.asarray(SCALE, bf16)
            grads = grad[span, lanes]
            scores = scores_t(rows[0:high, key_lanes], queries, bias[h], block, high, cut)
            weights = jnp.exp(scores - logsum[h : h + 1, span])
            d_weights = dot_t(rows[0:high, value_lanes], grads)
            correction = jnp.sum(weights * d_weights, axis=0, keepdims=True)
            d_scores = (weights * (d_weights - correction)).astype(bf16)
            dv[h, 0:high, :] += dot(weights.astype(bf16), grads)
            dk[h, 0:high, :] += dot(d_scores, queries)
            parts.append(dot(kt[lanes, 0:high], d_scores))
        dq[span, :] = (jnp.concatenate(parts, axis=0) * SCALE).T
    out[:, 0:128] = dq[...].astype(bf16)
    out[:, 128:256] = jnp.concatenate([dk[0], dk[1]], axis=1).astype(bf16)
    out[:, 256:384] = jnp.concatenate([dv[0], dv[1]], axis=1).astype(bf16)
    sums[...] = jnp.sum(out[...].astype(f32), axis=0, keepdims=True)
    for k in range(4):
        span = slice(k * PIECE, (k + 1) * PIECE)
        out_mine[span, :] = out[pl.ds(spots[k], PIECE), :]
        out_other[span, :] = out[pl.ds(spots[4 + k], PIECE), :]


smem = pl.BlockSpec(memory_space=pltpu.SMEM)
vmem = pl.BlockSpec(memory_space=pltpu.VMEM)
LIMIT = 40 * 2**20


def attend(info, slopes, mine, other):
    return pl.pallas_call(
        attend_kernel,
        out_shape=(
            jax.ShapeDtypeStruct((HALF, 128), bf16),
            jax.ShapeDtypeStruct((HALF, 128), bf16),
            jax.ShapeDtypeStruct((2, TOKENS), f32),
            jax.ShapeDtypeStruct((TOKENS, 384), bf16),
        ),
        in_specs=[smem, smem, vmem, vmem],
        out_specs=(vmem, vmem, vmem, vmem),
        scratch_shapes=[
            pltpu.VMEM((TOKENS, 128), bf16),
            pltpu.VMEM((128, TOKENS), bf16),
            pltpu.VMEM((2, TOKENS, 128), f32),
        ],
        compiler_params=pltpu.CompilerParams(vmem_limit_bytes=LIMIT),
        cost_estimate=pl.CostEstimate(
            flops=1000000, bytes_accessed=36000000, transcendentals=0
        ),
        name="attend",
    )(info, slopes, mine, other)


def attend_back(info, slopes, rows, mine, other, logsum):
    return pl.pallas_call(
        attend_back_kernel,
        out_shape=(
            jax.ShapeDtypeStruct((HALF, 384), bf16),
            jax.ShapeDtypeStruct((HALF, 384), bf16),
            jax.ShapeDtypeStruct((1, 384), f32),
        ),
        in_specs=[smem, smem, vmem, vmem, vmem, vmem],
        out_specs=(vmem, vmem, vmem),
        scratch_shapes=[
            pltpu.VMEM((TOKENS, 128), bf16),
            pltpu.VMEM((128, TOKENS), bf16),
            pltpu.VMEM((2, TOKENS, 128), f32),
            pltpu.VMEM((TOKENS, 128), f32),
            pltpu.VMEM((2, TOKENS, HEAD_DIM), f32),
            pltpu.VMEM((2, TOKENS, HEAD_DIM), f32),
            pltpu.VMEM((TOKENS, 384), bf16),
        ],
        compiler_params=pltpu.CompilerParams(vmem_limit_bytes=LIMIT),
        cost_estimate=pl.CostEstimate(
            flops=1000000, bytes_accessed=48000000, transcendentals=0
        ),
        name="attend_back",
    )(info, slopes, rows, mine, other, logsum)


def norm_parts(values):
    average = jnp.mean(values, axis=-1, keepdims=True)
    centered = values - average
    variance = jnp.mean(centered * centered, axis=-1, keepdims=True)
    scale = lax.rsqrt(variance + 1e-05)
    return centered * scale, scale


def norm(values, gain, offset):
    return norm_parts(values)[0] * gain + offset


def norm_back(values, gain, grads):
    unit, scale = norm_parts(values)
    weighted = grads * gain
    mean_one = jnp.mean(weighted, axis=-1, keepdims=True)
    mean_two = jnp.mean(weighted * unit, axis=-1, keepdims=True)
    d_values = scale * (weighted - mean_one - unit * mean_two)
    return d_values, jnp.sum(grads * unit, axis=0), jnp.sum(grads, axis=0)


def gelu(values):
    return jax.nn.gelu(values, approximate=True)


PAIR = 2 * PIECE


def wide_down(weight, down):
    for place in range(8):
        for side in range(2):
            at = place * 128 + side * 64
            down[place * 64 : (place + 1) * 64, side * 512 : (side + 1) * 512] = weight[
                0, at : at + 64, 512:1024
            ]


def gelu_parts(u):
    k = math.sqrt(2.0 / math.pi)
    square = u * u
    t = jnp.tanh(k * u * (1.0 + 0.044715 * square))
    half = 0.5 * (1.0 + t)
    slope = half + 0.5 * u * (1.0 - t * t) * (k * (1.0 + 3.0 * 0.044715 * square))
    return u * half, slope


def wide_kernel(
    rows_own, rows_other, grads_own, grads_other, weight, bias,
    out_own, out_other, d_own, d_other, sums, pack,
    rows, grads, down, total, d_total,
):
    step = pl.program_id(0)

    @pl.when(step == 0)
    def _():
        rows[0:PIECE, :] = rows_own[...]
        rows[PIECE:PAIR, :] = rows_other[...]
        grads[0:PIECE, :] = grads_own[...]
        grads[PIECE:PAIR, :] = grads_other[...]

    wide_down(weight, down)
    up = weight[0, :, 0:512]
    activated, slope = gelu_parts(dot(rows[...], up) + bias[0])
    activated = activated.astype(bf16)
    d_before = (dot_t(grads[...], down[...]) * slope).astype(bf16)
    sums[0] = jnp.sum(d_before.astype(f32), axis=0, keepdims=True)
    part = dot(activated, down[...])
    d_part = dot_t(d_before, up)
    g_up = outer(rows[...], d_before).astype(bf16)
    g_down = outer(activated, grads[...]).astype(bf16)
    for place in range(8):
        for side in range(2):
            at = place * 128 + side * 64
            pack[0, side, place, :, 0:512] = g_up[at : at + 64, :]
            pack[0, side, place, :, 512:1024] = g_down[
                place * 64 : (place + 1) * 64, side * 512 : (side + 1) * 512
            ]

    @pl.when(step == 0)
    def _():
        total[...] = part
        d_total[...] = d_part

    @pl.when(step > 0)
    def _():
        total[...] += part
        d_total[...] += d_part

    @pl.when(step == 3)
    def _():
        out_own[...] = total[0:PIECE, :]
        out_other[...] = total[PIECE:PAIR, :].astype(bf16)
        d_own[...] = d_total[0:PIECE, :]
        d_other[...] = d_total[PIECE:PAIR, :].astype(bf16)


def wide_part(rows_own, rows_other, grads_own, grads_other, weight, bias):
    fixed = pl.BlockSpec((PIECE, D), lambda i: (0, 0))
    each = lambda *shape: pl.BlockSpec((1,) + shape, lambda i: (i,) + (0,) * len(shape))
    return pl.pallas_call(
        wide_kernel,
        grid=(4,),
        out_shape=(
            jax.ShapeDtypeStruct((PIECE, D), f32),
            jax.ShapeDtypeStruct((PIECE, D), bf16),
            jax.ShapeDtypeStruct((PIECE, D), f32),
            jax.ShapeDtypeStruct((PIECE, D), bf16),
            jax.ShapeDtypeStruct((4, 1, 512), f32),
            jax.ShapeDtypeStruct((4, 2, 8, 64, D), bf16),
        ),
        in_specs=[fixed] * 4 + [each(D, D), each(1, 512)],
        out_specs=(fixed,) * 4 + (each(1, 512), each(2, 8, 64, D)),
        scratch_shapes=[
            pltpu.VMEM((PAIR, D), bf16),
            pltpu.VMEM((PAIR, D), bf16),
            pltpu.VMEM((512, D), bf16),
            pltpu.VMEM((PAIR, D), f32),
            pltpu.VMEM((PAIR, D), f32),
        ],
        compiler_params=pltpu.CompilerParams(vmem_limit_bytes=58 * 2**20),
        cost_estimate=pl.CostEstimate(
            flops=14 * PAIR * 2048 * D, bytes_accessed=50000000, transcendentals=0
        ),
        name="wide_part",
    )(rows_own, rows_other, grads_own, grads_other, weight, bias)


QUARTER = 16


def pack_first_kernel(info, weight, small, out):
    for place in range(8):
        for side in range(2):
            for part in range(3):
                at = part * D + side * 512 + (place % 4) * 128
                to = (side * 3 + part) * 128
                out[place, 0:16, to : to + 128] = weight[0, :, at : at + 128]
        out[place, 16:32, :] = small[...]


def pack_rest_kernel(info, weight, up, down, project, first, second, rows, wide):
    core, x = info[0], info[4]
    half = pl.ds(pl.multiple_of(core * 64, 64), 64)
    for place in range(8):
        for side in range(2):
            at = side * 2048 + (place % 4) * 512
            to = side * 512
            first[place, :, to : to + 512] = up[0, half, at : at + 512]
            for part in range(3):
                at = part * D + side * 512 + (place % 4) * 128
                to = (side * 3 + part) * 128
                second[place, :, to : to + 128] = weight[0, half, at : at + 128]
    at_row = pl.ds(pl.multiple_of(core * 64 + x * 16, 16), 16)
    long = pl.ds(pl.multiple_of(core * 256 + x * 64, 64), 64)
    rows[0:64, :] = down[0, long, :]
    rows[64:80, :] = project[0, at_row, :]
    rows[80:96, :] = project[1, at_row, :]
    wide[0:64, 512:1024] = down[1, long, 0:512]
    wide[64:128, 512:1024] = down[1, long, 512:1024]
    for place in range(8):
        pair = pl.ds(pl.multiple_of(place * 512 + core * 256 + (x >> 1) * 128, 128), 128)
        found = up[1, :, pair].astype(f32)
        found = jnp.where(x % 2 == 0, found[:, 0:64], found[:, 64:128])
        wide[:, place * 64 : (place + 1) * 64] = found.astype(bf16)


def join_halves_kernel(info, mine, other, *outs):
    core = info[0]
    for pieces, half in ((mine, core), (other, 1 - core)):
        for place in range(8):
            at = pl.ds(pl.multiple_of(place * 128 + half * 64, 64), 64)
            column = 0
            for out in outs:
                width = out.shape[1]
                out[at, :] = pieces[place, :, column : column + width]
                column += width


def join_halves(info, mine, other, widths):
    return pl.pallas_call(
        join_halves_kernel,
        out_shape=tuple(jax.ShapeDtypeStruct((D, width), bf16) for width in widths),
        in_specs=[smem, whole, whole],
        out_specs=(whole,) * len(widths),
        compiler_params=params_one,
        name="join_halves",
    )(info, mine, other)


def join_columns_kernel(info, mine, other, out):
    core, x = info[0], info[4]
    for pieces, half in ((mine, core), (other, 1 - core)):
        for k in range(4):
            for place in range(8):
                at = place * 128 + half * 64 + ((x - k) & 3) * 16
                out[pl.ds(pl.multiple_of(at, 16), 16), :] = pieces[k, place * 16 : (place + 1) * 16, :]


def join_down_kernel(info, down, mine, other, down_out):
    core, x, y_hi = info[0], info[4], info[2]
    down_out[pl.ds(pl.multiple_of(y_hi * 512, 64), 512), :] = down[0]
    for pieces, half in ((mine, core), (other, 1 - core)):
        for k in range(4):
            at = (1 - y_hi) * 512 + half * 256 + ((x - k) & 3) * 64
            down_out[pl.ds(pl.multiple_of(at, 64), 64), :] = pieces[k, 0:64, :]


def join_project_kernel(info, project, mine, other, first, second):
    core, x, y_hi = info[0], info[4], info[2]
    own = pl.ds(pl.multiple_of(y_hi * 128, 64), 128)
    first[own, :] = project[0]
    second[own, :] = project[1]
    for pieces, half in ((mine, core), (other, 1 - core)):
        for k in range(4):
            at = (1 - y_hi) * 128 + half * 64 + ((x - k) & 3) * 16
            at = pl.ds(pl.multiple_of(at, 16), 16)
            first[at, :] = pieces[k, 64:80, :]
            second[at, :] = pieces[k, 80:96, :]


def read_small_kernel(info, got, vectors, in_bias, unit_bias):
    z = info[1]
    for layer in range(LAYERS):
        for member in range(6):
            lanes = slice(member * 128, (member + 1) * 128)
            row = layer * 6 + member
            for place in range(8):
                vectors[row : row + 1, place * 128 : (place + 1) * 128] = got[
                    place, 16 + 2 * layer : 17 + 2 * layer, lanes
                ].astype(f32)
        row = slice(17 + 2 * layer, 18 + 2 * layer)
        here = slice(layer, layer + 1)
        for side in range(2):
            at = side * 384
            lanes = pl.ds(pl.multiple_of((z & 1) * 128, 128), 128)
            owner = side * 2 + (z >> 1)
            in_bias[here, at : at + 128] = got[owner, row, lanes].astype(f32)
            in_bias[here, at + 128 : at + 256] = jnp.zeros((1, 128), f32)
            in_bias[here, at + 256 : at + 384] = got[owner + 4, row, lanes].astype(f32)
            unit_bias[here, side * 512 : (side + 1) * 512] = got[side * 4 + z, row, 256:768].astype(f32)


def layer_block(shape, layer):
    return pl.BlockSpec((1,) + shape, lambda i: (layer, 0, 0))


whole = pl.BlockSpec(memory_space=pltpu.VMEM)
params_one = pltpu.CompilerParams(vmem_limit_bytes=LIMIT)


def pack_first(row_block, weight, small):
    return pl.pallas_call(
        pack_first_kernel,
        grid_spec=pltpu.PrefetchScalarGridSpec(
            num_scalar_prefetch=1,
            grid=(1,),
            in_specs=[
                pl.BlockSpec((1, 16, 3072), lambda i, info: (0, info[0], 0)),
                pl.BlockSpec((16, 768), lambda i, info: (0, 0)),
            ],
            out_specs=pl.BlockSpec((8, 32, 768), lambda i, info: (0, 0, 0)),
        ),
        out_shape=jax.ShapeDtypeStruct((8, 32, 768), bf16),
        compiler_params=params_one,
        name="pack_first",
    )(row_block, weight, small)


def pack_rest(info, weight, up, down, project):
    return pl.pallas_call(
        pack_rest_kernel,
        grid=(1,),
        out_shape=(
            jax.ShapeDtypeStruct((8, 64, 1024), bf16),
            jax.ShapeDtypeStruct((8, 64, 768), bf16),
            jax.ShapeDtypeStruct((96, D), bf16),
            jax.ShapeDtypeStruct((128, D), bf16),
        ),
        in_specs=[smem, layer_block((128, 3072), 1), whole, whole, whole],
        out_specs=(whole,) * 4,
        compiler_params=params_one,
        name="pack_rest",
    )(info, weight, up, down, project)


def read_small(info, got):
    return pl.pallas_call(
        read_small_kernel,
        out_shape=(
            jax.ShapeDtypeStruct((12, D), f32),
            jax.ShapeDtypeStruct((LAYERS, 768), f32),
            jax.ShapeDtypeStruct((LAYERS, D), f32),
        ),
        in_specs=[smem, whole],
        out_specs=(whole,) * 3,
        compiler_params=params_one,
        name="read_small",
    )(info, got)


def gather_x(piece):
    return jnp.stack([piece] + [shift_x(piece, k) for k in (1, 2, 3)])


def join_columns(info, mine, other):
    return pl.pallas_call(
        join_columns_kernel,
        out_shape=jax.ShapeDtypeStruct((D, mine.shape[2]), bf16),
        in_specs=[smem, whole, whole],
        out_specs=whole,
        compiler_params=params_one,
        name="join_columns",
    )(info, mine, other)


def join_down(info, down, mine, other):
    return pl.pallas_call(
        join_down_kernel,
        grid=(1,),
        out_shape=jax.ShapeDtypeStruct((D, D), bf16),
        in_specs=[smem, layer_block((512, D), 0), whole, whole],
        out_specs=whole,
        compiler_params=params_one,
        name="join_down",
    )(info, down, mine, other)


def join_project(info, project, mine, other):
    return pl.pallas_call(
        join_project_kernel,
        out_shape=(jax.ShapeDtypeStruct((256, D), bf16),) * 2,
        in_specs=[smem, whole, whole, whole],
        out_specs=(whole,) * 2,
        compiler_params=params_one,
        name="join_project",
    )(info, project, mine, other)


def to_ctx(value):
    return lax.all_to_all(value, CTX, split_axis=0, concat_axis=0, tiled=True)


def in_order(mine, other, core):
    return jnp.where(
        core == 0,
        jnp.concatenate([mine, other], axis=1),
        jnp.concatenate([other, mine], axis=1),
    )


def columns_at(value, at, width):
    return lax.dynamic_slice_in_dim(value, at * width, width, 1)


def forward_project(normed_all, w_in, in_bias, core):
    projected = (dot(normed_all, w_in) + in_bias).astype(bf16)
    received = swap(columns_at(projected, 1 - core, 384), "core")
    return columns_at(projected, core, 384), received


def forward_attention(rows, info, slopes, core, side):
    def attention(rows):
        ctx_mine, ctx_other, logsum, kept = attend(info, slopes, *rows)
        return in_order(ctx_mine, swap(ctx_other, "core"), core), logsum, kept

    side_done, (context, logsum, kept) = beside(side[0], side[1], rows, attention)
    return context, logsum, kept, side_done


def forward_middle(hidden, context, params, given=None, work=lambda v: None):
    (project, project_bias, gain_two, offset_two) = params[4:8]
    parts, (own, done) = beside(
        dot_others(context, project, dot),
        scatter_parts,
        (context, given),
        lambda v: (dot_own(v[0], project, dot), work(v[1])),
    )
    middle = hidden + sum_parts(own, parts) + project_bias
    return middle, norm(middle, gain_two, offset_two).astype(bf16), done


def last_send(last, params):
    return dot_others(last[1], params[10], dot)


def last_own(last, params):
    return last[0] + dot_own(last[1], params[10], dot) + params[11]


def backward_two(grad_down, d_before, params, kept, core, more):
    up = params[8]
    normed_two, _, activated = kept[6:]
    sum_up = jnp.sum(d_before.astype(f32), axis=0)

    def work_two(given):
        activated, grad_down, normed_two, d_before, value = given
        own = dot_own(d_before, up, dot_t)
        g_down = outer(activated, grad_down).astype(bf16)
        g_up = outer(normed_two, d_before).astype(bf16)
        return own, (more[1](value), g_down, g_up)

    parts, (own, grads) = beside(
        dot_others(d_before, up, dot_t),
        scatter_parts,
        (activated, grad_down, normed_two, d_before, more[0]),
        work_two,
    )
    return sum_parts(own, parts), grads, sum_up


def backward(gradient, d_normed, sum_up, params, kept, info, slopes, core, across, more):
    (gain_one, _, w_in, _, project, _, gain_two) = params[:7]
    hidden, normed_all, logsum, rows, context, middle = kept[:6]
    sum_down = jnp.sum(gradient.astype(bf16).astype(f32), axis=0)

    d_values, sum_gain_two, sum_offset_two = norm_back(middle, gain_two, d_normed)
    d_middle = gradient + d_values
    grad_out = d_middle.astype(bf16)
    grad_out_all, (sum_project, crossed) = beside(
        grad_out,
        gather_z,
        (grad_out, across[0]),
        lambda v: (jnp.sum(v[0].astype(f32), axis=0), across[1](v[1])),
    )

    def attention(grad_out_all):
        d_context = dot_t(grad_out_all, project).astype(bf16)
        received = swap(columns_at(d_context, 1 - core, 128), "core")
        mine = columns_at(d_context, core, 128)
        d_mine, d_other, sums = attend_back(info, slopes, rows, mine, received, logsum)
        return in_order(d_mine, swap(d_other, "core"), core), sums

    def attention_more(grad_out_all):
        d_joined, sums = attention(grad_out_all)
        return d_joined, sums, more(held, d_joined, sums, (sum_project, sum_gain_two, sum_offset_two, sum_down, sums, sum_up))

    crossed, grad_out_all, held = lax.optimization_barrier((crossed, grad_out_all, across[4]))
    crossed, (d_joined, sums, done_more) = beside(
        across[2](crossed, context, grad_out_all), across[3], grad_out_all, attention_more
    )

    def g_input():
        return outer(normed_all, d_joined).astype(bf16)

    def scatter(work):
        parts, (own, done) = beside(
            dot_others(d_joined, w_in, dot_t),
            scatter_parts,
            d_joined,
            lambda v: (dot_own(v, w_in, dot_t), work()),
        )
        return (own, parts), done

    vectors = (sum_project, sum_gain_two, sum_offset_two, sum_down, sums, sum_up)
    def finish(given):
        own, parts = given
        d_normed_one = sum_parts(own, parts)
        d_hidden, sum_gain_one, sum_offset_one = norm_back(hidden, gain_one, d_normed_one)
        return d_middle + d_hidden, (sum_gain_one, sum_offset_one)

    return crossed, vectors, done_more, g_input, grad_out_all, scatter, finish


def take(value, at, axis=0):
    return lax.dynamic_index_in_dim(value, at, axis, keepdims=False)


def groups_first(value, shape):
    split = value.reshape(shape)
    order = (1, 0) + tuple(range(2, len(shape)))
    return split.transpose(order)


def core_sum(pack, core):
    split = pack.reshape(8, 2, 64, -1)
    keep, send = take(split, core, 1), take(split, 1 - core, 1)
    return (keep.astype(f32) + swap(send, "core").astype(f32)).astype(bf16)


def pack_outer(g_down, g_up):
    pieces = (
        groups_first(g_down, (2, 16, 32, D)).reshape(16, 64, D),
        groups_first(g_up, (8, 16, 8, D)).reshape(16, 64, D),
    )
    return jnp.concatenate(pieces, axis=-1)


def pack_inner(g_project, g_input):
    project = g_project.reshape(2, 16, 8, 4, 256).transpose(1, 0, 3, 2, 4).reshape(16, 64, 256)
    return jnp.concatenate(
        [project, groups_first(g_input, (8, 16, 8, 768)).reshape(16, 64, 768)], axis=-1
    )


def to_xy(value):
    return lax.all_to_all(value, ("x", "y_lo"), split_axis=0, concat_axis=0, tiled=True)


def sum_pairs(value, at, axis):
    return take(value, at).astype(f32) + swap(take(value, 1 - at), axis).astype(f32)


def sum_z(value, z):
    split = value.reshape(2, 4, *value.shape[1:])
    total = take(split, z, 1).astype(f32)
    for k in (1, 2, 3):
        total = total + shift_z(take(split, (z + k) % 4, 1), k).astype(f32)
    return total.astype(bf16)


def spread_z(both, z):
    columns = both.reshape(4, 8, -1)
    blocks = [take(columns, z)] + [shift_z(take(columns, (z + 4 - k) % 4), 4 - k) for k in (1, 2, 3)]
    out = []
    for four in range(4):
        at = (four + 4 - z) % 4
        low = jnp.where(at == 0, blocks[0], blocks[1])
        high = jnp.where(at == 2, blocks[2], blocks[3])
        out.append(jnp.where(at < 2, low, high))
    return jnp.concatenate(out)


def y_rows(summed, y_hi):
    return sum_pairs(summed.reshape(2, 32, -1), y_hi, "y_hi").astype(bf16)


def across_y(own, to_hi, to_lo, to_both):
    axes = ("y_lo", "y_hi")
    total = own.astype(f32)
    for value, to in ((to_hi, [1, 0, 3, 2]), (to_lo, [2, 3, 0, 1]), (to_both, [3, 2, 1, 0])):
        total = total + lax.ppermute(value, axes, list(enumerate(to))).astype(f32)
    return total


def inner_core(pack, core):
    split = pack.reshape(4, 2, 2, 64, -1)
    keep, send = take(split, core, 2), take(split, 1 - core, 2)
    return (keep.astype(f32) + swap(send, "core").astype(f32)).astype(bf16)


def inner_x(low, x):
    total = take(low, x).astype(f32)
    for k in (1, 2, 3):
        total = total + shift_x(take(low, (x + k) % 4), k).astype(f32)
    return total.astype(bf16)


def inner_y(low, y_lo, y_hi):
    split = low.reshape(2, 2, 32, -1)
    piece = lambda a, b: take(take(split, a), b)
    return across_y(
        piece(y_lo, y_hi),
        piece(y_lo, 1 - y_hi),
        piece(1 - y_lo, y_hi),
        piece(1 - y_lo, 1 - y_hi),
    ).astype(bf16)


def inner_z(both, z):
    return jnp.concatenate([both[:, :256], spread_z(both[:, 256:], z)], axis=1)


def small_z(packed, z):
    split = packed.reshape(2, 4, -1)
    total = take(split, z, 1)
    for k in (1, 2, 3):
        total = total + shift_z(take(split, (z + k) % 4, 1), k)
    return total


def small_y(total, y_hi):
    own, other = take(total, y_hi), take(total, 1 - y_hi)
    return across_y(own, other, own, other)


def small_x(total):
    return total + shift_x(total, 1) + shift_x(total, 2) + shift_x(total, 3)


def unpack_wide_kernel(second, down, up):
    for pair in range(2):
        for y_lo in range(2):
            for core in range(2):
                low = second[(pair * 2) * 4 + y_lo * 2 + core].astype(f32)
                high = second[(pair * 2 + 1) * 4 + y_lo * 2 + core].astype(f32)
                for x, block in ((pair * 2, low), (pair * 2 + 1, high)):
                    at = core * 256 + x * 64
                    down[0, at : at + 64, y_lo * 512 : (y_lo + 1) * 512] = block[:, 512:1024]
                for place in range(8):
                    lanes = slice(place * 64, (place + 1) * 64)
                    at = place * 512 + core * 256 + pair * 128
                    up[0, y_lo * 64 : (y_lo + 1) * 64, at : at + 128] = jnp.concatenate(
                        [low[:, lanes], high[:, lanes]], axis=1
                    )


def unpack_wide(second):
    return pl.pallas_call(
        unpack_wide_kernel,
        grid=(1,),
        out_shape=(
            jax.ShapeDtypeStruct((LAYERS, 512, D), f32),
            jax.ShapeDtypeStruct((LAYERS, 128, FF), f32),
        ),
        in_specs=[whole],
        out_specs=(
            pl.BlockSpec((1, 512, D), lambda i: (1, 0, 0)),
            pl.BlockSpec((1, 128, FF), lambda i: (1, 0, 0)),
        ),
        compiler_params=params_one,
        name="unpack_wide",
    )(second)


def place_input(block, layer, row, inputs):
    rows = pl.ds(row, 8)
    for four in range(4):
        part_rows = block[four * 8 : (four + 1) * 8, :].astype(f32)
        for side in range(2):
            for part in range(3):
                to = part * D + side * 512 + four * 128
                at = (side * 3 + part) * 128
                inputs[layer, rows, to : to + 128] = part_rows[:, at : at + 128]


def unpack_full_kernel(full, old_down, old_up, down, up, inputs, project):
    for g in range(2):
        rows = slice(g * 8, (g + 1) * 8)
        down[0, g * 32 : (g + 1) * 32, :] = full[g, :, 0:D].astype(f32)
        for four in range(4):
            found = full[g, four * 8 : (four + 1) * 8, D : 2 * D].astype(f32)
            for side in range(2):
                at = side * 2048 + four * 512
                up[0, rows, at : at + 512] = found[:, side * 512 : (side + 1) * 512]
        place_input(full[g, :, 3328:4096], 0, g * 8, inputs)
        place_input(full[g, :, 2560:3328], 1, g * 8, inputs)
        for layer, at in ((0, 2048), (1, 2304)):
            block = full[g, :, at : at + 256].astype(f32)
            for four in range(4):
                project[layer, rows, four * 256 : (four + 1) * 256] = block[
                    four * 8 : (four + 1) * 8, :
                ]


def unpack_full(full, down, up):
    old = pl.BlockSpec(memory_space=pl.ANY)
    return pl.pallas_call(
        unpack_full_kernel,
        grid=(8,),
        out_shape=(
            jax.ShapeDtypeStruct((LAYERS, 512, D), f32),
            jax.ShapeDtypeStruct((LAYERS, 128, FF), f32),
            jax.ShapeDtypeStruct((LAYERS, 128, 3072), f32),
            jax.ShapeDtypeStruct((LAYERS, 128, D), f32),
        ),
        in_specs=[pl.BlockSpec((2, 32, 4224), lambda i: (i, 0, 0)), old, old],
        out_specs=(
            pl.BlockSpec((1, 64, D), lambda i: (0, i, 0)),
            pl.BlockSpec((1, 16, FF), lambda i: (0, i, 0)),
            pl.BlockSpec((LAYERS, 16, 3072), lambda i: (0, i, 0)),
            pl.BlockSpec((LAYERS, 16, D), lambda i: (0, i, 0)),
        ),
        input_output_aliases={1: 0, 2: 1},
        compiler_params=pltpu.CompilerParams(vmem_limit_bytes=58 * 2**20),
        name="unpack_full",
    )(full, down, up)


def pack_tail_kernel(
    info, g_input, gain, offset, project, gain_two, offset_two, down, sums, up, second, out
):
    core, z = info[0], info[1]
    out[:, :, :, 768:896] = jnp.zeros((16, 8, 8, 128), bf16)
    for owner in range(8):
        for g in range(16):
            at = owner * 128 + g * 8
            out[g, owner, :, 0:768] = g_input[at : at + 8, :]
        for block, vector in enumerate((gain, offset, project, gain_two, offset_two, down)):
            row = vector[0:1, owner * 128 : (owner + 1) * 128]
            out[block // 2, owner, block % 2 : block % 2 + 1, 768:896] = row.astype(bf16)
        for block in range(12):
            row = second[owner : owner + 1, block * 128 : (block + 1) * 128]
            to = 12 + block
            out[to // 2, owner, to % 2 : to % 2 + 1, 768:896] = row.astype(bf16)
    place = core * 4 + z
    for part, base in ((0, 0), (2, 4)):
        for odd in range(2):
            row = sums[0:1, part * 128 : (part + 1) * 128]
            row = jnp.where(place % 2 == odd, row, 0.0).astype(bf16)
            out[3, base + (place >> 1), odd : odd + 1, 768:896] = row
    for side in range(2):
        for block in range(4):
            row = up[0:1, side * 512 + block * 128 : side * 512 + (block + 1) * 128].astype(bf16)
            out[4 + block // 2, side * 4 + z, block % 2 : block % 2 + 1, 768:896] = row


def pack_tail(info, g_input, mixed, vectors, second):
    rows = [v.reshape(1, -1) for v in mixed + vectors]
    out = pl.pallas_call(
        pack_tail_kernel,
        out_shape=jax.ShapeDtypeStruct((16, 8, 8, 896), bf16),
        in_specs=[smem] + [whole] * 10,
        out_specs=whole,
        compiler_params=params_one,
        name="pack_tail",
    )(info, g_input, *rows, second)
    return out.reshape(128, 8, 896)


def pack_small(small, place):
    (gain_one, offset_one, project, gain_two, offset_two, down, sums, up) = small
    vectors = [
        v.reshape(8, 128) for v in (gain_one, offset_one, project, gain_two, offset_two, down)
    ]
    sums = sums.reshape(-1)
    inputs = lax.dynamic_update_slice_in_dim(jnp.zeros((2 * D,), f32), sums[:128], place * 128, 0)
    inputs = lax.dynamic_update_slice_in_dim(inputs, sums[256:], D + place * 128, 0)
    return jnp.concatenate(vectors + [inputs.reshape(8, 256), up], axis=1)


def on_device(
    inputs,
    cotangent,
    segments,
    norm_one_gain,
    norm_one_bias,
    input_weight,
    input_bias,
    project_weight,
    project_bias,
    norm_two_gain,
    norm_two_bias,
    up_weight,
    up_bias,
    down_weight,
    down_bias,
):
    y_hi, z = lax.axis_index("y_hi"), lax.axis_index("z")
    x, y_lo, core = lax.axis_index("x"), lax.axis_index("y_lo"), lax.axis_index("core")
    place = core * 4 + z
    rows_in = regroup(inputs[0], core, y_hi)
    cut = jnp.sum((segments[0] < 2).astype(jnp.int32))
    cut = regroup(jnp.broadcast_to(cut, (1, 128)), core, y_hi)[0, 0]
    info = jnp.stack([core, z, cut, y_hi]).astype(jnp.int32)
    corner = jnp.stack([core, z, y_hi, core * 4 + x, x, y_lo]).astype(jnp.int32)
    heads = (place * 2 + jnp.arange(2, dtype=jnp.int32)).astype(f32)
    slopes = jnp.exp2(-8.0 * (heads + 1.0) / HEADS)

    small = jnp.concatenate(
        [
            norm_one_gain,
            norm_one_bias,
            project_bias,
            norm_two_gain,
            norm_two_bias,
            down_bias,
            input_bias,
            up_bias,
        ],
        axis=1,
    )
    small = jnp.concatenate([small.reshape(4, 768), jnp.zeros((12, 768), bf16)], axis=0)
    first = pack_first(corner[3:4], input_weight, small)
    (raw_all, first), (up_zero, second, rows, wide) = beside(
        (rows_in, first),
        lambda v: (gather_z(v[0]), to_ctx(v[1])),
        corner,
        lambda v: pack_rest(v, input_weight, up_weight, down_weight, project_weight),
    )

    def first_norm(given):
        first, raw_all = given
        vectors, in_bias, unit_bias = read_small(corner, first)
        unit = norm_parts(raw_all.astype(f32))[0]
        normed_all = (unit * vectors[0] + vectors[1]).astype(bf16)
        return vectors, in_bias, unit_bias, normed_all, unit.astype(bf16)

    def first_weight(given):
        first, raw_all, rows = given
        (w_first, rows), parts = beside(
            (first[:, 0:16].reshape(128, 768), rows),
            lambda v: (gather_x(v[0]), swap(v[1], "y_hi")),
            (first, raw_all),
            first_norm,
        )
        w_first = join_columns(corner, w_first, swap(w_first, "core"))
        return w_first, rows, parts, forward_project(parts[3], w_first, parts[1][0], core)

    up_zero, (w_first, rows, first_parts, projected) = beside(
        up_zero, to_ctx, (first, raw_all, rows), first_weight
    )
    vectors, in_bias, unit_bias, normed_all, unit_all = first_parts
    wide = lax.all_gather(wide, CTX, axis=0, tiled=True)
    vector = [vectors[i] for i in range(12)]
    nothing = (jnp.zeros((8, 128), f32), lambda v: v, lambda v, *more: v, lambda v: v, None)
    unit_wide = first[:, 19:20, 256:768].reshape(8, 2, 4, 64)
    unit_wide = lax.dynamic_index_in_dim(unit_wide, core, 1, keepdims=False)
    unit_wide = unit_wide.transpose(1, 0, 2).reshape(4, 1, 512).astype(f32)
    hidden = rows_in.astype(f32)
    context, logsum, rows_kept, (pieces, second) = forward_attention(
        projected, info, slopes, core, ((rows, second), lambda v: (gather_x(v[0]), to_ctx(v[1])))
    )
    other = swap(pieces, "core")
    project_zero, project_one = join_project(corner, project_weight, pieces, other)
    context, wide = lax.optimization_barrier((context, wide))
    params_0 = (
        vector[0],
        vector[1],
        w_first,
        in_bias[0],
        project_zero,
        vector[2],
        vector[3],
        vector[4],
    )

    def fetch_other(halves, width):
        return join_halves(corner, halves, swap(halves, "core"), (width,))[0]

    middle, normed, up_zero = forward_middle(
        hidden, context, params_0, up_zero, lambda v: fetch_other(v, D)
    )
    wide = lax.all_gather(after(wide, normed), "x")
    normed_two, (w_second, down_zero) = beside(
        normed,
        gather_z,
        (second, pieces, other),
        lambda v: (fetch_other(v[0], 768), join_down(corner, down_weight, v[1], v[2])),
    )
    params_0 = params_0 + (up_zero, unit_bias[0], down_zero, vector[5])
    before = dot(normed_two, up_zero) + unit_bias[0]
    activated = gelu(before).astype(bf16)
    last = (middle, activated)
    kept_0 = (hidden, normed_all, logsum, rows_kept, context, middle, normed_two, before, activated)
    parts, hidden = beside(
        last_send(last, params_0), scatter_parts, last, lambda v: last_own(v, params_0)
    )
    hidden = sum_parts(hidden, parts)
    normed_all = gather_z(norm(hidden, vector[6], vector[7]).astype(bf16))
    params_1 = (
        vector[6],
        vector[7],
        w_second,
        in_bias[1],
        project_one,
        vector[8],
        vector[9],
        vector[10],
    )
    gradient = regroup(cotangent[0], core, y_hi)
    context, logsum, rows_kept, grad_other = forward_attention(
        forward_project(normed_all, w_second, in_bias[1], core),
        info,
        slopes,
        core,
        (gradient, lambda v: swap(v, "core")),
    )
    middle, normed_two, _ = forward_middle(hidden, context, params_1)
    own, other, d_own, d_other, sum_up, wide_grads = wide_part(
        normed_two, swap(normed_two, "core"), gradient, grad_other, wide, unit_wide
    )
    d_normed = d_own + swap(d_other, "core").astype(f32)
    output = middle + (own + swap(other, "core").astype(f32)) + vector[11]
    kept_1 = (hidden, normed_all, logsum, rows_kept, context, middle)
    wide_grads = lax.psum_scatter(wide_grads, "x", scatter_dimension=0, tiled=True)[0]
    units = lax.dynamic_update_slice_in_dim(
        jnp.zeros((8, 2, 4, 64), f32), sum_up.reshape(4, 8, 64).transpose(1, 0, 2)[:, None], core, 1
    )
    gradient = gradient.astype(f32)

    _, vectors_1, _, g_input, grad_out_all, scatter, finish = backward(
        gradient,
        d_normed,
        units.reshape(8, 512),
        params_1,
        kept_1,
        info,
        slopes,
        core,
        nothing,
        lambda *given: None,
    )
    left, inner_1 = scatter(
        lambda: pack_inner(outer(context, grad_out_all).astype(bf16), g_input())
    )
    gradient, norm_sums = finish(left)
    packed_1 = pack_small(norm_sums + vectors_1, place)
    grad_down, wide_grads = beside(
        gradient.astype(bf16),
        gather_z,
        wide_grads,
        lambda v: sum_pairs(v, y_lo, "y_lo").astype(bf16),
    )
    inner_1, wide_grads = lax.optimization_barrier((inner_1, wide_grads))
    inner_1 = lax.psum_scatter(inner_1, GRP, scatter_dimension=0, tiled=True)[0]
    wide_grads, d_before = beside(
        wide_grads,
        lambda v: sum_z(v, z),
        (grad_down, kept_0[7]),
        lambda v: jax.vjp(gelu, v[1])[1](dot_t(v[0], params_0[10]))[0].astype(bf16),
    )
    d_normed, (wide_grads, *grads), sum_up = backward_two(
        grad_down,
        d_before,
        params_0,
        kept_0,
        core,
        (wide_grads, lambda v: sum_pairs(v, y_hi, "y_hi").astype(bf16)),
    )
    wide_grads = lax.all_gather(wide_grads, GRP)

    def with_project(summed, context, grad_out_all):
        g_project = outer(context, grad_out_all).astype(bf16)
        rows = g_project.reshape(2, 16, 8, 4, 256).transpose(1, 0, 3, 2, 4).reshape(16, 64, 256)
        return jnp.concatenate([summed, core_sum(rows, core)], axis=-1)

    def tail_pack(inner_sum, d_joined, sums, vectors):
        w_in = params_0[2].astype(f32)
        gain = jnp.sum(outer(unit_all, d_joined) * w_in, axis=1)
        offset = jnp.sum(d_joined.astype(f32), axis=0, keepdims=True)
        offset = jnp.sum(offset * w_in, axis=1)
        g_input = outer(kept_0[1], d_joined).astype(bf16)
        packed = pack_tail(info, g_input, (gain, offset), vectors, packed_1)
        return packed, inner_sum

    crossed, _, (low, inner_1), _, _, scatter, finish = backward(
        gradient,
        d_normed,
        sum_up,
        params_0,
        kept_0,
        info,
        slopes,
        core,
        (grads, lambda v: core_sum(pack_outer(*v), core), with_project, to_xy, inner_1),
        tail_pack,
    )

    def to_all(value):
        return lax.all_to_all(value, GRP + CTX, split_axis=0, concat_axis=0, tiled=True)

    def outer_rows(given):
        crossed, inner_1 = given
        both = jnp.sum(crossed.astype(f32), axis=0).astype(bf16)
        both = y_rows(jnp.concatenate([both, inner_1], axis=1), y_hi)
        at = 2 * D + 512
        spread = spread_z(jnp.concatenate([both[:, D : 2 * D], both[:, at:]], axis=1), z)
        return [both[:, :D], spread[:, :D], both[:, 2 * D : at], spread[:, D:]]

    low, both = beside(low, to_all, (crossed, inner_1), outer_rows)
    low, wide_grads = lax.optimization_barrier((low, wide_grads))
    left, _ = scatter(lambda: None)
    gradient = regroup(finish(left)[0], core, y_hi)
    low = low.reshape(32, 32, 896).astype(f32)
    vector = jnp.sum(low[:, :, 768:].reshape(128, 8, 128), axis=0)
    vector = jnp.pad(vector, ((0, 24), (0, 0)))
    low = jnp.sum(low[:, :, :768], axis=0)
    low = jnp.concatenate([low, vector], axis=1).astype(bf16)
    full = lax.all_gather(jnp.concatenate(both + [low], axis=1), GRP)
    vector = full[0:12, 0:2, 4096:4224].astype(f32)
    g_down, g_up, g_input, g_project = unpack_full(full, *unpack_wide(wide_grads))
    packed = vector.reshape(LAYERS * 1536)
    vector = packed.reshape(LAYERS, -1)
    parts = [vector[:, i * 128 : (i + 1) * 128] for i in range(6)]
    return (
        regroup(output, core, y_hi)[None],
        gradient[None],
        parts[0],
        parts[1],
        g_input,
        vector[:, 768:1024],
        g_project,
        parts[2],
        parts[3],
        parts[4],
        g_up,
        vector[:, 1024:1536],
        g_down,
        parts[5],
    )


def solution(mesh):
    split = Mesh(mesh.devices.reshape(4, 2, 2, 2, 4), GRP + CTX)
    rows = P(GRP, CTX, None)
    vector = P(None, CTX)
    matrix = P(None, CTX, None)
    weights = (
        vector,
        vector,
        matrix,
        vector,
        matrix,
        vector,
        vector,
        vector,
        matrix,
        vector,
        matrix,
        vector,
    )
    return jax.shard_map(
        on_device,
        mesh=split,
        in_specs=(rows, rows, P(GRP, None)) + weights,
        out_specs=(rows, rows) + weights,
        check_vma=False,
    )
```

```python
import math

import jax
import jax.numpy as jnp
from jax import lax
from jax.experimental import pallas as pl
from jax.experimental.pallas import tpu as pltpu
from jax.sharding import Mesh
from jax.sharding import PartitionSpec as P

D = 1024
HEADS = 16
HEAD_DIM = 64
FF = 4096
PROMPT = 1024
TOKENS = 1536
PIECE = 192
LAYERS = 2
TILE = 256
HALF = 4 * PIECE
SCALE = HEAD_DIM ** (-0.5)
masked_value = -1e30

GRP = ("x", "y_lo", "core")
CTX = ("y_hi", "z")
bf16 = jnp.bfloat16
f32 = jnp.float32


def shift_z(value, step):
    return lax.ppermute(value, "z", [(i, (i + step) % 4) for i in range(4)])


def shift_x(value, step):
    return lax.ppermute(value, "x", [(i, (i + step) % 4) for i in range(4)])


def swap(value, axis):
    return lax.ppermute(value, axis, [(0, 1), (1, 0)])


def regroup(value, core, y_hi):
    got = lax.ppermute(value, ("core", "y_hi"), [(1, 2), (2, 1)])
    return jnp.where(core == y_hi, value, got)


def after(value, *others):
    return lax.optimization_barrier((value, others))[0]


def beside(send, transfer, given, work):
    send, given = lax.optimization_barrier((send, given))
    return lax.optimization_barrier((transfer(send), work(given)))


def gather_z(rows):
    half = rows.shape[0] // 2
    first, second = rows[:half], rows[half:]
    first_left, second_right = shift_z(first, 1), shift_z(second, 3)
    second_left, first_right = shift_z(second, 1), shift_z(first, 3)
    first_left, second_right = lax.optimization_barrier((first_left, second_right))
    first_far, second_far = shift_z(first_left, 1), shift_z(second_right, 3)
    return jnp.concatenate(
        [rows, first_left, second_left, first_far, second_far, first_right, second_right], axis=0
    )


def dot(left, right):
    return jnp.dot(left, right, preferred_element_type=f32)


def dot_t(left, right):
    return lax.dot_general(left, right, (((1,), (1,)), ((), ())), preferred_element_type=f32)


def outer(left, right):
    return lax.dot_general(left, right, (((0,), (0,)), ((), ())), preferred_element_type=f32)


def scatter_parts(others):
    return tuple(
        shift_z(others[(k - 1) * PIECE : k * PIECE], -k) for k in (1, 2, 3)
    )


def sum_parts(own, parts):
    total = own
    for part in parts:
        total = total + part.astype(f32)
    return total


def dot_others(left, weight, product):
    return product(left[PIECE:], weight).astype(bf16)


def dot_own(left, weight, product):
    return product(left[:PIECE], weight)


def tile_mask(block, low, high, cut):
    keys = lax.broadcasted_iota(jnp.int32, (high - low, TILE), 0) + low
    queries = lax.broadcasted_iota(jnp.int32, (high - low, TILE), 1) + block * TILE
    visible = keys <= queries
    if block * TILE >= PROMPT:
        visible = visible & ((keys >= cut) | (queries < cut))
    return visible


def fill_bias(bias, slopes, cut):
    keys = lax.broadcasted_iota(jnp.int32, (TOKENS, 128), 0)
    places = jnp.where(keys >= cut, keys - cut + PROMPT, keys).astype(f32)
    for h in range(2):
        bias[h] = places * slopes[h]


def scores_t(keys, queries, bias, block, high, cut):
    low = min(block * TILE, PROMPT)
    scores = dot_t(keys, queries)
    scores = scores + jnp.concatenate([bias[0:high], bias[0:high]], axis=1)
    tail = jnp.where(tile_mask(block, low, high, cut), scores[low:high], masked_value)
    if low == 0:
        return tail
    return jnp.concatenate([scores[:low], tail], axis=0)


def piece_places(info):
    core, z = info[0], info[1]
    out = []
    for side in range(2):
        half = core if side == 0 else 1 - core
        for k in range(4):
            out.append(pl.multiple_of((half * 4 + ((z - k) & 3)) * PIECE, 64))
    return out


def attend_kernel(info, slopes, mine, other, ctx_mine, ctx_other, logsum, rows, ctx, vt, bias):
    spots = piece_places(info)
    cut = info[2]
    for k in range(4):
        span = slice(k * PIECE, (k + 1) * PIECE)
        rows[pl.ds(spots[k], PIECE), :] = mine[span, :]
        rows[pl.ds(spots[4 + k], PIECE), :] = other[span, :]
    fill_bias(bias, slopes, cut)
    vt[...] = rows[:, 256:384].astype(f32).T.astype(bf16)
    for block in range(TOKENS // TILE):
        high = (block + 1) * TILE
        span = slice(block * TILE, high)
        parts = []
        for h in range(2):
            lanes = slice(h * HEAD_DIM, (h + 1) * HEAD_DIM)
            key_lanes = slice(128 + h * HEAD_DIM, 128 + (h + 1) * HEAD_DIM)
            queries = rows[span, lanes] * jnp.asarray(SCALE, bf16)
            scores = scores_t(rows[0:high, key_lanes], queries, bias[h], block, high, cut)
            top = jnp.max(scores, axis=0, keepdims=True)
            weights = jnp.exp(scores - top)
            total = jnp.sum(weights, axis=0, keepdims=True)
            found = dot(vt[lanes, 0:high], weights.astype(bf16))
            parts.append(found * (1.0 / total))
            logsum[h : h + 1, span] = top + jnp.log(total)
        ctx[span, :] = jnp.concatenate(parts, axis=0).T.astype(bf16)
    for k in range(4):
        span = slice(k * PIECE, (k + 1) * PIECE)
        ctx_mine[span, :] = ctx[pl.ds(spots[k], PIECE), :]
        ctx_other[span, :] = ctx[pl.ds(spots[4 + k], PIECE), :]


def attend_back_kernel(
    info, slopes, rows, mine, other, logsum, out_mine, out_other, sums, grad, kt, bias, dq, dk, dv, out
):
    spots = piece_places(info)
    cut = info[2]
    for k in range(4):
        span = slice(k * PIECE, (k + 1) * PIECE)
        grad[pl.ds(spots[k], PIECE), :] = mine[span, :]
        grad[pl.ds(spots[4 + k], PIECE), :] = other[span, :]
    fill_bias(bias, slopes, cut)
    kt[...] = rows[:, 128:256].astype(f32).T.astype(bf16)
    dk[...] = jnp.zeros_like(dk)
    dv[...] = jnp.zeros_like(dv)
    for block in range(TOKENS // TILE):
        high = (block + 1) * TILE
        span = slice(block * TILE, high)
        parts = []
        for h in range(2):
            lanes = slice(h * HEAD_DIM, (h + 1) * HEAD_DIM)
            key_lanes = slice(128 + h * HEAD_DIM, 128 + (h + 1) * HEAD_DIM)
            value_lanes = slice(256 + h * HEAD_DIM, 256 + (h + 1) * HEAD_DIM)
            queries = rows[span, lanes] * jnp.asarray(SCALE, bf16)
            grads = grad[span, lanes]
            scores = scores_t(rows[0:high, key_lanes], queries, bias[h], block, high, cut)
            weights = jnp.exp(scores - logsum[h : h + 1, span])
            d_weights = dot_t(rows[0:high, value_lanes], grads)
            correction = jnp.sum(weights * d_weights, axis=0, keepdims=True)
            d_scores = (weights * (d_weights - correction)).astype(bf16)
            dv[h, 0:high, :] += dot(weights.astype(bf16), grads)
            dk[h, 0:high, :] += dot(d_scores, queries)
            parts.append(dot(kt[lanes, 0:high], d_scores))
        dq[span, :] = (jnp.concatenate(parts, axis=0) * SCALE).T
    out[:, 0:128] = dq[...].astype(bf16)
    out[:, 128:256] = jnp.concatenate([dk[0], dk[1]], axis=1).astype(bf16)
    out[:, 256:384] = jnp.concatenate([dv[0], dv[1]], axis=1).astype(bf16)
    sums[...] = jnp.sum(out[...].astype(f32), axis=0, keepdims=True)
    for k in range(4):
        span = slice(k * PIECE, (k + 1) * PIECE)
        out_mine[span, :] = out[pl.ds(spots[k], PIECE), :]
        out_other[span, :] = out[pl.ds(spots[4 + k], PIECE), :]


smem = pl.BlockSpec(memory_space=pltpu.SMEM)
vmem = pl.BlockSpec(memory_space=pltpu.VMEM)
LIMIT = 40 * 2**20


def attend(info, slopes, mine, other):
    return pl.pallas_call(
        attend_kernel,
        out_shape=(
            jax.ShapeDtypeStruct((HALF, 128), bf16),
            jax.ShapeDtypeStruct((HALF, 128), bf16),
            jax.ShapeDtypeStruct((2, TOKENS), f32),
            jax.ShapeDtypeStruct((TOKENS, 384), bf16),
        ),
        in_specs=[smem, smem, vmem, vmem],
        out_specs=(vmem, vmem, vmem, vmem),
        scratch_shapes=[
            pltpu.VMEM((TOKENS, 128), bf16),
            pltpu.VMEM((128, TOKENS), bf16),
            pltpu.VMEM((2, TOKENS, 128), f32),
        ],
        compiler_params=pltpu.CompilerParams(vmem_limit_bytes=LIMIT),
        cost_estimate=pl.CostEstimate(
            flops=1000000, bytes_accessed=36000000, transcendentals=0
        ),
        name="attend",
    )(info, slopes, mine, other)


def attend_back(info, slopes, rows, mine, other, logsum):
    return pl.pallas_call(
        attend_back_kernel,
        out_shape=(
            jax.ShapeDtypeStruct((HALF, 384), bf16),
            jax.ShapeDtypeStruct((HALF, 384), bf16),
            jax.ShapeDtypeStruct((1, 384), f32),
        ),
        in_specs=[smem, smem, vmem, vmem, vmem, vmem],
        out_specs=(vmem, vmem, vmem),
        scratch_shapes=[
            pltpu.VMEM((TOKENS, 128), bf16),
            pltpu.VMEM((128, TOKENS), bf16),
            pltpu.VMEM((2, TOKENS, 128), f32),
            pltpu.VMEM((TOKENS, 128), f32),
            pltpu.VMEM((2, TOKENS, HEAD_DIM), f32),
            pltpu.VMEM((2, TOKENS, HEAD_DIM), f32),
            pltpu.VMEM((TOKENS, 384), bf16),
        ],
        compiler_params=pltpu.CompilerParams(vmem_limit_bytes=LIMIT),
        cost_estimate=pl.CostEstimate(
            flops=1000000, bytes_accessed=48000000, transcendentals=0
        ),
        name="attend_back",
    )(info, slopes, rows, mine, other, logsum)


def norm_parts(values):
    average = jnp.mean(values, axis=-1, keepdims=True)
    centered = values - average
    variance = jnp.mean(centered * centered, axis=-1, keepdims=True)
    scale = lax.rsqrt(variance + 1e-05)
    return centered * scale, scale


def norm(values, gain, offset):
    return norm_parts(values)[0] * gain + offset


def norm_back(values, gain, grads):
    unit, scale = norm_parts(values)
    weighted = grads * gain
    mean_one = jnp.mean(weighted, axis=-1, keepdims=True)
    mean_two = jnp.mean(weighted * unit, axis=-1, keepdims=True)
    d_values = scale * (weighted - mean_one - unit * mean_two)
    return d_values, jnp.sum(grads * unit, axis=0), jnp.sum(grads, axis=0)


def gelu(values):
    return jax.nn.gelu(values, approximate=True)


PAIR = 2 * PIECE


def wide_down(weight, down):
    for place in range(8):
        for side in range(2):
            at = place * 128 + side * 64
            down[place * 64 : (place + 1) * 64, side * 512 : (side + 1) * 512] = weight[
                0, at : at + 64, 512:1024
            ]


def gelu_parts(u):
    k = math.sqrt(2.0 / math.pi)
    square = u * u
    t = jnp.tanh(k * u * (1.0 + 0.044715 * square))
    half = 0.5 * (1.0 + t)
    slope = half + 0.5 * u * (1.0 - t * t) * (k * (1.0 + 3.0 * 0.044715 * square))
    return u * half, slope


def wide_kernel(
    rows_own, rows_other, grads_own, grads_other, weight, bias,
    out_own, out_other, d_own, d_other, sums, pack,
    rows, grads, down, total, d_total,
):
    step = pl.program_id(0)

    @pl.when(step == 0)
    def _():
        rows[0:PIECE, :] = rows_own[...]
        rows[PIECE:PAIR, :] = rows_other[...]
        grads[0:PIECE, :] = grads_own[...]
        grads[PIECE:PAIR, :] = grads_other[...]

    wide_down(weight, down)
    up = weight[0, :, 0:512]
    activated, slope = gelu_parts(dot(rows[...], up) + bias[0])
    activated = activated.astype(bf16)
    d_before = (dot_t(grads[...], down[...]) * slope).astype(bf16)
    sums[0] = jnp.sum(d_before.astype(f32), axis=0, keepdims=True)
    part = dot(activated, down[...])
    d_part = dot_t(d_before, up)
    g_up = outer(rows[...], d_before).astype(bf16)
    g_down = outer(activated, grads[...]).astype(bf16)
    for place in range(8):
        for side in range(2):
            at = place * 128 + side * 64
            pack[0, side, place, :, 0:512] = g_up[at : at + 64, :]
            pack[0, side, place, :, 512:1024] = g_down[
                place * 64 : (place + 1) * 64, side * 512 : (side + 1) * 512
            ]

    @pl.when(step == 0)
    def _():
        total[...] = part
        d_total[...] = d_part

    @pl.when(step > 0)
    def _():
        total[...] += part
        d_total[...] += d_part

    @pl.when(step == 3)
    def _():
        out_own[...] = total[0:PIECE, :]
        out_other[...] = total[PIECE:PAIR, :].astype(bf16)
        d_own[...] = d_total[0:PIECE, :]
        d_other[...] = d_total[PIECE:PAIR, :].astype(bf16)


def wide_part(rows_own, rows_other, grads_own, grads_other, weight, bias):
    fixed = pl.BlockSpec((PIECE, D), lambda i: (0, 0))
    each = lambda *shape: pl.BlockSpec((1,) + shape, lambda i: (i,) + (0,) * len(shape))
    return pl.pallas_call(
        wide_kernel,
        grid=(4,),
        out_shape=(
            jax.ShapeDtypeStruct((PIECE, D), f32),
            jax.ShapeDtypeStruct((PIECE, D), bf16),
            jax.ShapeDtypeStruct((PIECE, D), f32),
            jax.ShapeDtypeStruct((PIECE, D), bf16),
            jax.ShapeDtypeStruct((4, 1, 512), f32),
            jax.ShapeDtypeStruct((4, 2, 8, 64, D), bf16),
        ),
        in_specs=[fixed] * 4 + [each(D, D), each(1, 512)],
        out_specs=(fixed,) * 4 + (each(1, 512), each(2, 8, 64, D)),
        scratch_shapes=[
            pltpu.VMEM((PAIR, D), bf16),
            pltpu.VMEM((PAIR, D), bf16),
            pltpu.VMEM((512, D), bf16),
            pltpu.VMEM((PAIR, D), f32),
            pltpu.VMEM((PAIR, D), f32),
        ],
        compiler_params=pltpu.CompilerParams(vmem_limit_bytes=58 * 2**20),
        cost_estimate=pl.CostEstimate(
            flops=14 * PAIR * 2048 * D, bytes_accessed=50000000, transcendentals=0
        ),
        name="wide_part",
    )(rows_own, rows_other, grads_own, grads_other, weight, bias)


QUARTER = 16


def pack_first_kernel(info, weight, small, out):
    for place in range(8):
        for side in range(2):
            for part in range(3):
                at = part * D + side * 512 + (place % 4) * 128
                to = (side * 3 + part) * 128
                out[place, 0:16, to : to + 128] = weight[0, :, at : at + 128]
        out[place, 16:32, :] = small[...]


def pack_rest_kernel(info, weight, up, down, project, first, second, rows, wide):
    core, x = info[0], info[4]
    half = pl.ds(pl.multiple_of(core * 64, 64), 64)
    for place in range(8):
        for side in range(2):
            at = side * 2048 + (place % 4) * 512
            to = side * 512
            first[place, :, to : to + 512] = up[0, half, at : at + 512]
            for part in range(3):
                at = part * D + side * 512 + (place % 4) * 128
                to = (side * 3 + part) * 128
                second[place, :, to : to + 128] = weight[0, half, at : at + 128]
    at_row = pl.ds(pl.multiple_of(core * 64 + x * 16, 16), 16)
    long = pl.ds(pl.multiple_of(core * 256 + x * 64, 64), 64)
    rows[0:64, :] = down[0, long, :]
    rows[64:80, :] = project[0, at_row, :]
    rows[80:96, :] = project[1, at_row, :]
    wide[0:64, 512:1024] = down[1, long, 0:512]
    wide[64:128, 512:1024] = down[1, long, 512:1024]
    for place in range(8):
        pair = pl.ds(pl.multiple_of(place * 512 + core * 256 + (x >> 1) * 128, 128), 128)
        found = up[1, :, pair].astype(f32)
        found = jnp.where(x % 2 == 0, found[:, 0:64], found[:, 64:128])
        wide[:, place * 64 : (place + 1) * 64] = found.astype(bf16)


def join_halves_kernel(info, mine, other, *outs):
    core = info[0]
    for pieces, half in ((mine, core), (other, 1 - core)):
        for place in range(8):
            at = pl.ds(pl.multiple_of(place * 128 + half * 64, 64), 64)
            column = 0
            for out in outs:
                width = out.shape[1]
                out[at, :] = pieces[place, :, column : column + width]
                column += width


def join_halves(info, mine, other, widths):
    return pl.pallas_call(
        join_halves_kernel,
        out_shape=tuple(jax.ShapeDtypeStruct((D, width), bf16) for width in widths),
        in_specs=[smem, whole, whole],
        out_specs=(whole,) * len(widths),
        compiler_params=params_one,
        name="join_halves",
    )(info, mine, other)


def join_columns_kernel(info, mine, other, out):
    core, x = info[0], info[4]
    for pieces, half in ((mine, core), (other, 1 - core)):
        for k in range(4):
            for place in range(8):
                at = place * 128 + half * 64 + ((x - k) & 3) * 16
                out[pl.ds(pl.multiple_of(at, 16), 16), :] = pieces[k, place * 16 : (place + 1) * 16, :]


def join_down_kernel(info, down, mine, other, down_out):
    core, x, y_hi = info[0], info[4], info[2]
    down_out[pl.ds(pl.multiple_of(y_hi * 512, 64), 512), :] = down[0]
    for pieces, half in ((mine, core), (other, 1 - core)):
        for k in range(4):
            at = (1 - y_hi) * 512 + half * 256 + ((x - k) & 3) * 64
            down_out[pl.ds(pl.multiple_of(at, 64), 64), :] = pieces[k, 0:64, :]


def join_project_kernel(info, project, mine, other, first, second):
    core, x, y_hi = info[0], info[4], info[2]
    own = pl.ds(pl.multiple_of(y_hi * 128, 64), 128)
    first[own, :] = project[0]
    second[own, :] = project[1]
    for pieces, half in ((mine, core), (other, 1 - core)):
        for k in range(4):
            at = (1 - y_hi) * 128 + half * 64 + ((x - k) & 3) * 16
            at = pl.ds(pl.multiple_of(at, 16), 16)
            first[at, :] = pieces[k, 64:80, :]
            second[at, :] = pieces[k, 80:96, :]


def read_small_kernel(info, got, vectors, in_bias, unit_bias):
    z = info[1]
    for layer in range(LAYERS):
        for member in range(6):
            lanes = slice(member * 128, (member + 1) * 128)
            row = layer * 6 + member
            for place in range(8):
                vectors[row : row + 1, place * 128 : (place + 1) * 128] = got[
                    place, 16 + 2 * layer : 17 + 2 * layer, lanes
                ].astype(f32)
        row = slice(17 + 2 * layer, 18 + 2 * layer)
        here = slice(layer, layer + 1)
        for side in range(2):
            at = side * 384
            lanes = pl.ds(pl.multiple_of((z & 1) * 128, 128), 128)
            owner = side * 2 + (z >> 1)
            in_bias[here, at : at + 128] = got[owner, row, lanes].astype(f32)
            in_bias[here, at + 128 : at + 256] = jnp.zeros((1, 128), f32)
            in_bias[here, at + 256 : at + 384] = got[owner + 4, row, lanes].astype(f32)
            unit_bias[here, side * 512 : (side + 1) * 512] = got[side * 4 + z, row, 256:768].astype(f32)


def layer_block(shape, layer):
    return pl.BlockSpec((1,) + shape, lambda i: (layer, 0, 0))


whole = pl.BlockSpec(memory_space=pltpu.VMEM)
params_one = pltpu.CompilerParams(vmem_limit_bytes=LIMIT)


def pack_first(row_block, weight, small):
    return pl.pallas_call(
        pack_first_kernel,
        grid_spec=pltpu.PrefetchScalarGridSpec(
            num_scalar_prefetch=1,
            grid=(1,),
            in_specs=[
                pl.BlockSpec((1, 16, 3072), lambda i, info: (0, info[0], 0)),
                pl.BlockSpec((16, 768), lambda i, info: (0, 0)),
            ],
            out_specs=pl.BlockSpec((8, 32, 768), lambda i, info: (0, 0, 0)),
        ),
        out_shape=jax.ShapeDtypeStruct((8, 32, 768), bf16),
        compiler_params=params_one,
        name="pack_first",
    )(row_block, weight, small)


def pack_rest(info, weight, up, down, project):
    return pl.pallas_call(
        pack_rest_kernel,
        grid=(1,),
        out_shape=(
            jax.ShapeDtypeStruct((8, 64, 1024), bf16),
            jax.ShapeDtypeStruct((8, 64, 768), bf16),
            jax.ShapeDtypeStruct((96, D), bf16),
            jax.ShapeDtypeStruct((128, D), bf16),
        ),
        in_specs=[smem, layer_block((128, 3072), 1), whole, whole, whole],
        out_specs=(whole,) * 4,
        compiler_params=params_one,
        name="pack_rest",
    )(info, weight, up, down, project)


def read_small(info, got):
    return pl.pallas_call(
        read_small_kernel,
        out_shape=(
            jax.ShapeDtypeStruct((12, D), f32),
            jax.ShapeDtypeStruct((LAYERS, 768), f32),
            jax.ShapeDtypeStruct((LAYERS, D), f32),
        ),
        in_specs=[smem, whole],
        out_specs=(whole,) * 3,
        compiler_params=params_one,
        name="read_small",
    )(info, got)


def gather_x(piece):
    return jnp.stack([piece] + [shift_x(piece, k) for k in (1, 2, 3)])


def join_columns(info, mine, other):
    return pl.pallas_call(
        join_columns_kernel,
        out_shape=jax.ShapeDtypeStruct((D, mine.shape[2]), bf16),
        in_specs=[smem, whole, whole],
        out_specs=whole,
        compiler_params=params_one,
        name="join_columns",
    )(info, mine, other)


def join_down(info, down, mine, other):
    return pl.pallas_call(
        join_down_kernel,
        grid=(1,),
        out_shape=jax.ShapeDtypeStruct((D, D), bf16),
        in_specs=[smem, layer_block((512, D), 0), whole, whole],
        out_specs=whole,
        compiler_params=params_one,
        name="join_down",
    )(info, down, mine, other)


def join_project(info, project, mine, other):
    return pl.pallas_call(
        join_project_kernel,
        out_shape=(jax.ShapeDtypeStruct((256, D), bf16),) * 2,
        in_specs=[smem, whole, whole, whole],
        out_specs=(whole,) * 2,
        compiler_params=params_one,
        name="join_project",
    )(info, project, mine, other)


def to_ctx(value):
    return lax.all_to_all(value, CTX, split_axis=0, concat_axis=0, tiled=True)


def in_order(mine, other, core):
    return jnp.where(
        core == 0,
        jnp.concatenate([mine, other], axis=1),
        jnp.concatenate([other, mine], axis=1),
    )


def columns_at(value, at, width):
    return lax.dynamic_slice_in_dim(value, at * width, width, 1)


def forward_project(normed_all, w_in, in_bias, core):
    projected = (dot(normed_all, w_in) + in_bias).astype(bf16)
    received = swap(columns_at(projected, 1 - core, 384), "core")
    return columns_at(projected, core, 384), received


def forward_attention(rows, info, slopes, core, side):
    def attention(rows):
        ctx_mine, ctx_other, logsum, kept = attend(info, slopes, *rows)
        return in_order(ctx_mine, swap(ctx_other, "core"), core), logsum, kept

    side_done, (context, logsum, kept) = beside(side[0], side[1], rows, attention)
    return context, logsum, kept, side_done


def forward_middle(hidden, context, params, given=None, work=lambda v: None):
    (project, project_bias, gain_two, offset_two) = params[4:8]
    parts, (own, done) = beside(
        dot_others(context, project, dot),
        scatter_parts,
        (context, given),
        lambda v: (dot_own(v[0], project, dot), work(v[1])),
    )
    middle = hidden + sum_parts(own, parts) + project_bias
    return middle, norm(middle, gain_two, offset_two).astype(bf16), done


def last_send(last, params):
    return dot_others(last[1], params[10], dot)


def last_own(last, params):
    return last[0] + dot_own(last[1], params[10], dot) + params[11]


def backward_two(grad_down, d_before, params, kept, core, more):
    up = params[8]
    normed_two, _, activated = kept[6:]
    sum_up = jnp.sum(d_before.astype(f32), axis=0)

    def work_two(given):
        activated, grad_down, normed_two, d_before, value = given
        own = dot_own(d_before, up, dot_t)
        g_down = outer(activated, grad_down).astype(bf16)
        g_up = outer(normed_two, d_before).astype(bf16)
        return own, (more[1](value), g_down, g_up)

    parts, (own, grads) = beside(
        dot_others(d_before, up, dot_t),
        scatter_parts,
        (activated, grad_down, normed_two, d_before, more[0]),
        work_two,
    )
    return sum_parts(own, parts), grads, sum_up


def backward(gradient, d_normed, sum_up, params, kept, info, slopes, core, across, more):
    (gain_one, _, w_in, _, project, _, gain_two) = params[:7]
    hidden, normed_all, logsum, rows, context, middle = kept[:6]
    sum_down = jnp.sum(gradient.astype(bf16).astype(f32), axis=0)

    d_values, sum_gain_two, sum_offset_two = norm_back(middle, gain_two, d_normed)
    d_middle = gradient + d_values
    grad_out = d_middle.astype(bf16)
    grad_out_all, (sum_project, crossed) = beside(
        grad_out,
        gather_z,
        (grad_out, across[0]),
        lambda v: (jnp.sum(v[0].astype(f32), axis=0), across[1](v[1])),
    )

    def attention(grad_out_all):
        d_context = dot_t(grad_out_all, project).astype(bf16)
        received = swap(columns_at(d_context, 1 - core, 128), "core")
        mine = columns_at(d_context, core, 128)
        d_mine, d_other, sums = attend_back(info, slopes, rows, mine, received, logsum)
        return in_order(d_mine, swap(d_other, "core"), core), sums

    def attention_more(grad_out_all):
        d_joined, sums = attention(grad_out_all)
        return d_joined, sums, more(held, d_joined, sums, (sum_project, sum_gain_two, sum_offset_two, sum_down, sums, sum_up))

    crossed, grad_out_all, held = lax.optimization_barrier((crossed, grad_out_all, across[4]))
    crossed, (d_joined, sums, done_more) = beside(
        across[2](crossed, context, grad_out_all), across[3], grad_out_all, attention_more
    )

    def g_input():
        return outer(normed_all, d_joined).astype(bf16)

    def scatter(work):
        parts, (own, done) = beside(
            dot_others(d_joined, w_in, dot_t),
            scatter_parts,
            d_joined,
            lambda v: (dot_own(v, w_in, dot_t), work()),
        )
        return (own, parts), done

    vectors = (sum_project, sum_gain_two, sum_offset_two, sum_down, sums, sum_up)
    def finish(given):
        own, parts = given
        d_normed_one = sum_parts(own, parts)
        d_hidden, sum_gain_one, sum_offset_one = norm_back(hidden, gain_one, d_normed_one)
        return d_middle + d_hidden, (sum_gain_one, sum_offset_one)

    return crossed, vectors, done_more, g_input, grad_out_all, scatter, finish


def take(value, at, axis=0):
    return lax.dynamic_index_in_dim(value, at, axis, keepdims=False)


def groups_first(value, shape):
    split = value.reshape(shape)
    order = (1, 0) + tuple(range(2, len(shape)))
    return split.transpose(order)


def core_sum(pack, core):
    split = pack.reshape(8, 2, 64, -1)
    keep, send = take(split, core, 1), take(split, 1 - core, 1)
    return (keep.astype(f32) + swap(send, "core").astype(f32)).astype(bf16)


def pack_outer(g_down, g_up):
    pieces = (
        groups_first(g_down, (2, 16, 32, D)).reshape(16, 64, D),
        groups_first(g_up, (8, 16, 8, D)).reshape(16, 64, D),
    )
    return jnp.concatenate(pieces, axis=-1)


def pack_inner(g_project, g_input):
    project = g_project.reshape(2, 16, 8, 4, 256).transpose(1, 0, 3, 2, 4).reshape(16, 64, 256)
    return jnp.concatenate(
        [project, groups_first(g_input, (8, 16, 8, 768)).reshape(16, 64, 768)], axis=-1
    )


def to_xy(value):
    return lax.all_to_all(value, ("x", "y_lo"), split_axis=0, concat_axis=0, tiled=True)


def sum_pairs(value, at, axis):
    return take(value, at).astype(f32) + swap(take(value, 1 - at), axis).astype(f32)


def sum_z(value, z):
    split = value.reshape(2, 4, *value.shape[1:])
    total = take(split, z, 1).astype(f32)
    for k in (1, 2, 3):
        total = total + shift_z(take(split, (z + k) % 4, 1), k).astype(f32)
    return total.astype(bf16)


def spread_z(both, z):
    columns = both.reshape(4, 8, -1)
    blocks = [take(columns, z)] + [shift_z(take(columns, (z + 4 - k) % 4), 4 - k) for k in (1, 2, 3)]
    out = []
    for four in range(4):
        at = (four + 4 - z) % 4
        low = jnp.where(at == 0, blocks[0], blocks[1])
        high = jnp.where(at == 2, blocks[2], blocks[3])
        out.append(jnp.where(at < 2, low, high))
    return jnp.concatenate(out)


def y_rows(summed, y_hi):
    return sum_pairs(summed.reshape(2, 32, -1), y_hi, "y_hi").astype(bf16)


def across_y(own, to_hi, to_lo, to_both):
    axes = ("y_lo", "y_hi")
    total = own.astype(f32)
    for value, to in ((to_hi, [1, 0, 3, 2]), (to_lo, [2, 3, 0, 1]), (to_both, [3, 2, 1, 0])):
        total = total + lax.ppermute(value, axes, list(enumerate(to))).astype(f32)
    return total


def inner_core(pack, core):
    split = pack.reshape(4, 2, 2, 64, -1)
    keep, send = take(split, core, 2), take(split, 1 - core, 2)
    return (keep.astype(f32) + swap(send, "core").astype(f32)).astype(bf16)


def inner_x(low, x):
    total = take(low, x).astype(f32)
    for k in (1, 2, 3):
        total = total + shift_x(take(low, (x + k) % 4), k).astype(f32)
    return total.astype(bf16)


def inner_y(low, y_lo, y_hi):
    split = low.reshape(2, 2, 32, -1)
    piece = lambda a, b: take(take(split, a), b)
    return across_y(
        piece(y_lo, y_hi),
        piece(y_lo, 1 - y_hi),
        piece(1 - y_lo, y_hi),
        piece(1 - y_lo, 1 - y_hi),
    ).astype(bf16)


def inner_z(both, z):
    return jnp.concatenate([both[:, :256], spread_z(both[:, 256:], z)], axis=1)


def small_z(packed, z):
    split = packed.reshape(2, 4, -1)
    total = take(split, z, 1)
    for k in (1, 2, 3):
        total = total + shift_z(take(split, (z + k) % 4, 1), k)
    return total


def small_y(total, y_hi):
    own, other = take(total, y_hi), take(total, 1 - y_hi)
    return across_y(own, other, own, other)


def small_x(total):
    return total + shift_x(total, 1) + shift_x(total, 2) + shift_x(total, 3)


def unpack_wide_kernel(second, down, up):
    for pair in range(2):
        for y_lo in range(2):
            for core in range(2):
                low = second[(pair * 2) * 4 + y_lo * 2 + core].astype(f32)
                high = second[(pair * 2 + 1) * 4 + y_lo * 2 + core].astype(f32)
                for x, block in ((pair * 2, low), (pair * 2 + 1, high)):
                    at = core * 256 + x * 64
                    down[0, at : at + 64, y_lo * 512 : (y_lo + 1) * 512] = block[:, 512:1024]
                for place in range(8):
                    lanes = slice(place * 64, (place + 1) * 64)
                    at = place * 512 + core * 256 + pair * 128
                    up[0, y_lo * 64 : (y_lo + 1) * 64, at : at + 128] = jnp.concatenate(
                        [low[:, lanes], high[:, lanes]], axis=1
                    )


def unpack_wide(second):
    return pl.pallas_call(
        unpack_wide_kernel,
        grid=(1,),
        out_shape=(
            jax.ShapeDtypeStruct((LAYERS, 512, D), f32),
            jax.ShapeDtypeStruct((LAYERS, 128, FF), f32),
        ),
        in_specs=[whole],
        out_specs=(
            pl.BlockSpec((1, 512, D), lambda i: (1, 0, 0)),
            pl.BlockSpec((1, 128, FF), lambda i: (1, 0, 0)),
        ),
        compiler_params=params_one,
        name="unpack_wide",
    )(second)


def place_input(block, layer, row, inputs):
    rows = pl.ds(row, 8)
    for four in range(4):
        part_rows = block[four * 8 : (four + 1) * 8, :].astype(f32)
        for side in range(2):
            for part in range(3):
                to = part * D + side * 512 + four * 128
                at = (side * 3 + part) * 128
                inputs[layer, rows, to : to + 128] = part_rows[:, at : at + 128]


def unpack_full_kernel(full, old_down, old_up, down, up, inputs, project):
    for g in range(2):
        rows = slice(g * 8, (g + 1) * 8)
        down[0, g * 32 : (g + 1) * 32, :] = full[g, :, 0:D].astype(f32)
        for four in range(4):
            found = full[g, four * 8 : (four + 1) * 8, D : 2 * D].astype(f32)
            for side in range(2):
                at = side * 2048 + four * 512
                up[0, rows, at : at + 512] = found[:, side * 512 : (side + 1) * 512]
        place_input(full[g, :, 3328:4096], 0, g * 8, inputs)
        place_input(full[g, :, 2560:3328], 1, g * 8, inputs)
        for layer, at in ((0, 2048), (1, 2304)):
            block = full[g, :, at : at + 256].astype(f32)
            for four in range(4):
                project[layer, rows, four * 256 : (four + 1) * 256] = block[
                    four * 8 : (four + 1) * 8, :
                ]


def unpack_full(full, down, up):
    old = pl.BlockSpec(memory_space=pl.ANY)
    return pl.pallas_call(
        unpack_full_kernel,
        grid=(8,),
        out_shape=(
            jax.ShapeDtypeStruct((LAYERS, 512, D), f32),
            jax.ShapeDtypeStruct((LAYERS, 128, FF), f32),
            jax.ShapeDtypeStruct((LAYERS, 128, 3072), f32),
            jax.ShapeDtypeStruct((LAYERS, 128, D), f32),
        ),
        in_specs=[pl.BlockSpec((2, 32, 4224), lambda i: (i, 0, 0)), old, old],
        out_specs=(
            pl.BlockSpec((1, 64, D), lambda i: (0, i, 0)),
            pl.BlockSpec((1, 16, FF), lambda i: (0, i, 0)),
            pl.BlockSpec((LAYERS, 16, 3072), lambda i: (0, i, 0)),
            pl.BlockSpec((LAYERS, 16, D), lambda i: (0, i, 0)),
        ),
        input_output_aliases={1: 0, 2: 1},
        compiler_params=pltpu.CompilerParams(vmem_limit_bytes=58 * 2**20),
        name="unpack_full",
    )(full, down, up)


def pack_tail_kernel(
    info, g_input, gain, offset, project, gain_two, offset_two, down, sums, up, second, out
):
    core, z = info[0], info[1]
    out[:, :, :, 768:896] = jnp.zeros((16, 8, 8, 128), bf16)
    for owner in range(8):
        for g in range(16):
            at = owner * 128 + g * 8
            out[g, owner, :, 0:768] = g_input[at : at + 8, :]
        for block, vector in enumerate((gain, offset, project, gain_two, offset_two, down)):
            row = vector[0:1, owner * 128 : (owner + 1) * 128]
            out[block // 2, owner, block % 2 : block % 2 + 1, 768:896] = row.astype(bf16)
        for block in range(12):
            row = second[owner : owner + 1, block * 128 : (block + 1) * 128]
            to = 12 + block
            out[to // 2, owner, to % 2 : to % 2 + 1, 768:896] = row.astype(bf16)
    place = core * 4 + z
    for part, base in ((0, 0), (2, 4)):
        for odd in range(2):
            row = sums[0:1, part * 128 : (part + 1) * 128]
            row = jnp.where(place % 2 == odd, row, 0.0).astype(bf16)
            out[3, base + (place >> 1), odd : odd + 1, 768:896] = row
    for side in range(2):
        for block in range(4):
            row = up[0:1, side * 512 + block * 128 : side * 512 + (block + 1) * 128].astype(bf16)
            out[4 + block // 2, side * 4 + z, block % 2 : block % 2 + 1, 768:896] = row


def pack_tail(info, g_input, mixed, vectors, second):
    rows = [v.reshape(1, -1) for v in mixed + vectors]
    out = pl.pallas_call(
        pack_tail_kernel,
        out_shape=jax.ShapeDtypeStruct((16, 8, 8, 896), bf16),
        in_specs=[smem] + [whole] * 10,
        out_specs=whole,
        compiler_params=params_one,
        name="pack_tail",
    )(info, g_input, *rows, second)
    return out.reshape(128, 8, 896)


def pack_small(small, place):
    (gain_one, offset_one, project, gain_two, offset_two, down, sums, up) = small
    vectors = [
        v.reshape(8, 128) for v in (gain_one, offset_one, project, gain_two, offset_two, down)
    ]
    sums = sums.reshape(-1)
    inputs = lax.dynamic_update_slice_in_dim(jnp.zeros((2 * D,), f32), sums[:128], place * 128, 0)
    inputs = lax.dynamic_update_slice_in_dim(inputs, sums[256:], D + place * 128, 0)
    return jnp.concatenate(vectors + [inputs.reshape(8, 256), up], axis=1)


def on_device(
    inputs,
    cotangent,
    segments,
    norm_one_gain,
    norm_one_bias,
    input_weight,
    input_bias,
    project_weight,
    project_bias,
    norm_two_gain,
    norm_two_bias,
    up_weight,
    up_bias,
    down_weight,
    down_bias,
):
    y_hi, z = lax.axis_index("y_hi"), lax.axis_index("z")
    x, y_lo, core = lax.axis_index("x"), lax.axis_index("y_lo"), lax.axis_index("core")
    place = core * 4 + z
    rows_in = regroup(inputs[0], core, y_hi)
    cut = jnp.sum((segments[0] < 2).astype(jnp.int32))
    cut = regroup(jnp.broadcast_to(cut, (1, 128)), core, y_hi)[0, 0]
    info = jnp.stack([core, z, cut, y_hi]).astype(jnp.int32)
    corner = jnp.stack([core, z, y_hi, core * 4 + x, x, y_lo]).astype(jnp.int32)
    heads = (place * 2 + jnp.arange(2, dtype=jnp.int32)).astype(f32)
    slopes = jnp.exp2(-8.0 * (heads + 1.0) / HEADS)

    small = jnp.concatenate(
        [
            norm_one_gain,
            norm_one_bias,
            project_bias,
            norm_two_gain,
            norm_two_bias,
            down_bias,
            input_bias,
            up_bias,
        ],
        axis=1,
    )
    small = jnp.concatenate([small.reshape(4, 768), jnp.zeros((12, 768), bf16)], axis=0)
    first = pack_first(corner[3:4], input_weight, small)
    (raw_all, first), (up_zero, second, rows, wide) = beside(
        (rows_in, first),
        lambda v: (gather_z(v[0]), to_ctx(v[1])),
        corner,
        lambda v: pack_rest(v, input_weight, up_weight, down_weight, project_weight),
    )

    def first_norm(given):
        first, raw_all = given
        vectors, in_bias, unit_bias = read_small(corner, first)
        unit = norm_parts(raw_all.astype(f32))[0]
        normed_all = (unit * vectors[0] + vectors[1]).astype(bf16)
        return vectors, in_bias, unit_bias, normed_all, unit.astype(bf16)

    def first_weight(given):
        first, raw_all, rows = given
        (w_first, rows), parts = beside(
            (first[:, 0:16].reshape(128, 768), rows),
            lambda v: (gather_x(v[0]), swap(v[1], "y_hi")),
            (first, raw_all),
            first_norm,
        )
        w_first = join_columns(corner, w_first, swap(w_first, "core"))
        return w_first, rows, parts, forward_project(parts[3], w_first, parts[1][0], core)

    up_zero, (w_first, rows, first_parts, projected) = beside(
        up_zero, to_ctx, (first, raw_all, rows), first_weight
    )
    vectors, in_bias, unit_bias, normed_all, unit_all = first_parts
    wide = lax.all_gather(wide, CTX, axis=0, tiled=True)
    vector = [vectors[i] for i in range(12)]
    nothing = (jnp.zeros((8, 128), f32), lambda v: v, lambda v, *more: v, lambda v: v, None)
    unit_wide = first[:, 19:20, 256:768].reshape(8, 2, 4, 64)
    unit_wide = lax.dynamic_index_in_dim(unit_wide, core, 1, keepdims=False)
    unit_wide = unit_wide.transpose(1, 0, 2).reshape(4, 1, 512).astype(f32)
    hidden = rows_in.astype(f32)
    context, logsum, rows_kept, (pieces, second) = forward_attention(
        projected, info, slopes, core, ((rows, second), lambda v: (gather_x(v[0]), to_ctx(v[1])))
    )
    other = swap(pieces, "core")
    project_zero, project_one = join_project(corner, project_weight, pieces, other)
    context, wide = lax.optimization_barrier((context, wide))
    params_0 = (
        vector[0],
        vector[1],
        w_first,
        in_bias[0],
        project_zero,
        vector[2],
        vector[3],
        vector[4],
    )

    def fetch_other(halves, width):
        return join_halves(corner, halves, swap(halves, "core"), (width,))[0]

    middle, normed, up_zero = forward_middle(
        hidden, context, params_0, up_zero, lambda v: fetch_other(v, D)
    )
    wide = lax.all_gather(after(wide, normed), "x")
    normed_two, (w_second, down_zero) = beside(
        normed,
        gather_z,
        (second, pieces, other),
        lambda v: (fetch_other(v[0], 768), join_down(corner, down_weight, v[1], v[2])),
    )
    params_0 = params_0 + (up_zero, unit_bias[0], down_zero, vector[5])
    before = dot(normed_two, up_zero) + unit_bias[0]
    activated = gelu(before).astype(bf16)
    last = (middle, activated)
    kept_0 = (hidden, normed_all, logsum, rows_kept, context, middle, normed_two, before, activated)
    parts, hidden = beside(
        last_send(last, params_0), scatter_parts, last, lambda v: last_own(v, params_0)
    )
    hidden = sum_parts(hidden, parts)
    normed_all = gather_z(norm(hidden, vector[6], vector[7]).astype(bf16))
    params_1 = (
        vector[6],
        vector[7],
        w_second,
        in_bias[1],
        project_one,
        vector[8],
        vector[9],
        vector[10],
    )
    gradient = regroup(cotangent[0], core, y_hi)
    context, logsum, rows_kept, grad_other = forward_attention(
        forward_project(normed_all, w_second, in_bias[1], core),
        info,
        slopes,
        core,
        (gradient, lambda v: swap(v, "core")),
    )
    middle, normed_two, _ = forward_middle(hidden, context, params_1)
    own, other, d_own, d_other, sum_up, wide_grads = wide_part(
        normed_two, swap(normed_two, "core"), gradient, grad_other, wide, unit_wide
    )
    d_normed = d_own + swap(d_other, "core").astype(f32)
    output = middle + (own + swap(other, "core").astype(f32)) + vector[11]
    kept_1 = (hidden, normed_all, logsum, rows_kept, context, middle)
    wide_grads = lax.psum_scatter(wide_grads, "x", scatter_dimension=0, tiled=True)[0]
    units = lax.dynamic_update_slice_in_dim(
        jnp.zeros((8, 2, 4, 64), f32), sum_up.reshape(4, 8, 64).transpose(1, 0, 2)[:, None], core, 1
    )
    gradient = gradient.astype(f32)

    _, vectors_1, _, g_input, grad_out_all, scatter, finish = backward(
        gradient,
        d_normed,
        units.reshape(8, 512),
        params_1,
        kept_1,
        info,
        slopes,
        core,
        nothing,
        lambda *given: None,
    )
    left, inner_1 = scatter(
        lambda: pack_inner(outer(context, grad_out_all).astype(bf16), g_input())
    )
    gradient, norm_sums = finish(left)
    packed_1 = pack_small(norm_sums + vectors_1, place)
    grad_down, wide_grads = beside(
        gradient.astype(bf16),
        gather_z,
        wide_grads,
        lambda v: sum_pairs(v, y_lo, "y_lo").astype(bf16),
    )
    inner_1, wide_grads = lax.optimization_barrier((inner_1, wide_grads))
    inner_1 = lax.psum_scatter(inner_1, GRP, scatter_dimension=0, tiled=True)[0]
    wide_grads, d_before = beside(
        wide_grads,
        lambda v: sum_z(v, z),
        (grad_down, kept_0[7]),
        lambda v: jax.vjp(gelu, v[1])[1](dot_t(v[0], params_0[10]))[0].astype(bf16),
    )
    d_normed, (wide_grads, *grads), sum_up = backward_two(
        grad_down,
        d_before,
        params_0,
        kept_0,
        core,
        (wide_grads, lambda v: sum_pairs(v, y_hi, "y_hi").astype(bf16)),
    )
    wide_grads = lax.all_gather(wide_grads, GRP)

    def with_project(summed, context, grad_out_all):
        g_project = outer(context, grad_out_all).astype(bf16)
        rows = g_project.reshape(2, 16, 8, 4, 256).transpose(1, 0, 3, 2, 4).reshape(16, 64, 256)
        return jnp.concatenate([summed, core_sum(rows, core)], axis=-1)

    wide_all = wide_grads

    def tail_pack(inner_sum, d_joined, sums, vectors):
        w_in = params_0[2].astype(f32)
        gain = jnp.sum(outer(unit_all, d_joined) * w_in, axis=1)
        offset = jnp.sum(d_joined.astype(f32), axis=0, keepdims=True)
        offset = jnp.sum(offset * w_in, axis=1)
        g_input = outer(kept_0[1], d_joined).astype(bf16)
        packed = pack_tail(info, g_input, (gain, offset), vectors, packed_1)
        return packed, inner_sum, wide_all

    crossed, _, (low, inner_1, wide_grads), _, _, scatter, finish = backward(
        gradient,
        d_normed,
        sum_up,
        params_0,
        kept_0,
        info,
        slopes,
        core,
        (grads, lambda v: core_sum(pack_outer(*v), core), with_project, to_xy, inner_1),
        tail_pack,
    )

    def to_all(value):
        return lax.all_to_all(value, GRP + CTX, split_axis=0, concat_axis=0, tiled=True)

    def outer_rows(given):
        crossed, inner_1 = given
        both = jnp.sum(crossed.astype(f32), axis=0).astype(bf16)
        both = y_rows(jnp.concatenate([both, inner_1], axis=1), y_hi)
        at = 2 * D + 512
        spread = spread_z(jnp.concatenate([both[:, D : 2 * D], both[:, at:]], axis=1), z)
        return [both[:, :D], spread[:, :D], both[:, 2 * D : at], spread[:, D:]]

    low, both = beside(low, to_all, (crossed, inner_1), outer_rows)
    left, _ = scatter(lambda: None)
    gradient = regroup(finish(left)[0], core, y_hi)
    low = low.reshape(32, 32, 896).astype(f32)
    vector = jnp.sum(low[:, :, 768:].reshape(128, 8, 128), axis=0)
    vector = jnp.pad(vector, ((0, 24), (0, 0)))
    low = jnp.sum(low[:, :, :768], axis=0)
    low = jnp.concatenate([low, vector], axis=1).astype(bf16)
    full = lax.all_gather(jnp.concatenate(both + [low], axis=1), GRP)
    vector = full[0:12, 0:2, 4096:4224].astype(f32)
    g_down, g_up, g_input, g_project = unpack_full(full, *unpack_wide(wide_grads))
    packed = vector.reshape(LAYERS * 1536)
    vector = packed.reshape(LAYERS, -1)
    parts = [vector[:, i * 128 : (i + 1) * 128] for i in range(6)]
    return (
        regroup(output, core, y_hi)[None],
        gradient[None],
        parts[0],
        parts[1],
        g_input,
        vector[:, 768:1024],
        g_project,
        parts[2],
        parts[3],
        parts[4],
        g_up,
        vector[:, 1024:1536],
        g_down,
        parts[5],
    )


def solution(mesh):
    split = Mesh(mesh.devices.reshape(4, 2, 2, 2, 4), GRP + CTX)
    rows = P(GRP, CTX, None)
    vector = P(None, CTX)
    matrix = P(None, CTX, None)
    weights = (
        vector,
        vector,
        matrix,
        vector,
        matrix,
        vector,
        vector,
        vector,
        matrix,
        vector,
        matrix,
        vector,
    )
    return jax.shard_map(
        on_device,
        mesh=split,
        in_specs=(rows, rows, P(GRP, None)) + weights,
        out_specs=(rows, rows) + weights,
        check_vma=False,
    )
```
